128 devices in a mesh: row: 16 (over x, y_hi, core), col: 8 (over y_lo, z).
Axes of the slice: x: 4, y: 4 (y_hi: 2, y_lo: 2; y = y_hi * 2 + y_lo), z: 4, core: 2. Of those that a mesh axis runs over, the one named last changes fastest.
Arguments:
- node_feats: bfloat16 [4, 384, 256], P(None, 'row'), may hold values from -6 to 6
- pair_feats: bfloat16 [4, 384, 384, 128], P(None, 'row', 'col'), may hold values from -6 to 6
- distances: float32 [4, 384, 384], P(None, 'row', 'col'), may hold values from -4 to 4
- lengths: int32 [4], replicated, may hold values from 64 to 384, as said below
- node_cotan: bfloat16 [4, 384, 256], P(None, 'row'), may hold values from -6 to 6
- pair_cotan: bfloat16 [4, 384, 384, 128], P(None, 'row', 'col'), may hold values from -6 to 6
- w_qkv: bfloat16 [256, 768], replicated, may hold values from -0.375 to 0.375
- w_bias: bfloat16 [128, 8], replicated, may hold values from -0.5 to 0.5
- w_dist: float32 [8], replicated, may hold values from -1 to 1
- w_node_out: bfloat16 [256, 256], replicated, may hold values from -2 to 2
- g_node: float32 [256], replicated, may hold values from 0.1 to 1.9
- w_ab: bfloat16 [256, 64], replicated, may hold values from -0.375 to 0.375
- w_outer: bfloat16 [32, 4096], replicated, may hold values from -0.1875 to 0.1875
- b_outer: float32 [128], replicated, may hold values from -3 to 3
- g_tin: float32 [2, 128], replicated, may hold values from 0.1 to 1.9
- w_tin: bfloat16 [2, 128, 640], replicated, may hold values from -0.5 to 0.5
- g_tout: float32 [2, 128], replicated, may hold values from 0.1 to 1.9
- w_tout: bfloat16 [2, 128, 128], replicated, may hold values from -0.5 to 0.5
- g_trans: float32 [128], replicated, may hold values from 0.1 to 1.9
- w_up: bfloat16 [128, 512], replicated, may hold values from -0.5 to 0.5
- w_down: bfloat16 [512, 128], replicated, may hold values from -0.25 to 0.25
Outputs:
- node_out: float32 [4, 384, 256], P(None, 'row')
- pair_out: float32 [4, 384, 384, 128], P(None, 'row', 'col')
- grad_node: float32 [4, 384, 256], P(None, 'row')
- grad_pair: float32 [4, 384, 384, 128], P(None, 'row', 'col')
- grad_dist: float32 [4, 384, 384], P(None, 'row', 'col')
- grad_w_qkv: float32 [256, 768], replicated
- grad_w_bias: float32 [128, 8], replicated
- grad_w_dist: float32 [8], replicated
- grad_w_node_out: float32 [256, 256], replicated
- grad_g_node: float32 [256], replicated
- grad_w_ab: float32 [256, 64], replicated
- grad_w_outer: float32 [32, 4096], replicated
- grad_b_outer: float32 [128], replicated
- grad_g_tin: float32 [2, 128], replicated
- grad_w_tin: float32 [2, 128, 640], replicated
- grad_g_tout: float32 [2, 128], replicated
- grad_w_tout: float32 [2, 128, 128], replicated
- grad_g_trans: float32 [128], replicated
- grad_w_up: float32 [128, 512], replicated
- grad_w_down: float32 [512, 128], replicated
The draws below stay inside these ranges and needn't reach their ends.
Inputs may be any that keep to these rules, and one draw needn't show every extreme that they name: `lengths`: residues of each protein; in every draw at least one protein fills all 384 slots.
All inputs are finite; a program needn't handle non-finite values.
Results may differ from the reference program's by a relative error of at most 0.019.
Values may be sent and summed in bfloat16 or wider, within the bound.
No kernel may reach another device: no remote copies, remote signals or barrier semaphores. Data moves between devices by JAX's collectives and lax.ppermute only.
A program may use at most 256 MiB of HBM per device.

```python
import jax
import jax.numpy as jnp
from jax import lax

D = 256
C = 128
H = 8
HD = 32
CH = 128
OP = 32
FT = 512
NR = 384
ITEMS = 4


def draw_lengths(key, part):
    key = jax.random.fold_in(key, 11)
    first_key, second_key = jax.random.split(key)
    drawn = jax.random.randint(first_key, (ITEMS,), NR // 6, NR + 1)
    chosen = jax.random.randint(second_key, (), 0, ITEMS)
    return jnp.where(jnp.arange(ITEMS) == chosen, NR, drawn).astype(jnp.int32)


def steps_of(key, dims, shards, low, high):
    loudness = 1.0
    for position, parts in shards:
        draws = jax.random.uniform(jax.random.fold_in(jax.random.fold_in(key, 6), position), (parts,), jnp.float32, low / len(shards), high / len(shards))
        loudness = loudness * jnp.repeat(jnp.exp(draws), dims[position] // parts).reshape((-1,) + (1,) * (len(dims) - 1 - position))
    return loudness


def normal_values(stream_key, shape, deviation, reach, cuts=(), held_as=jnp.bfloat16):
    level = steps_of(stream_key, shape, cuts, -0.22, 0.18) if cuts else 1.0
    entries = jax.random.normal(stream_key, shape, jnp.float32) * deviation * level
    return jnp.minimum(jnp.maximum(entries, -reach), reach).astype(held_as)


def setup_inputs(seed: int = 0) -> dict:
    seeds = jax.random.split(jax.random.key(seed), 22)
    return {
        "node_feats": normal_values(seeds[0], (ITEMS, NR, D), 1.0, 6.0, ((1, 16),)),
        "pair_feats": normal_values(seeds[1], (ITEMS, NR, NR, C), 1.0, 6.0, ((1, 16), (2, 8))),
        "distances": normal_values(seeds[2], (ITEMS, NR, NR), 1.0, 4.0, ((1, 16), (2, 8)), jnp.float32),
        "lengths": draw_lengths(jax.random.fold_in(seeds[21], 71), 0),
        "node_cotan": normal_values(seeds[4], (ITEMS, NR, D), 1.0, 6.0, ((1, 16),)),
        "pair_cotan": normal_values(seeds[5], (ITEMS, NR, NR, C), 1.0, 6.0, ((1, 16), (2, 8))),
        "w_qkv": normal_values(seeds[6], (D, 3 * D), D ** -0.5, 0.375),
        "w_bias": normal_values(seeds[7], (C, H), C ** -0.5, 0.5),
        "w_dist": jnp.clip(jax.random.uniform(seeds[8], (H,), jnp.float32, -1.0, 1.0), -1.0, 1.0),
        "w_node_out": normal_values(seeds[9], (D, D), (D // 32) ** -0.5, 2.0),
        "g_node": jnp.clip(1.0 + 0.18 * jax.random.normal(seeds[10], (D,), jnp.float32), 0.1, 1.9),
        "w_ab": normal_values(seeds[11], (D, 2 * OP), D ** -0.5, 0.375),
        "w_outer": normal_values(seeds[12], (OP, OP * C), (OP * OP) ** -0.5, 0.1875),
        "b_outer": normal_values(seeds[13], (C,), 0.5, 3.0, (), jnp.float32),
        "g_tin": jnp.clip(1.0 + 0.18 * jax.random.normal(seeds[14], (2, C), jnp.float32), 0.1, 1.9),
        "w_tin": normal_values(seeds[15], (2, C, 4 * CH + C), C ** -0.5, 0.5),
        "g_tout": jnp.clip(1.0 + 0.18 * jax.random.normal(seeds[16], (2, CH), jnp.float32), 0.1, 1.9),
        "w_tout": normal_values(seeds[17], (2, CH, C), CH ** -0.5, 0.5),
        "g_trans": jnp.clip(1.0 + 0.18 * jax.random.normal(seeds[18], (C,), jnp.float32), 0.1, 1.9),
        "w_up": normal_values(seeds[19], (C, FT), C ** -0.5, 0.5),
        "w_down": normal_values(seeds[20], (FT, C), FT ** -0.5, 0.25),
    }


@jax.custom_vjp
def low(v):
    return lax.optimization_barrier(v.astype(jnp.bfloat16)).astype(jnp.float32)

@jax.custom_vjp
def low_back(v):
    return v

def low_keep(v):
    return (low(v), None)

def low_pass(kept, grad):
    return (grad,)

def back_keep(v):
    return (v, None)

def back_low(kept, grad):
    return (low(grad),)
low.defvjp(low_keep, low_pass)
low_back.defvjp(back_keep, back_low)
eps = 1e-05
highest = lax.Precision.HIGHEST

def layer_norm(values, gain_vec):
    centered = values - lax.optimization_barrier(jnp.mean(values, axis=-1, keepdims=True))
    spread = lax.optimization_barrier(jnp.mean(centered * centered, axis=-1, keepdims=True))
    return centered * lax.rsqrt(spread + eps) * gain_vec

def round_both(values):
    return low_back(low(values))

def matmul(inputs, weight):
    return jnp.einsum('...a,ab->...b', inputs, weight, precision=highest)

def triangle(pair_in, pair_keep, gain_in, weight_in, gain_out, weight_out, outgoing):
    normed = round_both(layer_norm(pair_in, gain_in))
    projected = low_back(matmul(normed, weight_in))
    left_side = round_both(jax.nn.sigmoid(projected[..., CH:2 * CH]) * projected[..., :CH] * pair_keep)
    right_side = round_both(jax.nn.sigmoid(projected[..., 3 * CH:4 * CH]) * projected[..., 2 * CH:3 * CH] * pair_keep)
    if outgoing:
        product = jnp.einsum('ikc,jkc->ijc', left_side, right_side, precision=highest)
    else:
        product = jnp.einsum('kic,kjc->ijc', left_side, right_side, precision=highest)
    product = low_back(product)
    update = low_back(matmul(round_both(layer_norm(product, gain_out)), weight_out))
    return pair_in + jax.nn.sigmoid(projected[..., 4 * CH:]) * update

def item_forward(node_item, pair_item, dist_item, length_item, params):
    w_qkv, w_bias, w_dist, w_node_out, g_node, w_ab, w_outer, b_outer, g_tin, w_tin, g_tout, w_tout, g_trans, w_up, w_down = params
    slot_ids = jnp.arange(NR, dtype=jnp.int32)
    res_mask = (slot_ids < length_item).astype(jnp.float32)
    pair_keep = (res_mask[:, None] * res_mask[None, :])[:, :, None]
    qkv = round_both(matmul(node_item, w_qkv))
    query_heads = qkv[:, :D].reshape(NR, H, HD)
    key_heads = qkv[:, D:2 * D].reshape(NR, H, HD)
    value_heads = qkv[:, 2 * D:].reshape(NR, H, HD)
    bias = round_both(jnp.einsum('ijc,ch->hij', pair_item, w_bias, precision=highest) + w_dist[:, None, None] * dist_item[None, :, :])
    score_scale = HD ** (-0.5)
    scores = low_back(jnp.einsum('ihd,jhd->hij', query_heads, key_heads, precision=highest) * score_scale + bias)
    scores = scores + ((res_mask - 1.0) * 1000000000.0)[None, None, :]
    attn_probs = low(jax.nn.softmax(scores, axis=-1))
    attended = round_both(jnp.einsum('hij,jhd->ihd', attn_probs, value_heads, precision=highest).reshape(NR, D))
    node_out = node_item + low_back(matmul(attended, w_node_out))
    normed_node = round_both(layer_norm(node_item, g_node))
    pair_rows = round_both(matmul(normed_node, w_ab))
    middle = round_both(matmul(pair_rows[:, :OP], w_outer)).reshape(NR, OP, C)
    outer_term = low_back(jnp.einsum('iqc,jq->ijc', middle, pair_rows[:, OP:], precision=highest)) + b_outer
    pair_one = pair_item + pair_keep * outer_term
    pair_two = triangle(pair_one, pair_keep, g_tin[0], w_tin[0], g_tout[0], w_tout[0], True)
    pair_three = triangle(pair_two, pair_keep, g_tin[1], w_tin[1], g_tout[1], w_tout[1], False)
    normed_three = round_both(layer_norm(pair_three, g_trans))
    hidden = low_back(matmul(normed_three, w_up))
    active = round_both(jax.nn.silu(hidden))
    pair_out = pair_three + low_back(matmul(active, w_down))
    return (node_out, pair_out)

def reference(node_feats, pair_feats, distances, lengths, node_cotan, pair_cotan, w_qkv, w_bias, w_dist, w_node_out, g_node, w_ab, w_outer, b_outer, g_tin, w_tin, g_tout, w_tout, g_trans, w_up, w_down):
    primals = tuple((array_in.astype(jnp.float32) for array_in in (node_feats, pair_feats, distances, w_qkv, w_bias, w_dist, w_node_out, g_node, w_ab, w_outer, b_outer, g_tin, w_tin, g_tout, w_tout, g_trans, w_up, w_down)))

    def forward(node_all, pair_all, dist_all, *params):

        def one_item(item_args):
            return item_forward(item_args[0], item_args[1], item_args[2], item_args[3], params)
        return lax.map(jax.checkpoint(one_item), (node_all, pair_all, dist_all, lengths))
    outputs, pullback = jax.vjp(forward, *primals)
    grads = pullback((node_cotan.astype(jnp.float32), pair_cotan.astype(jnp.float32)))
    return (outputs[0], outputs[1], grads[0], grads[1], grads[2], grads[3], grads[4], grads[5], grads[6], grads[7], grads[8], grads[9], grads[10], grads[11], grads[12], grads[13], grads[14], grads[15], grads[16], grads[17])
```

```python
import jax
import jax.numpy as jnp
from jax import lax
from jax.experimental import pallas as pl
from jax.experimental.pallas import tpu as pltpu
from jax.sharding import PartitionSpec as P

D = 256
C = 128
H = 8
HD = 32
CH = 128
OP = 32
FT = 512
ITEMS = 4
EPS = 1e-05
BOTH = ("row", "col")
F32 = jnp.float32
BF16 = jnp.bfloat16
HALF = 64
JH = 3
STEP_ROWS = 6
VMEM = 60 * 1024 * 1024


def half(values):
    return values.astype(BF16)


def dot(lhs, rhs, lhs_dim, rhs_dim):
    return lax.dot_general(
        lhs, rhs, (((lhs_dim,), (rhs_dim,)), ((), ())), preferred_element_type=F32
    )


def sigmoid(values):
    return 0.5 * jnp.tanh(0.5 * values) + 0.5


def norm_parts(values):
    scale = 1.0 / values.shape[0]
    centered = values - jnp.sum(values, axis=0, keepdims=True) * scale
    spread = jnp.sum(centered * centered, axis=0, keepdims=True) * scale
    inv = lax.rsqrt(spread + EPS)
    return centered * inv, inv


def norm_back(unit, inv, gain, grad):
    scale = 1.0 / unit.shape[0]
    scaled = grad * gain
    first = jnp.sum(scaled, axis=0, keepdims=True) * scale
    second = jnp.sum(scaled * unit, axis=0, keepdims=True) * scale
    return inv * (scaled - first - unit * second)


def fold(values):
    total = values[:, :128]
    for start in range(128, values.shape[1], 128):
        total = total + values[:, start : start + 128]
    return total


def tile_rows_of(ref):
    items, parts, rows = ref.shape[:3]
    return jnp.concatenate(
        [ref[b, h, m] for m in range(rows) for h in range(parts) for b in range(items)], axis=0
    )


def put_tile(ref, values):
    items, parts, rows, cols = ref.shape[:4]
    flipped = jnp.transpose(values)
    start = 0
    for m in range(rows):
        for h in range(parts):
            for b in range(items):
                ref[b, h, m] = flipped[start : start + cols]
                start += cols


def low_lanes(rows):
    return lax.broadcasted_iota(jnp.int32, (rows, 128), 1) < HALF


def swap(values):
    return pltpu.roll(values, HALF, 1)


def lane_row(values, m):
    return values[:, m * 128 : (m + 1) * 128]


def put_rows(ref, values):
    for m in range(ref.shape[0]):
        ref[m] = lane_row(values, m)


def get_rows(ref):
    return jnp.concatenate([ref[m] for m in range(ref.shape[0])], axis=1)


def put_double(ref, left, right):
    low = low_lanes(left.shape[0])
    for m in range(ref.shape[2]):
        one, two = lane_row(left, m), lane_row(right, m)
        ref[0, 0, m] = half(jnp.where(low, one, swap(two)))
        ref[0, 1, m] = half(jnp.where(low, swap(one), two))


def get_double(ref):
    low = low_lanes(ref.shape[3])
    left, right = [], []
    for m in range(ref.shape[2]):
        one, two = ref[0, 0, m].astype(F32), ref[0, 1, m].astype(F32)
        left.append(jnp.where(low, one, swap(two)))
        right.append(jnp.where(low, swap(one), two))
    return jnp.concatenate(left, axis=1), jnp.concatenate(right, axis=1)


def add_to(ref, values):
    @pl.when(pl.program_id(0) == 0)
    def _():
        ref[...] = values

    @pl.when(pl.program_id(0) != 0)
    def _():
        ref[...] += values


def enter_kernel(pair_ref, eye_ref, wb_ref, wd_ref, dist_ref, x_ref, bias_ref):
    rows = tile_rows_of(pair_ref)
    x_ref[...] = half(dot(eye_ref[...], rows, 1, 1))
    bias_ref[...] = half(dot(wb_ref[...], rows, 1, 1) + wd_ref[...] * dist_ref[...])


def front(values, gain, w_in, keep, sides_ref):
    unit, _ = norm_parts(values)
    proj = dot(w_in, half(unit * gain), 1, 0)
    put_double(
        sides_ref,
        sigmoid(proj[CH : 2 * CH]) * proj[:CH] * keep,
        sigmoid(proj[3 * CH :]) * proj[2 * CH : 3 * CH] * keep,
    )


def open_kernel(
    x_ref, mid_ref, bd_ref, bout_ref, keep_ref, gain_ref, w_ref, one_ref, sides_ref
):
    keep = keep_ref[...]
    outer = jnp.concatenate(
        [dot(mid_ref[p], bd_ref[0], 0, 0) for p in range(mid_ref.shape[0])], axis=1
    )
    pair_one = x_ref[...].astype(F32) + keep * (outer + bout_ref[...])
    one_ref[...] = pair_one
    front(pair_one, gain_ref[...], w_ref[: 4 * CH], keep, sides_ref)


def middle_kernel(
    one_ref,
    prod_ref,
    keep_ref,
    gin0_ref,
    wog_ref,
    gout_ref,
    wout_ref,
    gin1_ref,
    w1_ref,
    two_ref,
    sides_ref,
):
    pair_one = one_ref[...]
    unit, _ = norm_parts(pair_one)
    gate = sigmoid(dot(wog_ref[...], half(unit * gin0_ref[...]), 1, 0))
    prod_unit, _ = norm_parts(get_rows(prod_ref).astype(F32))
    update = dot(wout_ref[...], half(prod_unit * gout_ref[...]), 1, 0)
    pair_two = pair_one + gate * update
    two_ref[...] = pair_two
    front(pair_two, gin1_ref[...], w1_ref[: 4 * CH], keep_ref[...], sides_ref)


def rear_back(grad, gate, update, y_half, prod_unit, prod_inv, gout, wout_plain):
    d_update = half(grad * gate)
    dw_out = dot(d_update, y_half, 1, 1)
    d_y = half(dot(wout_plain, d_update, 1, 0)).astype(F32)
    d_prod = half(norm_back(prod_unit, prod_inv, gout, d_y))
    d_og = half(grad * update * gate * (1.0 - gate))
    return d_prod, d_og, dw_out, fold(d_y * prod_unit)


def turn_kernel(
    two_ref,
    prod_ref,
    cot_ref,
    eye_ref,
    gin_ref,
    wog_ref,
    gout_ref,
    wout_ref,
    wout_plain_ref,
    gtr_ref,
    wup_ref,
    wup_plain_ref,
    wdown_ref,
    wdown_plain_ref,
    out_ref,
    grad_ref,
    dprod_ref,
    dog_ref,
    dwdown_ref,
    dwup_ref,
    dgtr_ref,
    dwout_ref,
    dgout_ref,
):
    pair_two = two_ref[...]
    unit, _ = norm_parts(pair_two)
    gate = sigmoid(dot(wog_ref[...], half(unit * gin_ref[...]), 1, 0))
    prod_unit, prod_inv = norm_parts(get_rows(prod_ref).astype(F32))
    y_half = half(prod_unit * gout_ref[...])
    update = dot(wout_ref[...], y_half, 1, 0)
    pair_three = pair_two + gate * update
    tr_unit, tr_inv = norm_parts(pair_three)
    xt = half(tr_unit * gtr_ref[...])
    hidden = dot(wup_ref[...], xt, 1, 0)
    sig = sigmoid(hidden)
    act32 = hidden * sig
    active = half(act32)
    put_tile(out_ref, pair_three + dot(wdown_ref[...], active, 1, 0))
    cot32 = dot(eye_ref[...], tile_rows_of(cot_ref), 1, 1)
    cot = half(cot32)
    add_to(dwdown_ref, dot(active, cot, 1, 1))
    d_active = half(dot(wdown_plain_ref[...], cot, 1, 0)).astype(F32)
    d_hidden = half(d_active * (sig + act32 * (1.0 - sig)))
    add_to(dwup_ref, dot(d_hidden, xt, 1, 1))
    d_xt = half(dot(wup_plain_ref[...], d_hidden, 1, 0)).astype(F32)
    add_to(dgtr_ref, fold(d_xt * tr_unit))
    grad = cot32 + norm_back(tr_unit, tr_inv, gtr_ref[...], d_xt)
    grad_ref[...] = grad
    d_prod, d_og, dw_out, dg_out = rear_back(
        grad, gate, update, y_half, prod_unit, prod_inv, gout_ref[...], wout_plain_ref[...]
    )
    put_rows(dprod_ref, d_prod)
    dog_ref[...] = d_og
    add_to(dwout_ref, dw_out)
    add_to(dgout_ref, dg_out)


def front_back(values, keep, gain, w_in, w_plain, sides_ref, d_og, dw_ref, dg_ref):
    unit, inv = norm_parts(values)
    normed = half(unit * gain)
    proj = dot(w_in[: 4 * CH], normed, 1, 0)
    sig_left = sigmoid(proj[CH : 2 * CH])
    sig_right = sigmoid(proj[3 * CH :])
    d_left, d_right = get_double(sides_ref)
    left = d_left * keep * sig_left
    right = d_right * keep * sig_right
    d_proj = jnp.concatenate(
        [
            half(left),
            half(left * proj[:CH] * (1.0 - sig_left)),
            half(right),
            half(right * proj[2 * CH : 3 * CH] * (1.0 - sig_right)),
            d_og,
        ],
        axis=0,
    )
    add_to(dw_ref, dot(d_proj, normed, 1, 1))
    d_normed = half(dot(w_plain, d_proj, 1, 0)).astype(F32)
    add_to(dg_ref, fold(d_normed * unit))
    return norm_back(unit, inv, gain, d_normed)


def back_kernel(
    two_ref,
    one_ref,
    prod_ref,
    dsides_ref,
    dog_ref,
    grad_ref,
    keep_ref,
    gin1_ref,
    w1_ref,
    w1_plain_ref,
    gin0_ref,
    wog_ref,
    gout_ref,
    wout_ref,
    wout_plain_ref,
    grad_out_ref,
    dprod_ref,
    dog_out_ref,
    dwin_ref,
    dgin_ref,
    dwout_ref,
    dgout_ref,
):
    grad = grad_ref[...] + front_back(
        two_ref[...],
        keep_ref[...],
        gin1_ref[...],
        w1_ref,
        w1_plain_ref[...],
        dsides_ref,
        dog_ref[...],
        dwin_ref,
        dgin_ref,
    )
    grad_out_ref[...] = grad
    unit, _ = norm_parts(one_ref[...])
    gate = sigmoid(dot(wog_ref[...], half(unit * gin0_ref[...]), 1, 0))
    prod_unit, prod_inv = norm_parts(get_rows(prod_ref).astype(F32))
    y_half = half(prod_unit * gout_ref[...])
    update = dot(wout_ref[...], y_half, 1, 0)
    d_prod, d_og, dw_out, dg_out = rear_back(
        grad, gate, update, y_half, prod_unit, prod_inv, gout_ref[...], wout_plain_ref[...]
    )
    put_rows(dprod_ref, d_prod)
    dog_out_ref[...] = d_og
    add_to(dwout_ref, dw_out)
    add_to(dgout_ref, dg_out)


def close_kernel(
    one_ref,
    x_ref,
    dsides_ref,
    dog_ref,
    grad_ref,
    keep_ref,
    gin_ref,
    w_ref,
    w_plain_ref,
    mid_ref,
    bd_ref,
    dbias_ref,
    wb_ref,
    out_ref,
    dmid_ref,
    dwin_ref,
    dgin_ref,
    dright_out_ref,
    dbout_ref,
    dwb_ref,
):
    keep = keep_ref[...]
    grad = grad_ref[...] + front_back(
        one_ref[...],
        keep,
        gin_ref[...],
        w_ref,
        w_plain_ref[...],
        dsides_ref,
        dog_ref[...],
        dwin_ref,
        dgin_ref,
    )
    outer = grad * keep
    add_to(dbout_ref, fold(outer))
    outer = half(outer)
    at = pl.program_id(0)
    total = None
    for p in range(mid_ref.shape[0]):
        piece = lane_row(outer, p)
        part = dot(bd_ref[0], piece, 1, 1)

        @pl.when(at % JH == 0)
        def _(p=p, part=part):
            dmid_ref[p] = part

        @pl.when(at % JH != 0)
        def _(p=p, part=part):
            dmid_ref[p] += part

        part = dot(mid_ref[p], piece, 1, 0)
        total = part if total is None else total + part

    @pl.when(at < JH)
    def _():
        dright_out_ref[at % JH] = total

    @pl.when(at >= JH)
    def _():
        dright_out_ref[at % JH] += total

    d_bias = dbias_ref[...]
    add_to(dwb_ref, dot(d_bias, x_ref[...], 1, 1))
    put_tile(out_ref, grad + dot(wb_ref[...], d_bias, 1, 0))


def item_masks(items, dtype):
    lane = lax.broadcasted_iota(jnp.int32, (1, 256), 1)
    which = (lane // 16) % items
    return [((which == b) & (lane < JH * HALF)).astype(F32).astype(dtype) for b in range(items)]


def spread_items(piece, masks):
    parts = [piece[16 * j : 16 * j + 16] * mask for j in range(JH) for mask in masks]
    return jnp.concatenate(parts + [jnp.zeros((HALF, 256), piece.dtype)], axis=0)


def pick_items(values, masks):
    rows = []
    for j in range(JH):
        total = None
        for b, mask in enumerate(masks):
            start = HALF * j + 16 * b
            part = values[start : start + 16] * mask
            total = part if total is None else total + part
        rows.append(total)
    return jnp.concatenate(rows, axis=0)


def split_lanes(one, two, three):
    low = low_lanes(one.shape[0])
    return (
        jnp.concatenate([jnp.where(low, one, swap(two)), three], axis=1),
        jnp.concatenate([jnp.where(low, swap(one), two), swap(three)], axis=1),
    )


def join_lanes(left, right):
    low = low_lanes(left.shape[0])
    return (
        jnp.where(low, left[:, :128], swap(right[:, :128])),
        jnp.where(low, swap(left[:, :128]), right[:, :128]),
        jnp.where(low, left[:, 128:], swap(right[:, 128:])),
    )


def thirds(values):
    rows = values.shape[0] // JH
    return [values[rows * j : rows * (j + 1)] for j in range(JH)]


def load_double(ref, cols, l_ref, r_ref):
    def step(q, carry):
        left, right = [], []
        for r in range(ref.shape[0] // cols):
            one, two = split_lanes(*thirds(ref[r * cols + q].astype(F32)))
            left.append(one)
            right.append(two)
        l_ref[q] = half(jnp.concatenate(left, axis=0))
        r_ref[q] = half(jnp.concatenate(right, axis=0))
        return carry

    lax.fori_loop(0, cols, step, 0)


def load_single(ref, cols, x_ref):
    def step(q, carry):
        rows = []
        for r in range(ref.shape[0] // cols):
            rows += split_lanes(*thirds(ref[r * cols + q].astype(F32)))
        x_ref[q] = half(jnp.concatenate(rows, axis=0))
        return carry

    lax.fori_loop(0, cols, step, 0)


def put_slab(ref, at, left, right):
    ref[at] = half(jnp.concatenate(join_lanes(left, right), axis=0))


def block_rows(ref, block, at):
    return ref[block, pl.ds(pl.multiple_of(at * 48, 16), 48), :]


def out_product_kernel(s_ref, p_ref, l_ref, r_ref):
    cols, residues, _ = l_ref.shape
    masks = item_masks(ITEMS, BF16)
    load_double(s_ref, cols, l_ref, r_ref)

    def step(at, carry):
        total = None
        for q in range(cols):
            part = dot(l_ref[q], spread_items(block_rows(r_ref, q, at), masks), 1, 1)
            total = part if total is None else total + part
        for r in range(residues // 24):
            tile = total[24 * r : 24 * r + 24]
            put_slab(p_ref, r * cols + at, tile[:12], tile[12:])
        return carry

    lax.fori_loop(0, cols, step, 0)


def flip(values, eye):
    return half(dot(eye, values, 1, 1))


def in_product_kernel(s_ref, eye_ref, p_ref, l_ref, r_ref):
    cols = l_ref.shape[0]
    masks = item_masks(ITEMS, F32)
    load_double(s_ref, cols, l_ref, r_ref)

    def step(at, carry):
        left = flip(l_ref[at], eye_ref[...])
        for q in range(cols):
            rows = pick_items(dot(left, r_ref[q], 1, 0), masks)
            for h in range(2):
                tile = rows[24 * h : 24 * h + 24]
                put_slab(p_ref, (2 * at + h) * cols + q, tile[:12], tile[12:])
        return carry

    lax.fori_loop(0, cols, step, 0)


def in_back_kernel(s_ref, dp_ref, d_ref, l_ref, r_ref, x_ref):
    cols, residues, _ = l_ref.shape
    masks = item_masks(ITEMS, BF16)
    load_double(s_ref, cols, l_ref, r_ref)
    load_single(dp_ref, cols, x_ref)

    def step(at, carry):
        left = right = None
        for q in range(cols):
            part = dot(r_ref[q], spread_items(block_rows(x_ref, q, at), masks), 1, 1)
            left = part if left is None else left + part
            wide = spread_items(x_ref[at, 48 * q : 48 * q + 48, :], masks)
            part = dot(l_ref[q], wide, 1, 0)
            right = part if right is None else right + part
        for r in range(residues // 24):
            rows = slice(24 * r, 24 * r + 24)
            put_slab(d_ref, r * cols + at, left[rows], right[rows])
        return carry

    lax.fori_loop(0, cols, step, 0)


def out_back_kernel(s_ref, dp_ref, eye_ref, d_ref, l_ref, r_ref, x_ref, g_ref):
    cols, residues, _ = l_ref.shape
    masks = item_masks(ITEMS, BF16)
    wide_masks = item_masks(ITEMS, F32)
    load_double(s_ref, cols, l_ref, r_ref)
    load_single(dp_ref, cols, x_ref)

    def right_step(at, carry):
        flipped = flip(x_ref[at], eye_ref[...])
        for q in range(cols):
            rows = pick_items(dot(flipped, l_ref[q], 1, 0), wide_masks)
            g_ref[q, pl.ds(pl.multiple_of(at * 48, 16), 48), :] = rows
        return carry

    lax.fori_loop(0, cols, right_step, 0)

    def left_step(at, carry):
        left = None
        for q in range(cols):
            wide = spread_items(r_ref[at, 48 * q : 48 * q + 48, :], masks)
            part = dot(x_ref[q], wide, 1, 0)
            left = part if left is None else left + part
        for r in range(residues // 24):
            rows = slice(24 * r, 24 * r + 24)
            put_slab(d_ref, r * cols + at, left[rows], g_ref[at, rows, :])
        return carry

    lax.fori_loop(0, cols, left_step, 0)


def cost(flops, nbytes):
    return pl.CostEstimate(flops=int(flops), bytes_accessed=int(nbytes), transcendentals=0)


def call(kernel, steps, ins, outs, flops, scratch=()):
    nbytes = sum(a.size * a.dtype.itemsize for a, _, _ in ins)
    nbytes += sum(s.size * s.dtype.itemsize for s, _, _ in outs)
    return pl.pallas_call(
        kernel,
        grid=(steps,),
        in_specs=[pl.BlockSpec(block, index) for _, block, index in ins],
        out_specs=[pl.BlockSpec(block, index) for _, block, index in outs],
        out_shape=[shape for shape, _, _ in outs],
        scratch_shapes=list(scratch),
        compiler_params=pltpu.CompilerParams(vmem_limit_bytes=VMEM),
        cost_estimate=cost(flops, nbytes),
    )(*[a for a, _, _ in ins])


def whole(array):
    rank = len(array.shape)
    return (array, tuple(array.shape), lambda s: (0,) * rank)


def sds(shape, dtype):
    return jax.ShapeDtypeStruct(shape, dtype)


def per_device(
    node_feats,
    pair_feats,
    distances,
    lengths,
    node_cotan,
    pair_cotan,
    w_qkv,
    w_bias,
    w_dist,
    w_node_out,
    g_node,
    w_ab,
    w_outer,
    b_outer,
    g_tin,
    w_tin,
    g_tout,
    w_tout,
    g_trans,
    w_up,
    w_down,
):
    row_count = lax.axis_size("row")
    col_count = lax.axis_size("col")
    row_index = lax.axis_index("row")
    col_index = lax.axis_index("col")
    items, tile_rows, tile_cols = pair_feats.shape[:3]
    residues = tile_rows * row_count
    devices = row_count * col_count
    il, jl = tile_rows // 2, tile_cols // JH
    lane_rows = JH * il
    slots = lane_rows * 128
    steps = lane_rows // STEP_ROWS
    width = STEP_ROWS * 128
    score_scale = HD ** (-0.5)

    def slot_block(s):
        return (s % JH) * (il // STEP_ROWS) + s // JH

    def chan(array):
        return (array, (array.shape[0], width), lambda s: (0, slot_block(s)))

    def rows_of(array):
        return (array, (STEP_ROWS, C, 128), lambda s: (slot_block(s), 0, 0))

    def double(array):
        return (array, (1, 2, STEP_ROWS, C, 128), lambda s: (s % JH, 0, s // JH, 0, 0))

    def tile(array):
        return (array, (items, 2, STEP_ROWS, jl, C), lambda s: (0, 0, s // JH, s % JH, 0))

    def pairs_of(array):
        return (array, (STEP_ROWS, 2 * items * OP, C), lambda s: (s // JH, 0, 0))

    def f_chan():
        return chan(sds((C, slots), F32))

    def f_whole(*shape):
        return whole(sds(shape, F32))

    def column(vector):
        return whole(vector.reshape(-1, 1))

    def split_tile(array):
        return array.reshape((items, 2, il) + array.shape[2:])

    def to_slots(array):
        lead = array.shape[:-3]
        array = array.reshape(lead + (items, 2, il, JH, jl))
        at = len(lead)
        order = tuple(range(at)) + tuple(at + d for d in (3, 2, 1, 0, 4))
        return jnp.transpose(array, order).reshape(lead + (lane_rows, 128))

    def from_slots(array):
        lead = array.shape[:-2]
        array = array.reshape(lead + (JH, il, 2, items, jl))
        at = len(lead)
        order = tuple(range(at)) + tuple(at + d for d in (3, 2, 1, 0, 4))
        return jnp.transpose(array, order).reshape(lead + (items, tile_rows, tile_cols))

    row_ids = row_index * tile_rows + jnp.arange(tile_rows, dtype=jnp.int32)
    col_ids = col_index * tile_cols + jnp.arange(tile_cols, dtype=jnp.int32)
    row_keep = (row_ids[None, :] < lengths[:, None]).astype(F32)
    col_keep = (col_ids[None, :] < lengths[:, None]).astype(F32)
    keep = to_slots(row_keep[:, :, None] * col_keep[:, None, :]).reshape(1, slots)
    eye = jnp.eye(C, dtype=BF16)
    eye_lanes = jnp.eye(256, dtype=BF16)
    w_in_t = [jnp.transpose(w_tin[t]) for t in range(2)]
    w_out_t = [jnp.transpose(w_tout[t]) for t in range(2)]

    def spread(array, axis):
        count = lax.axis_size(axis) if isinstance(axis, str) else devices
        return swap_all(jnp.broadcast_to(array[None], (count,) + array.shape), axis)

    def swap_all(array, axis):
        return lax.all_to_all(array, axis, split_axis=0, concat_axis=0, tiled=True)

    def tie(*arrays):
        return lax.optimization_barrier(arrays)

    node_rows = jnp.transpose(node_feats, (1, 0, 2)).reshape(tile_rows * items, D)
    cot_rows = jnp.transpose(node_cotan, (1, 0, 2)).reshape(tile_rows * items, D)
    node_full = node_rows.astype(F32)
    parts = tile_cols // tile_rows
    group = row_count // parts
    fetched = []
    for turn in range(parts):
        moves = []
        for src in range(devices):
            src_row, src_col = divmod(src, col_count)
            dst_row = ((src_row + turn) % parts) * group + src_col
            moves.append((src, dst_row * col_count + src_row // parts))
        fetched.append(lax.ppermute(node_rows, BOTH, moves))
    first = row_index // group
    fetched = jnp.stack(fetched)
    col_rows = jnp.concatenate(
        [
            lax.dynamic_index_in_dim(fetched, (first - h) % parts, 0, keepdims=False)
            for h in range(parts)
        ],
        axis=0,
    )
    share = tile_rows * items // col_count

    def node_norm(values):
        centered = values - jnp.mean(values, axis=-1, keepdims=True)
        inv = lax.rsqrt(jnp.mean(centered * centered, axis=-1, keepdims=True) + EPS)
        return centered * inv, inv

    heads_here = H // col_count
    head_width = heads_here * HD
    head_start = col_index * head_width
    w_local = jnp.concatenate(
        [
            lax.dynamic_slice_in_dim(w_qkv, part * D + head_start, head_width, 1)
            for part in range(3)
        ],
        axis=1,
    )
    wo_local = lax.dynamic_slice_in_dim(w_node_out, head_start, head_width, 0)
    qkv = half(dot(node_rows, w_local, 1, 0))
    node_unit, _ = node_norm(node_full)
    normed_node = half(node_unit * g_node)
    pair_rows = half(dot(normed_node, w_ab[:, :OP], 1, 0))
    left_node = pair_rows
    col_unit, _ = node_norm(col_rows.astype(F32))
    right_cols = half(dot(half(col_unit * g_node), w_ab[:, OP:], 1, 0))
    right_cols = right_cols.reshape(tile_cols, items, OP)
    everyone = spread(qkv[:, head_width:].reshape(-1, 128), "row")
    everyone = everyone.reshape(residues, items, 2 * head_width)
    right_wide = jnp.einsum(
        "xy,zxqj->zxqyj",
        jnp.eye(2 * items, dtype=BF16),
        jnp.tile(
            jnp.transpose(right_cols.reshape(JH, jl, items, OP), (0, 2, 3, 1)), (1, 2, 1, 1)
        ),
    ).reshape(JH, 2 * items * OP, 128)
    middle = half(dot(left_node, w_outer, 1, 0)).reshape(2, il, items * OP, C)
    middle = jnp.transpose(middle, (1, 0, 2, 3)).reshape(il, 2 * items * OP, C)
    dist_slots = to_slots(distances)

    x_chan, bias = call(
        enter_kernel,
        steps,
        [
            tile(split_tile(pair_feats)),
            whole(eye),
            whole(jnp.transpose(w_bias)),
            column(w_dist),
            chan(dist_slots.reshape(1, slots)),
        ],
        [chan(sds((C, slots), BF16)), chan(sds((H, slots), BF16))],
        2 * slots * C * C,
    )

    def lane_sum(values):
        return jnp.sum(values, axis=1)[None]

    def padded(arrays):
        flat = jnp.concatenate(arrays, axis=0)
        rows = -(-flat.shape[0] // (devices * 8)) * 8
        flat = jnp.pad(flat, ((0, devices * rows - flat.shape[0]), (0, 0)))
        return flat.reshape(devices, rows, 128)

    def scatter_sum(array):
        return jnp.sum(swap_all(array, BOTH).astype(F32), axis=0)

    def to_channels(rows):
        rows = rows.reshape(-1, C, 128)
        return swap_all(jnp.transpose(rows, (1, 0, 2)), BOTH)

    def to_pairs(slabs):
        got = jnp.transpose(swap_all(slabs, BOTH), (1, 0, 2))
        return got if got.shape[0] == lane_rows else got.reshape(sides.shape)

    sides = sds((JH, 2, il, C, 128), BF16)
    single = sds((lane_rows, C, 128), BF16)
    slab1 = whole(sds((devices, lane_rows, 128), BF16))
    slab2 = whole(sds((devices, 2 * lane_rows, 128), BF16))
    block = pltpu.VMEM((col_count, residues, 256), BF16)
    block32 = pltpu.VMEM((col_count, residues, 256), F32)
    chan_flops = 2 * col_count * col_count * residues * 256 * 256

    g_in = [column(g_tin[t]) for t in range(2)]
    g_out = [column(g_tout[t]) for t in range(2)]
    keep_in = chan(keep)
    bd = (right_wide, (1,) + right_wide.shape[1:], lambda s: (s % JH, 0, 0))
    pos_flops = 2 * slots * C * C
    pair_one, sides0 = call(
        open_kernel,
        steps,
        [
            chan(x_chan),
            pairs_of(middle),
            bd,
            column(b_outer),
            keep_in,
            g_in[0],
            whole(w_in_t[0]),
        ],
        [f_chan(), double(sides)],
        6 * pos_flops,
    )
    everyone, bias = tie(everyone, bias)
    bias_rows = swap_all(bias.reshape(H, lane_rows, 128), "col")
    sides0, bias_rows = tie(sides0, bias_rows)
    slabs0 = to_channels(sides0)
    bias_rows = from_slots(bias_rows.reshape(col_count, heads_here, lane_rows, 128))
    bias_rows = jnp.transpose(bias_rows, (2, 1, 3, 0, 4)).reshape(
        items, heads_here, tile_rows, residues
    )
    key_all = everyone[..., :head_width].reshape(residues, items, heads_here, HD)
    value_all = everyone[..., head_width:].reshape(residues, items, heads_here, HD)
    query = qkv[:, :head_width].reshape(tile_rows, items, heads_here, HD)
    all_ids = jnp.arange(residues, dtype=jnp.int32)
    key_keep = (all_ids[None, :] < lengths[:, None]).astype(F32)

    def product(spec, *operands):
        return jnp.einsum(spec, *operands, preferred_element_type=F32)

    scores = (
        product("ighd,jghd->ghij", query, key_all) * score_scale
        + bias_rows.astype(F32)
        + ((key_keep - 1.0) * 1000000000.0)[:, None, None, :]
    )
    probs = jax.nn.softmax(scores, axis=-1)
    probs_half = half(probs)
    attended = half(
        product("ghij,jghd->ighd", probs_half, value_all).reshape(
            tile_rows * items, head_width
        )
    )
    node_part = half(dot(attended, wo_local, 1, 0))
    dwo_own = dot(attended, cot_rows, 0, 0)
    d_attended = half(dot(cot_rows, wo_local, 1, 1)).reshape(tile_rows, items, heads_here, HD)
    d_probs = product("ighd,jghd->ghij", d_attended, value_all)
    d_value = product("ghij,ighd->jghd", probs_half, d_attended)
    d_scores = half(probs * (d_probs - jnp.sum(probs * d_probs, axis=-1, keepdims=True)))
    d_query = product("ghij,jghd->ighd", d_scores, key_all) * score_scale
    d_key = product("ghij,ighd->jghd", d_scores, query) * score_scale
    d_bias = jnp.transpose(
        d_scores.reshape(items, heads_here, tile_rows, col_count, tile_cols), (3, 1, 0, 2, 4)
    )
    d_bias = to_slots(d_bias).reshape(col_count, heads_here * lane_rows, 128)
    sent = jnp.concatenate([d_bias, node_part.reshape(col_count, -1, 128)], axis=1)
    d_kv = jnp.concatenate(
        [d_key.reshape(-1, head_width), d_value.reshape(-1, head_width)], axis=1
    )
    slabs0, sent = tie(slabs0, sent)
    got = swap_all(sent, "col")
    bias_lanes = heads_here * lane_rows
    d_bias = got[:, :bias_lanes].reshape(H, lane_rows, 128)
    node_sum = jnp.sum(got[:, bias_lanes:].astype(F32), axis=0)
    (p0,) = call(
        out_product_kernel, 1, [whole(slabs0)], [slab1], chan_flops, [block, block]
    )
    p0, d_bias, node_sum = tie(p0, d_bias, node_sum)
    prod0 = to_pairs(p0)
    prod0, d_kv = tie(prod0, d_kv)
    d_kv = swap_all(half(d_kv).reshape(row_count, -1, 128), "row")
    d_kv = jnp.sum(d_kv.astype(F32), axis=0).reshape(tile_rows * items, 2 * head_width)
    d_qkv = half(jnp.concatenate([d_query.reshape(-1, head_width), d_kv], axis=1))
    dw_qkv_own = dot(d_qkv, node_rows, 0, 0)
    pair_two, sides1 = call(
        middle_kernel,
        steps,
        [
            chan(pair_one),
            rows_of(prod0),
            keep_in,
            g_in[0],
            whole(w_in_t[0][4 * CH :]),
            g_out[0],
            whole(w_out_t[0]),
            g_in[1],
            whole(w_in_t[1]),
        ],
        [f_chan(), double(sides)],
        7 * pos_flops,
    )
    sides1, d_qkv = tie(sides1, d_qkv)
    slabs1 = to_channels(sides1)
    slabs1, d_qkv = tie(slabs1, d_qkv)
    d_att = swap_all(half(dot(d_qkv, w_local, 1, 1)).reshape(col_count, -1, 128), "col")
    d_att = jnp.sum(d_att.astype(F32), axis=0).reshape(share, D)
    d_bias32 = d_bias.astype(F32)
    grad_dist = from_slots(jnp.sum(d_bias32 * w_dist[:, None, None], axis=0))
    dw_dist = jnp.sum(d_bias32 * dist_slots[None], axis=(1, 2))
    d_bias_chan = d_bias.reshape(H, slots)

    (p1,) = call(
        in_product_kernel,
        1,
        [whole(slabs1), whole(eye_lanes)],
        [slab1],
        chan_flops,
        [block, block],
    )
    p1, d_att = tie(p1, d_att)
    prod1 = to_pairs(p1)
    head_grads = jnp.concatenate([dw_qkv_own, dwo_own], axis=0)
    prod1, head_grads = tie(prod1, head_grads)
    head_grads = swap_all(head_grads.reshape(row_count, -1, 128), "row")
    head_grads = jnp.sum(head_grads, axis=0)
    (
        pair_out,
        grad2,
        dprod1,
        dog1,
        dw_down,
        dw_up_t,
        dg_trans,
        dw_out1_t,
        dg_out1,
    ) = call(
        turn_kernel,
        steps,
        [
            chan(pair_two),
            rows_of(prod1),
            tile(split_tile(pair_cotan)),
            whole(eye),
            g_in[1],
            whole(w_in_t[1][4 * CH :]),
            g_out[1],
            whole(w_out_t[1]),
            whole(w_tout[1]),
            column(g_trans),
            whole(jnp.transpose(w_up)),
            whole(w_up),
            whole(jnp.transpose(w_down)),
            whole(w_down),
        ],
        [
            tile(sds((items, 2, il, tile_cols, C), F32)),
            f_chan(),
            rows_of(single),
            chan(sds((C, slots), BF16)),
            f_whole(FT, C),
            f_whole(FT, C),
            f_whole(C, 128),
            f_whole(C, CH),
            f_whole(CH, 128),
        ],
        30 * pos_flops,
    )
    dprod1, head_grads = tie(dprod1, head_grads)
    dp1 = to_channels(dprod1)
    (d1,) = call(
        in_back_kernel,
        1,
        [whole(slabs1), whole(dp1)],
        [slab2],
        2 * chan_flops,
        [block, block, block],
    )
    dsides1 = to_pairs(d1)
    grad1, dprod0, dog0, dw_in1_t, dg_in1, dw_out0_t, dg_out0 = call(
        back_kernel,
        steps,
        [
            chan(pair_two),
            chan(pair_one),
            rows_of(prod0),
            double(dsides1),
            chan(dog1),
            chan(grad2),
            keep_in,
            g_in[1],
            whole(w_in_t[1]),
            whole(w_tin[1]),
            g_in[0],
            whole(w_in_t[0][4 * CH :]),
            g_out[0],
            whole(w_out_t[0]),
            whole(w_tout[0]),
        ],
        [
            f_chan(),
            rows_of(single),
            chan(sds((C, slots), BF16)),
            f_whole(5 * CH, C),
            f_whole(C, 128),
            f_whole(C, CH),
            f_whole(CH, 128),
        ],
        20 * pos_flops,
    )
    dp0 = to_channels(dprod0)
    mid_arrays = [
        dw_in1_t,
        dw_out0_t,
        lane_sum(dg_in1),
        lane_sum(dg_out0),
        dw_down,
        dw_up_t,
        dw_out1_t,
        jnp.pad(dw_dist, (0, 128 - H))[None],
        lane_sum(dg_trans),
        lane_sum(dg_out1),
    ]
    mid_sent = half(padded(mid_arrays))
    dp0, mid_sent = tie(dp0, mid_sent)
    mid_part = scatter_sum(mid_sent)
    (d0,) = call(
        out_back_kernel,
        1,
        [whole(slabs0), whole(dp0), whole(eye_lanes)],
        [slab2],
        2 * chan_flops,
        [block, block, block, block32],
    )
    d0, mid_part = tie(d0, mid_part)
    dsides0 = to_pairs(d0)
    mid_part = half(jnp.concatenate([mid_part, head_grads], axis=0))
    dsides0, mid_part = tie(dsides0, mid_part)
    mid_all = spread(mid_part, BOTH)
    grad_pair, d_middle, dw_in0_t, dg_in0, d_right_wide, db_outer, dw_bias_t = call(
        close_kernel,
        steps,
        [
            chan(pair_one),
            chan(x_chan),
            double(dsides0),
            chan(dog0),
            chan(grad1),
            keep_in,
            g_in[0],
            whole(w_in_t[0]),
            whole(w_tin[0]),
            pairs_of(middle),
            bd,
            chan(d_bias_chan),
            whole(w_bias),
        ],
        [
            tile(sds((items, 2, il, tile_cols, C), F32)),
            pairs_of(sds(middle.shape, F32)),
            f_whole(5 * CH, C),
            f_whole(C, 128),
            f_whole(*right_wide.shape),
            f_whole(C, 128),
            f_whole(H, C),
        ],
        18 * pos_flops,
    )

    grad_pair, mid_all, d_middle = tie(grad_pair, mid_all, d_middle)
    mid_rows = mid_all.shape[1] - head_grads.shape[0]
    d_middle = jnp.transpose(half(d_middle).reshape(il, 2, items * OP, C), (1, 0, 2, 3))
    d_middle = d_middle.reshape(tile_rows * items, OP * C)
    dw_outer = dot(left_node, d_middle, 0, 0)
    d_left = dot(d_middle, w_outer, 1, 1)
    d_right = jnp.einsum(
        "zxqxj->zxqj", d_right_wide.reshape(JH, 2 * items, OP, 2 * items, jl)
    )
    d_right = jnp.sum(d_right.reshape(JH, 2, items, OP, jl), axis=1)
    d_right = jnp.transpose(d_right, (0, 3, 1, 2))
    d_right = d_right.reshape(tile_cols * items, OP)
    unit_ab = jnp.concatenate(
        [dot(half(node_unit), half(d_left), 0, 0), dot(half(col_unit), half(d_right), 0, 0)],
        axis=1,
    )
    late_arrays = [
        dw_in0_t,
        dw_outer.reshape(-1, 128),
        unit_ab.reshape(-1, 128),
        dw_bias_t,
        lane_sum(dg_in0),
        lane_sum(db_outer),
    ]
    own_row = (jnp.arange(row_count) == row_index).astype(F32)
    own_col = (jnp.arange(row_count) // parts == col_index).astype(F32)
    send_left = own_row[:, None, None, None] * d_left.reshape(1, col_count, share, OP)
    send_right = own_col[:, None, None, None] * jnp.tile(
        d_right.reshape(parts, col_count, share, OP), (group, 1, 1, 1)
    )
    sent = half(jnp.concatenate([send_left, send_right], axis=-1)).reshape(devices, -1, 128)
    rows = sent.shape[1]
    sent = jnp.concatenate([sent, half(padded(late_arrays))], axis=1)
    got = scatter_sum(sent)
    late_part = got[rows:]
    d_pair_rows = half(got[:rows]).reshape(share, 2 * OP)
    node_share = lax.dynamic_slice_in_dim(node_full, col_index * share, share, 0)
    cot_share = lax.dynamic_slice_in_dim(cot_rows, col_index * share, share, 0)
    unit, inv = node_norm(node_share)
    d_normed = half(dot(d_pair_rows, w_ab, 1, 1)).astype(F32)
    scaled = d_normed * g_node
    d_norm = inv * (
        scaled
        - jnp.mean(scaled, axis=-1, keepdims=True)
        - unit * jnp.mean(scaled * unit, axis=-1, keepdims=True)
    )
    grad_share = cot_share.astype(F32) + d_att + d_norm
    out_share = node_share + node_sum.reshape(share, D)
    nodes = spread(jnp.stack([out_share, grad_share]).reshape(-1, 128), "col")
    nodes = nodes.reshape(col_count, 2, share, D)

    def node_result(which):
        array = nodes[:, which].reshape(tile_rows, items, D)
        return jnp.transpose(array, (1, 0, 2))

    head_grads = mid_all[:, mid_rows:].astype(F32).reshape(row_count, col_count, -1)
    head_grads = jnp.transpose(head_grads, (1, 0, 2)).reshape(col_count, 4, head_width, D)
    g_qkv = jnp.transpose(head_grads[:, :3], (3, 1, 0, 2)).reshape(D, 3 * D)
    g_node_out = head_grads[:, 3].reshape(D, D)

    def cut(flat, arrays):
        start, pieces = 0, []
        for array in arrays:
            pieces.append(flat[start : start + array.shape[0]])
            start += array.shape[0]
        return pieces

    (
        s_in1_t,
        s_out0_t,
        s_gin1,
        s_gout0,
        s_down,
        s_up_t,
        s_out1_t,
        s_dist,
        s_trans,
        s_gout1,
    ) = cut(mid_all[:, :mid_rows].reshape(-1, 128).astype(F32), mid_arrays)
    late_all = spread(half(late_part), BOTH).reshape(-1, 128).astype(F32)
    s_in0_t, s_outer, s_ab, s_bias_t, s_gin0, s_bout = cut(late_all, late_arrays)
    s_ab = s_ab.reshape(D, 2 * OP)
    s_gnode = jnp.sum(s_ab * w_ab.astype(F32), axis=1)
    s_ab = s_ab * g_node[:, None]
    return (
        node_result(0),
        pair_out.reshape(pair_feats.shape),
        node_result(1),
        grad_pair.reshape(pair_feats.shape),
        grad_dist,
        g_qkv,
        jnp.transpose(s_bias_t),
        s_dist[0, :H],
        g_node_out,
        s_gnode,
        s_ab,
        s_outer.reshape(OP, OP * C),
        s_bout.reshape(C),
        jnp.concatenate([s_gin0, s_gin1]),
        jnp.stack([jnp.transpose(s_in0_t), jnp.transpose(s_in1_t)]),
        jnp.concatenate([s_gout0, s_gout1]),
        jnp.stack([jnp.transpose(s_out0_t), jnp.transpose(s_out1_t)]),
        s_trans[0],
        jnp.transpose(s_up_t),
        s_down,
    )


def solution(mesh):
    pair = P(None, "row", "col", None)
    node = P(None, "row", None)
    dist = P(None, "row", "col")
    return jax.shard_map(
        per_device,
        mesh=mesh,
        in_specs=(node, pair, dist, P(), node, pair) + (P(),) * 15,
        out_specs=(node, pair, node, pair, dist) + (P(),) * 15,
        check_vma=False,
    )
```

```python
import functools

import jax
import jax.numpy as jnp
import ml_dtypes
import numpy as np
from jax import lax
from jax.experimental import pallas as pl
from jax.experimental.pallas import tpu as pltpu
from jax.sharding import PartitionSpec as P

D = 256
C = 128
H = 8
HD = 32
CH = 128
OP = 32
FT = 512
ITEMS = 4
EPS = 1e-05
BOTH = ("row", "col")
F32 = jnp.float32
BF16 = jnp.bfloat16
HALF = 64
JH = 3
VMEM = 60 * 1024 * 1024
SMALL_VMEM = 28 * 1024 * 1024


def half(values):
    return values.astype(BF16)


def dot(lhs, rhs, lhs_dim, rhs_dim):
    return lax.dot_general(
        lhs, rhs, (((lhs_dim,), (rhs_dim,)), ((), ())), preferred_element_type=F32
    )


def sigmoid(values):
    return 0.5 * jnp.tanh(0.5 * values) + 0.5


def norm_parts(values):
    scale = 1.0 / values.shape[0]
    centered = values - jnp.sum(values, axis=0, keepdims=True) * scale
    spread = jnp.sum(centered * centered, axis=0, keepdims=True) * scale
    inv = lax.rsqrt(spread + EPS)
    return centered * inv, inv


def norm_back(unit, inv, gain, grad):
    scale = 1.0 / unit.shape[0]
    scaled = grad * gain
    first = jnp.sum(scaled, axis=0, keepdims=True) * scale
    second = jnp.sum(scaled * unit, axis=0, keepdims=True) * scale
    return inv * (scaled - first - unit * second)


def lane_rows_of(width):
    return [(m, slice(128 * m, 128 * m + 128)) for m in range(width // 128)]


def tile_rows_of(ref):
    items, parts, rows = ref.shape[:3]
    return jnp.concatenate(
        [ref[b, h, m] for m in range(rows) for h in range(parts) for b in range(items)],
        axis=0,
    )


def put_tile(ref, m, values):
    items, parts, _, cols = ref.shape[:4]
    flipped = jnp.transpose(values)
    start = 0
    for h in range(parts):
        for b in range(items):
            ref[b, h, m] = flipped[start : start + cols]
            start += cols


def low_lanes(rows):
    return lax.broadcasted_iota(jnp.int32, (rows, 128), 1) < HALF


def swap(values):
    return pltpu.roll(values, HALF, 1)


def put_double(ref, m, left, right):
    low = low_lanes(left.shape[0])
    ref[0, 0, m] = half(jnp.where(low, left, swap(right)))
    ref[0, 1, m] = half(jnp.where(low, swap(left), right))


def get_double(ref, m):
    low = low_lanes(ref.shape[3])
    one, two = ref[0, 0, m].astype(F32), ref[0, 1, m].astype(F32)
    return jnp.where(low, one, swap(two)), jnp.where(low, swap(one), two)


def add_to(ref, values):
    @pl.when(pl.program_id(0) == 0)
    def _():
        ref[...] = values

    @pl.when(pl.program_id(0) != 0)
    def _():
        ref[...] += values


def add_diagonal(ref, total_ref, grad_ref, unit_ref):
    add_to(total_ref, dot(grad_ref[...], unit_ref[...], 1, 1))

    @pl.when(pl.program_id(0) == pl.num_programs(0) - 1)
    def _():
        rows = lax.broadcasted_iota(jnp.int32, total_ref.shape, 0)
        cols = lax.broadcasted_iota(jnp.int32, total_ref.shape, 1)
        picked = jnp.where(rows == cols, total_ref[...], 0.0)
        ref[...] = jnp.broadcast_to(jnp.sum(picked, axis=0, keepdims=True), ref.shape)


def bias_kernel(pair_ref, eye_ref, wb_ref, wd_ref, dist_ref, x_ref, bias_ref):
    x_chan = half(dot(eye_ref[...], tile_rows_of(pair_ref), 1, 1))
    x_ref[...] = x_chan
    bias_ref[...] = half(dot(wb_ref[...], x_chan, 0, 0) + wd_ref[...] * dist_ref[...])


def cotangent_kernel(cot_ref, eye_ref, wdown_plain_ref, out_ref, dact_ref):
    cot = half(dot(eye_ref[...], tile_rows_of(cot_ref), 1, 1))
    out_ref[...] = cot
    dact_ref[...] = half(dot(wdown_plain_ref[...], cot, 1, 0))


def put_sides(proj_ref, keep_ref, sides_ref, wide_ref):
    count = keep_ref.shape[1]
    for m, here in lane_rows_of(proj_ref.shape[1]):
        keep = keep_ref[0, m : m + 1, :]
        left = sigmoid(proj_ref[CH : 2 * CH, here]) * proj_ref[:CH, here] * keep
        right = (
            sigmoid(proj_ref[3 * CH : 4 * CH, here]) * proj_ref[2 * CH : 3 * CH, here] * keep
        )
        low = low_lanes(left.shape[0])
        wide_ref[:, m, :] = jnp.where(low, left, swap(right))
        wide_ref[:, m + count, :] = jnp.where(low, swap(left), right)
    sides_ref[...] = half(wide_ref[...])


def diagonal_blocks(right):
    which = lax.broadcasted_iota(jnp.int32, (8, 128), 0)
    lane = lax.broadcasted_iota(jnp.int32, (8, 128), 1) // 16
    same = (which == lane).astype(F32)
    return half(jnp.concatenate([same * right[q : q + 1] for q in range(OP)], axis=0))


def node_kernel(node_ref, col_ref, gain_ref, wab_ref, wout_ref, perm_ref, mid_ref, right_ref):
    def normed(ref):
        values = ref[...].astype(F32)
        scale = 1.0 / values.shape[1]
        centered = values - jnp.sum(values, axis=1, keepdims=True) * scale
        spread = jnp.sum(centered * centered, axis=1, keepdims=True) * scale
        return half(centered * lax.rsqrt(spread + EPS) * gain_ref[...])

    left = half(dot(wab_ref[...], normed(node_ref), 0, 1))
    mid_ref[...] = dot(left[:OP], wout_ref[...], 0, 0)
    right = half(dot(wab_ref[...], normed(col_ref), 0, 1))
    right = dot(right[OP:], perm_ref[...], 1, 0)
    for j in range(JH):
        right_ref[j] = right[:, 128 * j : 128 * j + 128]


def open_kernel(
    pair_ref,
    eye_ref,
    mid_ref,
    bd_ref,
    bout_ref,
    keep_ref,
    gain_ref,
    w_ref,
    one_ref,
    sides_ref,
    mids_ref,
    mid_t_ref,
    outer_ref,
    normed_ref,
    proj_ref,
    x_ref,
    wide_ref,
):
    @pl.when(pl.program_id(0) == 0)
    def _():
        for m in range(mids_ref.shape[1] // 128):
            rows = [
                mid_ref[8 * m : 8 * m + 8, 128 * q : 128 * q + 128] for q in range(OP)
            ]
            stack = jnp.concatenate(rows, axis=0)
            mids_ref[:, 128 * m : 128 * m + 128] = half(stack)
            mid_t_ref[128 * m : 128 * m + 128, :] = half(jnp.transpose(stack))

    x_ref[...] = half(dot(eye_ref[...], tile_rows_of(pair_ref), 1, 1))
    outer_ref[...] = dot(mid_t_ref[...], diagonal_blocks(bd_ref[0]), 1, 0)
    for m, here in lane_rows_of(x_ref.shape[1]):
        outer = outer_ref[128 * m : 128 * m + 128, :]
        keep = keep_ref[0, m : m + 1, :]
        pair_one = x_ref[:, here].astype(F32) + keep * (outer + bout_ref[0])
        one_ref[:, here] = pair_one
        unit, _ = norm_parts(pair_one)
        normed_ref[:, here] = half(unit * gain_ref[0])
    proj_ref[...] = dot(w_ref[0, :, : 4 * CH], normed_ref[...], 0, 0)
    put_sides(proj_ref, keep_ref, sides_ref, wide_ref)


def factor_kernel(
    in_ref, keep_ref, gain_ref, w_ref, unit_ref, inv_ref, normed_ref, factor_ref, *rest
):
    proj_ref = rest[-1]
    for _, here in lane_rows_of(in_ref.shape[1]):
        unit, inv = norm_parts(in_ref[:, here])
        unit_ref[:, here] = half(unit)
        inv_ref[:, here] = inv
        normed_ref[:, here] = half(unit * gain_ref[0])
    proj_ref[...] = dot(w_ref[0], normed_ref[...], 0, 0)
    for m, here in lane_rows_of(in_ref.shape[1]):
        keep = keep_ref[0, m : m + 1, :]
        for side in range(2):
            start = 2 * CH * side
            sig = sigmoid(proj_ref[start + CH : start + 2 * CH, here])
            first = keep * sig
            factor_ref[start : start + CH, here] = half(first)
            factor_ref[start + CH : start + 2 * CH, here] = half(
                first * proj_ref[start : start + CH, here] * (1.0 - sig)
            )
        if len(rest) > 1:
            rest[0][:, here] = half(sigmoid(proj_ref[4 * CH :, here]))


def rear_kernel(
    prod_ref, gate_ref, gout_ref, wout_ref, unit_ref, inv_ref, slope_ref, y_ref, update_ref
):
    for m, here in lane_rows_of(gate_ref.shape[1]):
        unit, inv = norm_parts(prod_ref[m].astype(F32))
        unit_ref[:, here] = half(unit)
        inv_ref[:, here] = inv
        y_ref[:, here] = half(unit * gout_ref[0])
    update_ref[...] = dot(wout_ref[0], y_ref[...], 0, 0)
    for _, here in lane_rows_of(gate_ref.shape[1]):
        gate = gate_ref[:, here].astype(F32)
        slope_ref[:, here] = half(update_ref[:, here] * gate * (1.0 - gate))


def middle_kernel(
    one_ref,
    gate_ref,
    prod_ref,
    keep_ref,
    gout_ref,
    wout_ref,
    gin_ref,
    w_ref,
    two_ref,
    sides_ref,
    gate_out_ref,
    y_ref,
    update_ref,
    proj_ref,
    wide_ref,
):
    for m, here in lane_rows_of(one_ref.shape[1]):
        unit, _ = norm_parts(prod_ref[m].astype(F32))
        y_ref[:, here] = half(unit * gout_ref[0])
    update_ref[...] = dot(wout_ref[0], y_ref[...], 0, 0)
    for _, here in lane_rows_of(one_ref.shape[1]):
        pair_two = one_ref[:, here] + gate_ref[:, here].astype(F32) * update_ref[:, here]
        two_ref[:, here] = pair_two
        unit, _ = norm_parts(pair_two)
        y_ref[:, here] = half(unit * gin_ref[0])
    proj_ref[...] = dot(w_ref[0], y_ref[...], 0, 0)
    put_sides(proj_ref, keep_ref, sides_ref, wide_ref)
    for _, here in lane_rows_of(one_ref.shape[1]):
        gate_out_ref[:, here] = half(sigmoid(proj_ref[4 * CH :, here]))


def transition(two_ref, gate_ref, prod_ref, gout_ref, wout_ref, gtr_ref, wup_ref, refs):
    y_ref, prod_unit_ref, prod_inv_ref, update_ref = refs[:4]
    three_ref, xt_ref, tr_unit_ref, tr_inv_ref, hidden_ref = refs[4:]
    rows = lane_rows_of(two_ref.shape[1])
    for m, here in rows:
        unit, inv = norm_parts(prod_ref[m].astype(F32))
        if prod_unit_ref is not None:
            prod_inv_ref[:, here] = inv
            prod_unit_ref[:, here] = half(unit)
        y_ref[:, here] = half(unit * gout_ref[0])
    update_ref[...] = dot(wout_ref[0], y_ref[...], 0, 0)
    for _, here in rows:
        pair_three = (
            two_ref[:, here] + gate_ref[:, here].astype(F32) * update_ref[:, here]
        )
        if three_ref is not None:
            three_ref[:, here] = pair_three
        unit, inv = norm_parts(pair_three)
        if tr_unit_ref is not None:
            tr_inv_ref[:, here] = inv
            tr_unit_ref[:, here] = half(unit)
        xt_ref[:, here] = half(unit * gtr_ref[0])
    hidden_ref[...] = dot(wup_ref[...], xt_ref[...], 0, 0)


def put_hidden_back(hidden_ref, dact_ref, dhid_ref, active_ref=None):
    for _, here in lane_rows_of(hidden_ref.shape[1]):
        for start in range(0, FT, CH):
            part = slice(start, start + CH)
            hidden = hidden_ref[part, here]
            sig = sigmoid(hidden)
            act32 = hidden * sig
            if active_ref is not None:
                active_ref[part, here] = half(act32)
            dhid_ref[part, here] = half(
                dact_ref[part, here].astype(F32) * (sig + act32 * (1.0 - sig))
            )


def turn_kernel(
    two_ref,
    gate_ref,
    prod_ref,
    cot_ref,
    dact_ref,
    gout_ref,
    wout_ref,
    gtr_ref,
    wup_ref,
    grad_ref,
    dprod_ref,
    dgtr_ref,
    dgout_ref,
    small_ref,
    xt_ref,
    tr_unit_ref,
    tr_inv_ref,
    prod_unit_ref,
    prod_inv_ref,
    update_ref,
    hidden_ref,
    dhid_ref,
    tr_total_ref,
    out_total_ref,
):
    rows = lane_rows_of(two_ref.shape[1])
    refs = (small_ref, prod_unit_ref, prod_inv_ref, update_ref)
    refs += (None, xt_ref, tr_unit_ref, tr_inv_ref, hidden_ref)
    transition(two_ref, gate_ref, prod_ref, gout_ref, wout_ref, gtr_ref, wup_ref, refs)
    put_hidden_back(hidden_ref, dact_ref, dhid_ref)
    small_ref[...] = half(dot(wup_ref[...], dhid_ref[...], 1, 0))
    for _, here in rows:
        grad = cot_ref[:, here].astype(F32) + norm_back(
            tr_unit_ref[:, here].astype(F32),
            tr_inv_ref[:, here],
            gtr_ref[0],
            small_ref[:, here].astype(F32),
        )
        grad_ref[:, here] = grad
        xt_ref[:, here] = half(grad * gate_ref[:, here].astype(F32))
    add_diagonal(dgtr_ref, tr_total_ref, small_ref, tr_unit_ref)
    small_ref[...] = half(dot(wout_ref[0], xt_ref[...], 1, 0))
    put_product_back(dprod_ref, prod_unit_ref, prod_inv_ref, gout_ref, small_ref)
    add_diagonal(dgout_ref, out_total_ref, small_ref, prod_unit_ref)


def put_product_back(dprod_ref, unit_ref, inv_ref, gain_ref, dy_ref):
    for m, here in lane_rows_of(unit_ref.shape[1]):
        dprod_ref[m] = half(
            norm_back(
                unit_ref[:, here].astype(F32),
                inv_ref[:, here],
                gain_ref[0],
                dy_ref[:, here].astype(F32),
            )
        )


def finish_kernel(
    two_ref,
    gate_ref,
    prod_ref,
    cot_ref,
    dact_ref,
    grad_ref,
    gout_ref,
    wout_ref,
    gtr_ref,
    wup_ref,
    wdown_ref,
    out_ref,
    dwdown_ref,
    dwup_ref,
    dwout_ref,
    y_ref,
    xt_ref,
    update_ref,
    three_ref,
    hidden_ref,
    dhid_ref,
    active_ref,
    dwup_t_ref,
):
    refs = (y_ref, None, None, update_ref, three_ref, xt_ref, None, None, hidden_ref)
    transition(two_ref, gate_ref, prod_ref, gout_ref, wout_ref, gtr_ref, wup_ref, refs)
    put_hidden_back(hidden_ref, dact_ref, dhid_ref, active_ref)
    update_ref[...] = dot(wdown_ref[...], active_ref[...], 0, 0)
    for m, here in lane_rows_of(two_ref.shape[1]):
        put_tile(out_ref, m, three_ref[:, here] + update_ref[:, here])
    add_to(dwdown_ref, dot(active_ref[...], cot_ref[...], 1, 1))
    add_to(dwup_t_ref, dot(dhid_ref[...], xt_ref[...], 1, 1))
    d_update = half(grad_ref[...] * gate_ref[...].astype(F32))
    add_to(dwout_ref, dot(y_ref[...], d_update, 1, 1))

    @pl.when(pl.program_id(0) == pl.num_programs(0) - 1)
    def _():
        put_flipped(dwup_ref, dwup_t_ref)


def put_front_grads(sides_ref, factor_ref, slope_ref, grad_ref, dproj_ref):
    for m, here in lane_rows_of(grad_ref.shape[1]):
        sides = get_double(sides_ref, m)
        for at in range(4):
            part = slice(CH * at, CH * at + CH)
            dproj_ref[part, here] = half(sides[at // 2] * factor_ref[part, here].astype(F32))
        dproj_ref[4 * CH :, here] = half(grad_ref[:, here] * slope_ref[:, here].astype(F32))


def front_back(unit_ref, inv_ref, gain_ref, dn_ref, here):
    return norm_back(
        unit_ref[:, here].astype(F32),
        inv_ref[:, here],
        gain_ref[0],
        dn_ref[:, here].astype(F32),
    )


def back_kernel(
    dsides_ref,
    factor_ref,
    slope_ref,
    unit_ref,
    inv_ref,
    grad_ref,
    gin_ref,
    w_ref,
    gate_ref,
    prod_unit_ref,
    prod_inv_ref,
    gout_ref,
    wout_ref,
    grad_out_ref,
    dprod_ref,
    dgin_ref,
    dgout_ref,
    dproj_ref,
    dupd_ref,
    small_ref,
    in_total_ref,
    out_total_ref,
):
    put_front_grads(dsides_ref, factor_ref, slope_ref, grad_ref, dproj_ref)
    small_ref[...] = half(dot(w_ref[0], dproj_ref[...], 1, 0))
    for _, here in lane_rows_of(grad_ref.shape[1]):
        grad = grad_ref[:, here] + front_back(unit_ref, inv_ref, gin_ref, small_ref, here)
        grad_out_ref[:, here] = grad
        dupd_ref[:, here] = half(grad * gate_ref[:, here].astype(F32))
    add_diagonal(dgin_ref, in_total_ref, small_ref, unit_ref)
    small_ref[...] = half(dot(wout_ref[0], dupd_ref[...], 1, 0))
    put_product_back(dprod_ref, prod_unit_ref, prod_inv_ref, gout_ref, small_ref)
    add_diagonal(dgout_ref, out_total_ref, small_ref, prod_unit_ref)


def put_flipped(out_ref, total_ref):
    for start in range(0, total_ref.shape[0], 128):
        out_ref[start : start + 128, :] = jnp.transpose(total_ref[start : start + 128, :])


def weights_kernel(
    dsides_ref,
    factor_ref,
    slope_ref,
    grad_ref,
    normed_ref,
    next_grad_ref,
    gate_ref,
    prod_unit_ref,
    gout_ref,
    dbias_ref,
    x_ref,
    dwin_ref,
    dwout_ref,
    dwb_ref,
    dproj_ref,
    dwin_t_ref,
):
    put_front_grads(dsides_ref, factor_ref, slope_ref, grad_ref, dproj_ref)
    add_to(dwin_t_ref, dot(dproj_ref[...], normed_ref[...], 1, 1))

    @pl.when(pl.program_id(0) == pl.num_programs(0) - 1)
    def _():
        put_flipped(dwin_ref, dwin_t_ref)

    d_update = half(next_grad_ref[...] * gate_ref[...].astype(F32))
    y_half = half(prod_unit_ref[...].astype(F32) * gout_ref[0])
    add_to(dwout_ref, dot(y_half, d_update, 1, 1))
    add_to(dwb_ref, dot(dbias_ref[...], x_ref[...], 1, 1))


def close_kernel(
    dsides_ref,
    factor_ref,
    slope_ref,
    unit_ref,
    inv_ref,
    grad_ref,
    keep_ref,
    gin_ref,
    w_ref,
    mids_ref,
    bd_ref,
    dbias_ref,
    wb_ref,
    out_ref,
    dmid_ref,
    dwin_ref,
    dgin_ref,
    dright_ref,
    dbout_ref,
    dproj_ref,
    small_ref,
    outer_ref,
    in_total_ref,
    dmid_t_ref,
    bias_ref,
    dwin_t_ref,
):
    put_front_grads(dsides_ref, factor_ref, slope_ref, grad_ref, dproj_ref)
    small_ref[...] = half(dot(w_ref[0], dproj_ref[...], 1, 0))
    bias_ref[...] = dot(wb_ref[...], dbias_ref[...], 1, 0)
    total = None
    for m, here in lane_rows_of(grad_ref.shape[1]):
        grad = grad_ref[:, here] + front_back(unit_ref, inv_ref, gin_ref, small_ref, here)
        put_tile(out_ref, m, grad + bias_ref[:, here])
        outer = grad * keep_ref[0, m : m + 1, :]
        outer_ref[128 * m : 128 * m + 128, :] = half(outer)
        total = outer if total is None else total + outer
    normed = half(unit_ref[...].astype(F32) * gin_ref[0])
    add_to(dmid_t_ref, dot(outer_ref[...], diagonal_blocks(bd_ref[0]), 1, 1))
    right = dot(mids_ref[...], outer_ref[...], 1, 0)
    which = lax.broadcasted_iota(jnp.int32, (8, 128), 0)
    lane = lax.broadcasted_iota(jnp.int32, (8, 128), 1) // 16
    for q in range(OP):
        picked = jnp.where(which == lane, right[8 * q : 8 * q + 8], 0.0)
        dright_ref[0, q : q + 1, :] = jnp.sum(picked, axis=0, keepdims=True)
    add_to(dwin_t_ref, dot(dproj_ref[...], normed, 1, 1))
    ones = jnp.ones((8, 128), F32)
    add_to(
        dbout_ref,
        lax.dot_general(
            ones,
            total,
            (((1,), (1,)), ((), ())),
            preferred_element_type=F32,
            precision=lax.Precision.HIGHEST,
        ),
    )
    add_diagonal(dgin_ref, in_total_ref, small_ref, unit_ref)

    @pl.when(pl.program_id(0) == pl.num_programs(0) - 1)
    def _():
        for m in range(dmid_t_ref.shape[0] // 128):
            stack = jnp.transpose(dmid_t_ref[128 * m : 128 * m + 128, :])
            for q in range(OP):
                dmid_ref[8 * m : 8 * m + 8, 128 * q : 128 * q + 128] = stack[
                    8 * q : 8 * q + 8
                ]
        put_flipped(dwin_ref, dwin_t_ref)


def tail_kernel(count, *refs):
    weight_refs, refs = refs[:count], refs[count:]
    dmid_ref, left_ref, wouter_ref, unit_ref, dright_ref, col_unit_ref = refs[:6]
    wouter_pad_ref, pick_left_ref, pick_right_ref, mask_ref = refs[6:10]
    out_ref, outer_ref, small_ref = refs[10:]
    d_mid = half(dmid_ref[...])
    outer = dot(left_ref[...], d_mid, 0, 0)
    for q in range(OP):
        outer_ref[OP * q : OP * q + OP, :] = outer[:, 128 * q : 128 * q + 128]
    d_left = dot(d_mid, wouter_ref[...], 1, 1)
    sums = [dot(half(d_left), unit_ref[...], 0, 0)]
    total = None
    for j in range(JH):
        part = dot(half(dright_ref[j]), col_unit_ref[j], 1, 0)
        total = part if total is None else total + part
    sums = jnp.concatenate(sums + [total], axis=0)
    small_ref[: 2 * OP, :] = sums[:, :128]
    small_ref[2 * OP :, :] = sums[:, 128:]
    lefts, rights = None, [None, None]
    for s in range(2):
        part = half(dot(d_mid, wouter_pad_ref[s], 1, 1))
        part = dot(pick_left_ref[s], part, 1, 0)
        lefts = part if lefts is None else lefts + part
        for j in range(JH):
            above = jnp.zeros((HALF * s + OP, 128), F32)
            spread = [above, dright_ref[j]]
            if s == 0:
                spread.append(jnp.zeros((HALF, 128), F32))
            spread = jnp.concatenate(spread, axis=0)
            spread = half(jnp.transpose(spread))
            for h in range(2):
                part = dot(pick_right_ref[h, s, j], spread, 1, 0)
                rights[h] = part if rights[h] is None else rights[h] + part
    sources = list(weight_refs) + [outer_ref, small_ref]
    pieces = [(ref, at) for ref in sources for at in range(0, ref.shape[0], 8)]
    rows = mask_ref.shape[0] // 2
    cols = out_ref.shape[0] // rows
    for r in range(rows):
        nodes = mask_ref[r : r + 1] * lefts + mask_ref[rows + r : rows + r + 1] * rights[r % 2]
        for c in range(cols):
            at = 3 * (r * cols + c)
            parts = [ref[k : k + 8, :] for ref, k in pieces[at : at + 3]]
            parts += [jnp.zeros((8, 128), F32)] * (3 - len(parts))
            out_ref[r * cols + c] = half(
                jnp.concatenate(parts + [nodes[8 * c : 8 * c + 8]], axis=0)
            )


def item_masks(items, cols, dtype):
    lane = lax.broadcasted_iota(jnp.int32, (1, 256 * cols), 1) % 256
    which = (lane // 16) % items
    return [((which == b) & (lane < JH * HALF)).astype(F32).astype(dtype) for b in range(items)]


def spread_items(piece, masks):
    parts = [piece[16 * j : 16 * j + 16] * mask for j in range(JH) for mask in masks]
    return jnp.concatenate(
        parts + [jnp.zeros((HALF, piece.shape[1]), piece.dtype)], axis=0
    )


def pick_items(values, masks):
    rows = []
    for j in range(JH):
        total = None
        for b, mask in enumerate(masks):
            start = HALF * j + 16 * b
            part = values[start : start + 16] * mask
            total = part if total is None else total + part
        rows.append(total)
    return jnp.concatenate(rows, axis=0)


def split_lanes(one, two, three):
    low = low_lanes(one.shape[0])
    return (
        jnp.concatenate([jnp.where(low, one, swap(two)), three], axis=1),
        jnp.concatenate([jnp.where(low, swap(one), two), swap(three)], axis=1),
    )


def join_lanes(left, right):
    low = low_lanes(left.shape[0])
    return (
        jnp.where(low, left[:, :128], swap(right[:, :128])),
        jnp.where(low, swap(left[:, :128]), right[:, :128]),
        jnp.where(low, left[:, 128:], swap(right[:, 128:])),
    )


def thirds(values):
    rows = values.shape[0] // JH
    return [values[rows * j : rows * (j + 1)] for j in range(JH)]


def block_lanes(q):
    return pl.ds(pl.multiple_of(q * 256, 256), 256)


def load_double(ref, cols, l_ref, r_ref):
    def step(q, carry):
        for r in range(0, ref.shape[0] // cols, 2):
            left, right = [], []
            for h in range(2):
                one, two = split_lanes(*thirds(ref[(r + h) * cols + q].astype(F32)))
                left.append(one)
                right.append(two)
            rows = slice(24 * r, 24 * r + 48)
            l_ref[rows, block_lanes(q)] = half(jnp.concatenate(left, axis=0))
            r_ref[rows, block_lanes(q)] = half(jnp.concatenate(right, axis=0))
        return carry

    lax.fori_loop(0, cols, step, 0)


def load_single(ref, cols, x_ref):
    def step(q, carry):
        for r in range(0, ref.shape[0] // cols, 2):
            parts = []
            for h in range(2):
                parts += split_lanes(*thirds(ref[(r + h) * cols + q].astype(F32)))
            rows = slice(24 * r, 24 * r + 48)
            x_ref[rows, block_lanes(q)] = half(jnp.concatenate(parts, axis=0))
        return carry

    lax.fori_loop(0, cols, step, 0)


def put_slab(ref, at, left, right):
    ref[at] = half(jnp.concatenate(join_lanes(left, right), axis=0))


def rows_at(at):
    return pl.ds(pl.multiple_of(at * 48, 16), 48)


def stack_blocks(piece_of, cols, masks):
    return jnp.concatenate([spread_items(piece_of(q), masks) for q in range(cols)], axis=0)


def unpack_kernel(s_ref, l_ref, r_ref):
    load_double(s_ref, l_ref.shape[1] // 256, l_ref, r_ref)


def out_product_kernel(s_ref, p_ref, l_ref, r_ref):
    residues, cols = l_ref.shape[0], l_ref.shape[1] // 256
    masks = item_masks(ITEMS, cols, BF16)
    load_double(s_ref, cols, l_ref, r_ref)

    def step(at, carry):
        total = dot(l_ref[...], spread_items(r_ref[rows_at(at), :], masks), 1, 1)
        for r in range(residues // 24):
            tile = total[24 * r : 24 * r + 24]
            put_slab(p_ref, r * cols + at, tile[:12], tile[12:])
        return carry

    lax.fori_loop(0, cols, step, 0)


def flip(values, eye):
    return half(dot(eye, values, 1, 1))


def flip_all(ref, eye_ref, out_ref):
    for q in range(ref.shape[1] // 256):
        part = slice(256 * q, 256 * q + 256)
        out_ref[part, :] = flip(ref[:, part], eye_ref[...])


def in_product_kernel(s_ref, eye_ref, p_ref, l_ref, r_ref, f_ref):
    cols = l_ref.shape[1] // 256
    masks = item_masks(ITEMS, 1, F32)
    load_double(s_ref, cols, l_ref, r_ref)
    flip_all(l_ref, eye_ref, f_ref)

    def step(q, carry):
        total = dot(f_ref[...], r_ref[:, block_lanes(q)], 1, 0)
        for at in range(cols):
            rows = pick_items(total[256 * at : 256 * at + 256], masks)
            for h in range(2):
                tile = rows[24 * h : 24 * h + 24]
                put_slab(p_ref, (2 * at + h) * cols + q, tile[:12], tile[12:])
        return carry

    lax.fori_loop(0, cols, step, 0)


def in_back_kernel(l_ref, r_ref, dp_ref, d_ref, x_ref):
    residues, cols = l_ref.shape[0], l_ref.shape[1] // 256
    masks = item_masks(ITEMS, cols, BF16)
    one_masks = item_masks(ITEMS, 1, BF16)
    load_single(dp_ref, cols, x_ref)

    def step(at, carry):
        left = dot(r_ref[...], spread_items(x_ref[rows_at(at), :], masks), 1, 1)
        wide = stack_blocks(
            lambda q: x_ref[48 * q : 48 * q + 48, block_lanes(at)], cols, one_masks
        )
        right = dot(l_ref[...], wide, 1, 0)
        for r in range(residues // 24):
            rows = slice(24 * r, 24 * r + 24)
            put_slab(d_ref, r * cols + at, left[rows], right[rows])
        return carry

    lax.fori_loop(0, cols, step, 0)


def out_back_kernel(l_ref, r_ref, dp_ref, eye_ref, d_ref, x_ref, g_ref, f_ref):
    residues, cols = l_ref.shape[0], l_ref.shape[1] // 256
    masks = item_masks(ITEMS, 1, F32)
    one_masks = item_masks(ITEMS, 1, BF16)
    load_single(dp_ref, cols, x_ref)
    flip_all(x_ref, eye_ref, f_ref)

    def right_step(q, carry):
        total = dot(f_ref[...], l_ref[:, block_lanes(q)], 1, 0)
        for at in range(cols):
            g_ref[48 * at : 48 * at + 48, block_lanes(q)] = pick_items(
                total[256 * at : 256 * at + 256], masks
            )
        return carry

    lax.fori_loop(0, cols, right_step, 0)

    def left_step(at, carry):
        wide = stack_blocks(
            lambda q: r_ref[48 * q : 48 * q + 48, block_lanes(at)], cols, one_masks
        )
        left = dot(x_ref[...], wide, 1, 0)
        for r in range(residues // 24):
            rows = slice(24 * r, 24 * r + 24)
            put_slab(d_ref, r * cols + at, left[rows], g_ref[rows, block_lanes(at)])
        return carry

    lax.fori_loop(0, cols, left_step, 0)


def cost(flops, nbytes):
    return pl.CostEstimate(flops=int(flops), bytes_accessed=int(nbytes), transcendentals=0)


def call(kernel, steps, ins, outs, flops, scratch=(), vmem=VMEM):
    nbytes = sum(a.size * a.dtype.itemsize for a, _, _ in ins)
    nbytes += sum(s.size * s.dtype.itemsize for s, _, _ in outs)
    return pl.pallas_call(
        kernel,
        grid=(steps,),
        in_specs=[pl.BlockSpec(block, index) for _, block, index in ins],
        out_specs=[pl.BlockSpec(block, index) for _, block, index in outs],
        out_shape=[shape for shape, _, _ in outs],
        scratch_shapes=list(scratch),
        compiler_params=pltpu.CompilerParams(vmem_limit_bytes=vmem),
        cost_estimate=cost(flops, nbytes),
        name=getattr(kernel, "__name__", "tail_kernel"),
    )(*[a for a, _, _ in ins])


def whole(array):
    rank = len(array.shape)
    return (array, tuple(array.shape), lambda s: (0,) * rank)


def sds(shape, dtype):
    return jax.ShapeDtypeStruct(shape, dtype)


def per_device(
    node_feats,
    pair_feats,
    distances,
    lengths,
    node_cotan,
    pair_cotan,
    w_qkv,
    w_bias,
    w_dist,
    w_node_out,
    g_node,
    w_ab,
    w_outer,
    b_outer,
    g_tin,
    w_tin,
    g_tout,
    w_tout,
    g_trans,
    w_up,
    w_down,
):
    row_count = lax.axis_size("row")
    col_count = lax.axis_size("col")
    row_index = lax.axis_index("row")
    col_index = lax.axis_index("col")
    items, tile_rows, tile_cols = pair_feats.shape[:3]
    residues = tile_rows * row_count
    devices = row_count * col_count
    il, jl = tile_rows // 2, tile_cols // JH
    lane_rows = JH * il
    slots = lane_rows * 128
    steps = JH
    width = il * 128
    score_scale = HD ** (-0.5)

    def chan(array):
        return (array, (array.shape[0], width), lambda s: (0, s))

    def rows_of(array):
        return (array, (il, C, 128), lambda s: (s, 0, 0))

    def double(array):
        return (array, (1, 2, il, C, 128), lambda s: (s, 0, 0, 0, 0))

    def tile(array):
        return (array, (items, 2, il, jl, C), lambda s: (0, 0, 0, s, 0))

    def f_chan():
        return chan(sds((C, slots), F32))

    def f_whole(*shape):
        return whole(sds(shape, F32))

    columns = jnp.concatenate([b_outer[None], g_tin, g_tout, g_trans[None]], axis=0)
    columns = columns[:, :, None]

    def column(which):
        return (columns, (1, C, 1), lambda s: (which, 0, 0))

    def layer_of(array):
        return (array, (1,) + array.shape[1:], lambda s: (s, 0, 0))

    def layer(array, which):
        return (array, (1,) + array.shape[1:], lambda s: (which, 0, 0))

    def split_tile(array):
        return array.reshape((items, 2, il) + array.shape[2:])

    def to_slots(array):
        lead = array.shape[:-3]
        array = array.reshape(lead + (items, 2, il, JH, jl))
        at = len(lead)
        order = tuple(range(at)) + tuple(at + d for d in (3, 2, 1, 0, 4))
        return jnp.transpose(array, order).reshape(lead + (lane_rows, 128))

    def from_slots(array):
        lead = array.shape[:-2]
        array = array.reshape(lead + (JH, il, 2, items, jl))
        at = len(lead)
        order = tuple(range(at)) + tuple(at + d for d in (3, 2, 1, 0, 4))
        return jnp.transpose(array, order).reshape(lead + (items, tile_rows, tile_cols))

    def slot_index(dim):
        return lax.broadcasted_iota(jnp.int32, (JH, il, 128), dim)

    lane = slot_index(2)
    row_ids = row_index * tile_rows + (lane // HALF) * il + slot_index(1)
    col_ids = col_index * tile_cols + slot_index(0) * jl + lane % jl
    limit = jnp.tile(jnp.repeat(lengths, jl), 2)[None, None, :]
    keep = ((row_ids < limit) & (col_ids < limit)).astype(F32)
    eye = np.eye(C, dtype=ml_dtypes.bfloat16)
    eye_lanes = np.eye(256, dtype=ml_dtypes.bfloat16)

    def spread(array, axis):
        count = lax.axis_size(axis) if isinstance(axis, str) else devices
        return swap_all(jnp.broadcast_to(array[None], (count,) + array.shape), axis)

    def swap_all(array, axis):
        return lax.all_to_all(array, axis, split_axis=0, concat_axis=0, tiled=True)

    def tie(*arrays):
        return lax.optimization_barrier(arrays)

    node_rows = jnp.transpose(node_feats, (1, 0, 2)).reshape(tile_rows * items, D)
    cot_rows = jnp.transpose(node_cotan, (1, 0, 2)).reshape(tile_rows * items, D)
    node_full = node_rows.astype(F32)
    parts = tile_cols // tile_rows
    group = row_count // parts
    fetched = []
    for turn in range(parts):
        moves = []
        for src in range(devices):
            src_row, src_col = divmod(src, col_count)
            dst_row = ((src_row + turn) % parts) * group + src_col
            moves.append((src, dst_row * col_count + src_row // parts))
        fetched.append(lax.ppermute(node_rows, BOTH, moves))
    first = row_index // group
    fetched = jnp.stack(fetched)
    col_rows = jnp.concatenate(
        [
            lax.dynamic_index_in_dim(fetched, (first - h) % parts, 0, keepdims=False)
            for h in range(parts)
        ],
        axis=0,
    )
    share = tile_rows * items // col_count

    def node_norm(values):
        centered = values - jnp.mean(values, axis=-1, keepdims=True)
        inv = lax.rsqrt(jnp.mean(centered * centered, axis=-1, keepdims=True) + EPS)
        return centered * inv, inv

    heads_here = H // col_count
    head_width = heads_here * HD
    head_start = col_index * head_width
    w_local = jnp.concatenate(
        [
            lax.dynamic_slice_in_dim(w_qkv, part * D + head_start, head_width, 1)
            for part in range(3)
        ],
        axis=1,
    )
    wo_local = lax.dynamic_slice_in_dim(w_node_out, head_start, head_width, 0)
    node_unit, _ = node_norm(node_full)
    normed_node = half(node_unit * g_node)
    left_node = half(dot(normed_node, w_ab[:, :OP], 1, 0))
    col_unit, _ = node_norm(col_rows.astype(F32))
    def il_first(rows):
        rows = rows.reshape(2, il, items, rows.shape[1])
        return jnp.transpose(rows, (1, 0, 2, 3)).reshape(-1, rows.shape[3])

    left_node = il_first(left_node)
    perm = np.zeros((JH, jl, items, JH, 2, items, jl), ml_dtypes.bfloat16)
    for j in range(JH):
        for n in range(jl):
            for b in range(items):
                perm[j, n, b, j, :, b, n] = 1
    middle, right_wide = call(
        node_kernel,
        1,
        [
            whole(il_first(node_rows)),
            whole(col_rows),
            whole(g_node[None]),
            whole(w_ab),
            whole(w_outer),
            whole(perm.reshape(tile_cols * items, JH * 128)),
        ],
        [
            whole(sds((tile_rows * items, OP * C), F32)),
            whole(sds((JH, OP, 128), F32)),
        ],
        1000,
    )
    dist_slots = to_slots(distances)

    def padded(arrays):
        flat = jnp.concatenate(arrays, axis=0)
        rows = -(-flat.shape[0] // (devices * 8)) * 8
        flat = jnp.pad(flat, ((0, devices * rows - flat.shape[0]), (0, 0)))
        return flat.reshape(devices, rows, 128)

    def scatter_sum(array):
        return jnp.sum(swap_all(array, BOTH).astype(F32), axis=0)

    def to_channels(rows):
        return swap_all(jnp.transpose(rows, (1, 0, 2)), BOTH)

    def to_pairs(slabs):
        got = jnp.transpose(swap_all(slabs, BOTH), (1, 0, 2))
        return got if got.shape[0] == lane_rows else got.reshape(sides.shape)

    sides = sds((JH, 2, il, C, 128), BF16)
    single = sds((lane_rows, C, 128), BF16)
    slab1 = whole(sds((devices, lane_rows, 128), BF16))
    slab2 = whole(sds((devices, 2 * lane_rows, 128), BF16))
    blocks = whole(sds((residues, col_count * 256), BF16))
    block = pltpu.VMEM((residues, col_count * 256), BF16)
    flips = pltpu.VMEM((col_count * 256, residues), BF16)
    block32 = pltpu.VMEM((residues, col_count * 256), F32)
    chan_flops = 2 * col_count * col_count * residues * 256 * 256
    sums = f_whole(8, C)
    sides_out = (
        sds((C, 2 * lane_rows, 128), BF16),
        (C, 2 * il, 128),
        lambda s: (0, s, 0),
    )
    part = pltpu.VMEM((C, width), BF16)
    square = pltpu.VMEM((C, C), F32)
    wide = pltpu.VMEM((C, 2 * il, 128), F32)
    line = pltpu.VMEM((1, width), F32)

    def part32(rows=C):
        return pltpu.VMEM((rows, width), F32)


    def b_chan(rows=C):
        return chan(sds((rows, slots), BF16))

    g_in = [column(1 + t) for t in range(2)]
    g_out = [column(3 + t) for t in range(2)]
    keep_in = layer_of(keep)
    bd = (right_wide, (1,) + right_wide.shape[1:], lambda s: (s, 0, 0))
    pos_flops = 2 * slots * C * C

    def factors(values, t, more=()):
        return call(
            factor_kernel,
            steps,
            [chan(values), keep_in, g_in[t], layer(w_tin, t)],
            [b_chan(), chan(sds((1, slots), F32)), b_chan(), b_chan(4 * CH), *more],
            5 * pos_flops,
            [part32(5 * CH)],
        )

    pair_one, sides0, mids = call(
        open_kernel,
        steps,
        [
            tile(split_tile(pair_feats)),
            whole(eye),
            whole(middle),
            bd,
            column(0),
            keep_in,
            g_in[0],
            layer(w_tin, 0),
        ],
        [f_chan(), sides_out, whole(sds((2 * items * OP, width), BF16))],
        6 * pos_flops,
        [
            pltpu.VMEM((width, 2 * items * OP), BF16),
            pltpu.VMEM((width, 128), F32),
            part,
            part32(4 * CH),
            part,
            wide,
        ],
    )
    slabs0 = swap_all(sides0, BOTH)
    unit0, inv0, _, factor0, gate0 = factors(pair_one, 0, [b_chan()])
    x_chan, bias = call(
        bias_kernel,
        steps,
        [
            tile(split_tile(pair_feats)),
            whole(eye),
            whole(w_bias),
            (w_dist.reshape(-1, 1), (H, 1), lambda s: (0, 0)),
            chan(dist_slots.reshape(1, slots)),
        ],
        [b_chan(), b_chan(H)],
        pos_flops // 10,
    )

    qkv = half(dot(node_rows, w_local, 1, 0))
    slabs0, own = tie(slabs0, qkv[:, head_width:].reshape(-1, 128))
    everyone = spread(own, "row").reshape(residues, items, 2 * head_width)
    (p0,) = call(
        out_product_kernel,
        1,
        [whole(slabs0)],
        [slab1],
        chan_flops,
        [block, block],
        SMALL_VMEM,
    )
    p0, everyone = tie(p0, everyone)
    prod0 = to_pairs(p0)
    cot, d_active = call(
        cotangent_kernel,
        steps,
        [tile(split_tile(pair_cotan)), whole(eye), whole(w_down)],
        [b_chan(), b_chan(FT)],
        5 * pos_flops,
    )

    prod0, bias = tie(prod0, bias)
    bias_rows = swap_all(bias.reshape(H, lane_rows, 128), "col")
    pair_two, sides1, gate1 = call(
        middle_kernel,
        steps,
        [
            chan(pair_one),
            chan(gate0),
            rows_of(prod0),
            keep_in,
            g_out[0],
            layer(w_tout, 0),
            g_in[1],
            layer(w_tin, 1),
        ],
        [f_chan(), sides_out, b_chan()],
        6 * pos_flops,
        [part, part32(), part32(5 * CH), wide],
    )
    sides1, bias_rows = tie(sides1, bias_rows)
    slabs1 = swap_all(sides1, BOTH)
    unit1, inv1, normed1, factor1 = factors(pair_two, 1)

    def rear(product, gate, t):
        return call(
            rear_kernel,
            steps,
            [rows_of(product), chan(gate), g_out[t], layer(w_tout, t)],
            [b_chan(), chan(sds((1, slots), F32)), b_chan()],
            pos_flops,
            [part, part32()],
        )

    prod_unit0, prod_inv0, slope0 = rear(prod0, gate0, 0)

    bias_rows = from_slots(bias_rows.reshape(col_count, heads_here, lane_rows, 128))
    bias_rows = jnp.transpose(bias_rows, (2, 1, 3, 0, 4)).reshape(
        items, heads_here, tile_rows, residues
    )
    key_all = everyone[..., :head_width].reshape(residues, items, heads_here, HD)
    value_all = everyone[..., head_width:].reshape(residues, items, heads_here, HD)
    query = qkv[:, :head_width].reshape(tile_rows, items, heads_here, HD)
    all_ids = jnp.arange(residues, dtype=jnp.int32)
    key_keep = (all_ids[None, :] < lengths[:, None]).astype(F32)

    def product(spec, *operands):
        return jnp.einsum(spec, *operands, preferred_element_type=F32)

    scores = (
        product("ighd,jghd->ghij", query, key_all) * score_scale
        + bias_rows.astype(F32)
        + ((key_keep - 1.0) * 1000000000.0)[:, None, None, :]
    )
    probs = jax.nn.softmax(scores, axis=-1)
    probs_half = half(probs)
    attended = half(
        product("ghij,jghd->ighd", probs_half, value_all).reshape(
            tile_rows * items, head_width
        )
    )
    node_part = half(dot(attended, wo_local, 1, 0))
    d_attended = half(dot(cot_rows, wo_local, 1, 1)).reshape(tile_rows, items, heads_here, HD)
    d_probs = product("ighd,jghd->ghij", d_attended, value_all)
    d_value = product("ghij,ighd->jghd", probs_half, d_attended)
    d_scores = half(probs * (d_probs - jnp.sum(probs * d_probs, axis=-1, keepdims=True)))
    d_query = product("ghij,jghd->ighd", d_scores, key_all) * score_scale
    d_key = product("ghij,ighd->jghd", d_scores, query) * score_scale
    d_bias = jnp.transpose(
        d_scores.reshape(items, heads_here, tile_rows, col_count, tile_cols), (3, 1, 0, 2, 4)
    )
    d_bias = to_slots(d_bias).reshape(col_count, heads_here * lane_rows, 128)
    sent = jnp.concatenate([d_bias, node_part.reshape(col_count, -1, 128)], axis=1)
    d_kv = jnp.concatenate(
        [d_key.reshape(-1, head_width), d_value.reshape(-1, head_width)], axis=1
    )
    slabs1, sent = tie(slabs1, sent)
    got = swap_all(sent, "col")
    bias_lanes = heads_here * lane_rows
    d_bias = got[:, :bias_lanes].reshape(H, lane_rows, 128)
    node_sum = jnp.sum(got[:, bias_lanes:].astype(F32), axis=0)
    (p1,) = call(
        in_product_kernel,
        1,
        [whole(slabs1), whole(eye_lanes)],
        [slab1],
        chan_flops,
        [block, block, flips],
        SMALL_VMEM,
    )
    p1, d_bias, node_sum = tie(p1, d_bias, node_sum)
    prod1 = to_pairs(p1)
    d_bias32 = d_bias.astype(F32)
    grad_dist = from_slots(jnp.sum(d_bias32 * w_dist[:, None, None], axis=0))
    dw_dist = jnp.sum(d_bias32 * dist_slots[None], axis=(1, 2))
    d_bias_chan = d_bias.reshape(H, slots)

    prod1, d_kv, cot, d_active = tie(prod1, half(d_kv), cot, d_active)
    d_kv = swap_all(d_kv.reshape(row_count, -1, 128), "row")
    grad2, dprod1, dg_trans, dg_out1 = call(
        turn_kernel,
        steps,
        [
            chan(pair_two),
            chan(gate1),
            rows_of(prod1),
            chan(cot),
            chan(d_active),
            g_out[1],
            layer(w_tout, 1),
            column(5),
            whole(w_up),
        ],
        [f_chan(), rows_of(single), sums, sums],
        10 * pos_flops,
        [
            part,
            part,
            part,
            line,
            part,
            line,
            part32(),
            part32(FT),
            pltpu.VMEM((FT, width), BF16),
            square,
            square,
        ],
    )
    dprod1, d_kv = tie(dprod1, d_kv)
    dp1 = to_channels(dprod1)
    _, _, slope1 = rear(prod1, gate1, 1)
    pair_out, dw_down, dw_up, dw_out1 = call(
        finish_kernel,
        steps,
        [
            chan(pair_two),
            chan(gate1),
            rows_of(prod1),
            chan(cot),
            chan(d_active),
            chan(grad2),
            g_out[1],
            layer(w_tout, 1),
            column(5),
            whole(w_up),
            whole(w_down),
        ],
        [
            tile(sds((items, 2, il, tile_cols, C), F32)),
            f_whole(FT, C),
            f_whole(FT, C),
            f_whole(C, CH),
        ],
        13 * pos_flops,
        [
            part,
            part,
            part32(),
            part32(),
            part32(FT),
            pltpu.VMEM((FT, width), BF16),
            pltpu.VMEM((FT, width), BF16),
            pltpu.VMEM((FT, C), F32),
        ],
    )
    d_kv = jnp.sum(d_kv.astype(F32), axis=0).reshape(tile_rows * items, 2 * head_width)
    d_qkv = half(jnp.concatenate([d_query.reshape(-1, head_width), d_kv], axis=1))
    d_att = half(dot(d_qkv, w_local, 1, 1)).reshape(col_count, -1, 128)

    dp1, d_att, dw_down, dw_up, dw_out1 = tie(
        dp1, d_att, dw_down, dw_up, dw_out1
    )
    d_att = swap_all(d_att, "col")
    l1, r1 = call(unpack_kernel, 1, [whole(slabs1)], [blocks, blocks], pos_flops)
    (d1,) = call(
        in_back_kernel,
        1,
        [whole(l1), whole(r1), whole(dp1)],
        [slab2],
        2 * chan_flops,
        [block],
    )
    d1, d_att = tie(d1, d_att)
    dsides1 = to_pairs(d1)
    d_att = jnp.sum(d_att.astype(F32), axis=0).reshape(share, D)
    head_grads = jnp.concatenate(
        [dot(d_qkv, node_rows, 0, 0), dot(attended, cot_rows, 0, 0)], axis=0
    )

    mid_arrays = [
        dw_down,
        dw_up,
        dw_out1,
        jnp.pad(dw_dist[None], ((0, 7), (0, 128 - H))),
        dg_trans,
        dg_out1,
    ]
    dsides1, mid_sent, factor1, unit1, slope1, prod_unit0 = tie(
        dsides1, half(padded(mid_arrays)), factor1, unit1, slope1, prod_unit0
    )
    mid_part = swap_all(mid_sent, BOTH)
    grad1, dprod0, dg_in1, dg_out0 = call(
        back_kernel,
        steps,
        [
            double(dsides1),
            chan(factor1),
            chan(slope1),
            chan(unit1),
            chan(inv1),
            chan(grad2),
            g_in[1],
            layer(w_tin, 1),
            chan(gate0),
            chan(prod_unit0),
            chan(prod_inv0),
            g_out[0],
            layer(w_tout, 0),
        ],
        [f_chan(), rows_of(single), sums, sums],
        8 * pos_flops,
        [pltpu.VMEM((5 * CH, width), BF16), part, part, square, square],
    )
    dprod0, mid_part = tie(dprod0, mid_part)
    dp0 = to_channels(dprod0)
    mid_part = jnp.sum(mid_part.astype(F32), axis=0)

    dp0, head_grads = tie(dp0, head_grads)
    head_grads = swap_all(head_grads.reshape(row_count, -1, 128), "row")
    l0, r0 = call(unpack_kernel, 1, [whole(slabs0)], [blocks, blocks], pos_flops)
    (d0,) = call(
        out_back_kernel,
        1,
        [whole(l0), whole(r0), whole(dp0), whole(eye_lanes)],
        [slab2],
        2 * chan_flops,
        [block, block32, flips],
    )
    d0, head_grads = tie(d0, head_grads)
    dsides0 = to_pairs(d0)
    head_grads = jnp.sum(head_grads, axis=0)
    dw_in1, dw_out0, dw_bias_t = call(
        weights_kernel,
        steps,
        [
            double(dsides1),
            chan(factor1),
            chan(slope1),
            chan(grad2),
            chan(normed1),
            chan(grad1),
            chan(gate0),
            chan(prod_unit0),
            g_out[0],
            chan(d_bias_chan),
            chan(x_chan),
        ],
        [f_whole(5 * CH, C), f_whole(C, CH), f_whole(H, C)],
        6 * pos_flops,
        [pltpu.VMEM((5 * CH, width), BF16), pltpu.VMEM((5 * CH, C), F32)],
    )
    mid_part = half(jnp.concatenate([mid_part, head_grads], axis=0))

    dsides0, mid_part, dw_in1, dw_out0, dw_bias_t = tie(
        dsides0, mid_part, dw_in1, dw_out0, dw_bias_t
    )
    mid_all = spread(mid_part, BOTH)
    grad_pair, d_middle, dw_in0, dg_in0, d_right_wide, db_outer = call(
        close_kernel,
        steps,
        [
            double(dsides0),
            chan(factor0),
            chan(slope0),
            chan(unit0),
            chan(inv0),
            chan(grad1),
            keep_in,
            g_in[0],
            layer(w_tin, 0),
            whole(mids),
            bd,
            chan(d_bias_chan),
            whole(w_bias),
        ],
        [
            tile(sds((items, 2, il, tile_cols, C), F32)),
            whole(sds(middle.shape, F32)),
            f_whole(5 * CH, C),
            sums,
            (sds((JH, OP, 128), F32), (1, OP, 128), lambda s: (s, 0, 0)),
            sums,
        ],
        14 * pos_flops,
        [
            pltpu.VMEM((5 * CH, width), BF16),
            part,
            pltpu.VMEM((width, 128), BF16),
            square,
            pltpu.VMEM((width, 2 * items * OP), F32),
            part32(),
            pltpu.VMEM((5 * CH, C), F32),
        ],
    )
    grad_pair, mid_all, d_middle = tie(grad_pair, mid_all, d_middle)
    mid_rows = mid_all.shape[1] - head_grads.shape[0]
    pick_left = np.zeros((2, col_count, 8, il, 2, items), ml_dtypes.bfloat16)
    pick_right = np.zeros((parts, 2, JH, col_count, 8, 2, items, jl), ml_dtypes.bfloat16)
    for c in range(col_count):
        for n in range(share):
            i, b = divmod(c * share + n, items)
            pick_left[n % 2, c, n // 2, i % il, i // il, b] = 1
            for h in range(parts):
                j = h * tile_rows + i
                pick_right[h, n % 2, j // jl, c, n // 2, :, b, j % jl] = 1
    pick_left = pick_left.reshape(2, 8 * col_count, tile_rows * items)
    pick_right = pick_right.reshape(parts, 2, JH, 8 * col_count, 128)
    places = jnp.zeros((2, 128, OP * C), BF16)
    places = places.at[0, :OP].set(w_outer).at[1, HALF : HALF + OP].set(w_outer)
    own_row = (jnp.arange(row_count) == row_index).astype(F32)
    own_col = (jnp.arange(row_count) // parts == col_index).astype(F32)
    masks = jnp.broadcast_to(
        jnp.concatenate([own_row, own_col])[:, None], (2 * row_count, 128)
    )
    col_units = jnp.transpose(half(col_unit).reshape(JH, jl, items, D), (0, 2, 1, 3))
    col_units = jnp.tile(col_units.reshape(JH, items * jl, D), (1, 2, 1))
    late_arrays = [dw_in0, dg_in0, db_outer, dw_in1, dw_out0, dg_in1, dg_out0, dw_bias_t]
    late_rows = [a.shape[0] for a in late_arrays] + [OP * OP, 4 * OP]
    (sent,) = call(
        functools.partial(tail_kernel, len(late_arrays)),
        1,
        [whole(a) for a in late_arrays]
        + [
            whole(d_middle),
            whole(left_node),
            whole(w_outer),
            whole(il_first(half(node_unit))),
            whole(d_right_wide),
            whole(col_units),
            whole(places),
            whole(pick_left),
            whole(pick_right),
            whole(masks),
        ],
        [whole(sds((devices, 32, 128), BF16))],
        1000,
        [pltpu.VMEM((OP * OP, 128), F32), pltpu.VMEM((4 * OP, 128), F32)],
    )
    got = scatter_sum(sent)
    late_part = got[:24]
    d_pair_rows = half(got[24 : 24 + share // 2]).reshape(share, 2 * OP)
    node_share = lax.dynamic_slice_in_dim(node_full, col_index * share, share, 0)
    cot_share = lax.dynamic_slice_in_dim(cot_rows, col_index * share, share, 0)
    unit, inv = node_norm(node_share)
    d_normed = half(dot(d_pair_rows, w_ab, 1, 1)).astype(F32)
    scaled = d_normed * g_node
    d_norm = inv * (
        scaled
        - jnp.mean(scaled, axis=-1, keepdims=True)
        - unit * jnp.mean(scaled * unit, axis=-1, keepdims=True)
    )
    grad_share = cot_share.astype(F32) + d_att + d_norm
    out_share = node_share + node_sum.reshape(share, D)
    late_all = spread(half(late_part), BOTH)
    mine = jnp.stack([out_share, grad_share]).reshape(-1, 128)
    late_all, mine = tie(late_all, mine)
    nodes = spread(mine, "col").reshape(col_count, 2, share, D)

    def node_result(which):
        array = nodes[:, which].reshape(tile_rows, items, D)
        return jnp.transpose(array, (1, 0, 2))

    head_grads = mid_all[:, mid_rows:].astype(F32).reshape(row_count, col_count, -1)
    head_grads = jnp.transpose(head_grads, (1, 0, 2)).reshape(col_count, 4, head_width, D)
    g_qkv = jnp.transpose(head_grads[:, :3], (3, 1, 0, 2)).reshape(D, 3 * D)
    g_node_out = head_grads[:, 3].reshape(D, D)

    def widen(blocks):
        count = blocks.shape[0] // 128
        return jnp.concatenate([blocks[128 * n : 128 * n + 128] for n in range(count)], axis=1)

    def cut(flat, counts):
        start, pieces = 0, []
        for rows in counts:
            pieces.append(flat[start : start + rows])
            start += rows
        return pieces

    (
        s_down,
        s_up,
        s_out1,
        s_dist,
        s_trans,
        s_gout1,
    ) = cut(mid_all[:, :mid_rows].reshape(-1, 128).astype(F32), [a.shape[0] for a in mid_arrays])
    late_all = late_all.reshape(-1, 128).astype(F32)
    s_in0, s_gin0, s_bout, s_in1, s_out0, s_gin1, s_gout0, s_bias_t, s_outer, s_ab = cut(
        late_all, late_rows
    )
    s_outer = jnp.transpose(s_outer.reshape(OP, OP, C), (1, 0, 2))
    s_ab = jnp.transpose(s_ab.reshape(2, 2 * OP, 128), (0, 2, 1))
    s_ab = s_ab.reshape(D, 2 * OP)
    s_gnode = jnp.sum(s_ab * w_ab.astype(F32), axis=1)
    s_ab = s_ab * g_node[:, None]
    return (
        node_result(0),
        pair_out.reshape(pair_feats.shape),
        node_result(1),
        grad_pair.reshape(pair_feats.shape),
        grad_dist,
        g_qkv,
        jnp.transpose(s_bias_t),
        s_dist[0, :H],
        g_node_out,
        s_gnode,
        s_ab,
        s_outer.reshape(OP, OP * C),
        s_bout[0],
        jnp.stack([s_gin0[0], s_gin1[0]]),
        jnp.stack([widen(s_in0), widen(s_in1)]),
        jnp.stack([s_gout0[0], s_gout1[0]]),
        jnp.stack([s_out0, s_out1]),
        s_trans[0],
        widen(s_up),
        s_down,
    )


def solution(mesh):
    pair = P(None, "row", "col", None)
    node = P(None, "row", None)
    dist = P(None, "row", "col")
    return jax.shard_map(
        per_device,
        mesh=mesh,
        in_specs=(node, pair, dist, P(), node, pair) + (P(),) * 15,
        out_specs=(node, pair, node, pair, dist) + (P(),) * 15,
        check_vma=False,
    )
```

```python
import functools

import jax
import jax.numpy as jnp
import ml_dtypes
import numpy as np
from jax import lax
from jax.experimental import pallas as pl
from jax.experimental.pallas import tpu as pltpu
from jax.sharding import PartitionSpec as P

D = 256
C = 128
H = 8
HD = 32
CH = 128
OP = 32
FT = 512
ITEMS = 4
EPS = 1e-05
BOTH = ("row", "col")
F32 = jnp.float32
BF16 = jnp.bfloat16
HALF = 64
JH = 3
VMEM = 60 * 1024 * 1024
SMALL_VMEM = 28 * 1024 * 1024


def half(values):
    return values.astype(BF16)


def dot(lhs, rhs, lhs_dim, rhs_dim):
    return lax.dot_general(
        lhs, rhs, (((lhs_dim,), (rhs_dim,)), ((), ())), preferred_element_type=F32
    )


def sigmoid(values):
    return 0.5 * jnp.tanh(0.5 * values) + 0.5


def norm_parts(values):
    scale = 1.0 / values.shape[0]
    centered = values - jnp.sum(values, axis=0, keepdims=True) * scale
    spread = jnp.sum(centered * centered, axis=0, keepdims=True) * scale
    inv = lax.rsqrt(spread + EPS)
    return centered * inv, inv


def norm_back(unit, inv, gain, grad):
    scale = 1.0 / unit.shape[0]
    scaled = grad * gain
    first = jnp.sum(scaled, axis=0, keepdims=True) * scale
    second = jnp.sum(scaled * unit, axis=0, keepdims=True) * scale
    return inv * (scaled - first - unit * second)


def lane_rows_of(width):
    return [(m, slice(128 * m, 128 * m + 128)) for m in range(width // 128)]


def tile_rows_of(ref):
    items, parts, rows = ref.shape[:3]
    return jnp.concatenate(
        [ref[b, h, m] for m in range(rows) for h in range(parts) for b in range(items)],
        axis=0,
    )


def put_tile(ref, m, values):
    items, parts, _, cols = ref.shape[:4]
    flipped = jnp.transpose(values)
    start = 0
    for h in range(parts):
        for b in range(items):
            ref[b, h, m] = flipped[start : start + cols]
            start += cols


def low_lanes(rows):
    return lax.broadcasted_iota(jnp.int32, (rows, 128), 1) < HALF


def swap(values):
    return pltpu.roll(values, HALF, 1)


def get_double(ref, m):
    low = low_lanes(ref.shape[3])
    one, two = ref[0, 0, m].astype(F32), ref[0, 1, m].astype(F32)
    return jnp.where(low, one, swap(two)), jnp.where(low, swap(one), two)


def add_to(ref, values):
    @pl.when(pl.program_id(0) == 0)
    def _():
        ref[...] = values

    @pl.when(pl.program_id(0) != 0)
    def _():
        ref[...] += values


def add_diagonal(ref, total_ref, grad_ref, unit_ref):
    add_to(total_ref, dot(grad_ref[...], unit_ref[...], 1, 1))

    @pl.when(pl.program_id(0) == pl.num_programs(0) - 1)
    def _():
        rows = lax.broadcasted_iota(jnp.int32, total_ref.shape, 0)
        cols = lax.broadcasted_iota(jnp.int32, total_ref.shape, 1)
        picked = jnp.where(rows == cols, total_ref[...], 0.0)
        ref[...] = jnp.broadcast_to(jnp.sum(picked, axis=0, keepdims=True), ref.shape)


def bias_kernel(pair_ref, eye_ref, wb_ref, wd_ref, dist_ref, x_ref, bias_ref):
    x_chan = half(dot(eye_ref[...], tile_rows_of(pair_ref), 1, 1))
    x_ref[...] = x_chan
    bias_ref[...] = half(dot(wb_ref[...], x_chan, 0, 0) + wd_ref[...] * dist_ref[...])


def cotangent_kernel(cot_ref, eye_ref, wdown_plain_ref, out_ref, dact_ref):
    cot = half(dot(eye_ref[...], tile_rows_of(cot_ref), 1, 1))
    out_ref[...] = cot
    dact_ref[...] = half(dot(wdown_plain_ref[...], cot, 1, 0))


def put_sides(proj_ref, keep_ref, sides_ref, wide_ref):
    count = keep_ref.shape[1]
    for m, here in lane_rows_of(proj_ref.shape[1]):
        keep = keep_ref[0, m : m + 1, :]
        left = sigmoid(proj_ref[CH : 2 * CH, here]) * proj_ref[:CH, here] * keep
        right = (
            sigmoid(proj_ref[3 * CH : 4 * CH, here]) * proj_ref[2 * CH : 3 * CH, here] * keep
        )
        low = low_lanes(left.shape[0])
        wide_ref[:, m, :] = jnp.where(low, left, swap(right))
        wide_ref[:, m + count, :] = jnp.where(low, swap(left), right)
    sides_ref[...] = half(wide_ref[...])


def diagonal_blocks(right):
    which = lax.broadcasted_iota(jnp.int32, (8, 128), 0)
    lane = lax.broadcasted_iota(jnp.int32, (8, 128), 1) // 16
    same = (which == lane).astype(F32)
    return half(jnp.concatenate([same * right[q : q + 1] for q in range(OP)], axis=0))


def node_kernel(node_ref, col_ref, gain_ref, wab_ref, wout_ref, perm_ref, mid_ref, right_ref):
    def normed(ref):
        values = ref[...].astype(F32)
        scale = 1.0 / values.shape[1]
        centered = values - jnp.sum(values, axis=1, keepdims=True) * scale
        spread = jnp.sum(centered * centered, axis=1, keepdims=True) * scale
        return half(centered * lax.rsqrt(spread + EPS) * gain_ref[...])

    left = half(dot(wab_ref[...], normed(node_ref), 1, 1))
    mid_ref[...] = dot(left[:OP], wout_ref[...], 0, 0)
    right = half(dot(wab_ref[...], normed(col_ref), 1, 1))
    right = dot(right[OP:], perm_ref[...], 1, 0)
    for j in range(JH):
        right_ref[j] = right[:, 128 * j : 128 * j + 128]


def open_kernel(
    pair_ref,
    eye_ref,
    mid_ref,
    bd_ref,
    bout_ref,
    keep_ref,
    gain_ref,
    w_ref,
    one_ref,
    sides_ref,
    mids_ref,
    mid_t_ref,
    outer_ref,
    normed_ref,
    proj_ref,
    x_ref,
    wide_ref,
):
    @pl.when(pl.program_id(0) == 0)
    def _():
        for m in range(mids_ref.shape[1] // 128):
            rows = [
                mid_ref[8 * m : 8 * m + 8, 128 * q : 128 * q + 128] for q in range(OP)
            ]
            stack = jnp.concatenate(rows, axis=0)
            mids_ref[:, 128 * m : 128 * m + 128] = half(stack)
            mid_t_ref[128 * m : 128 * m + 128, :] = half(jnp.transpose(stack))

    x_ref[...] = half(dot(eye_ref[...], tile_rows_of(pair_ref), 1, 1))
    outer_ref[...] = dot(mid_t_ref[...], diagonal_blocks(bd_ref[0]), 1, 0)
    for m, here in lane_rows_of(x_ref.shape[1]):
        outer = outer_ref[128 * m : 128 * m + 128, :]
        keep = keep_ref[0, m : m + 1, :]
        pair_one = x_ref[:, here].astype(F32) + keep * (outer + bout_ref[0])
        one_ref[:, here] = pair_one
        unit, _ = norm_parts(pair_one)
        normed_ref[:, here] = half(unit * gain_ref[0])
    proj_ref[...] = dot(w_ref[0, :, : 4 * CH], normed_ref[...], 0, 0)
    put_sides(proj_ref, keep_ref, sides_ref, wide_ref)


def factor_kernel(
    in_ref, keep_ref, gain_ref, w_ref, unit_ref, inv_ref, normed_ref, factor_ref, *rest
):
    proj_ref = rest[-1]
    for _, here in lane_rows_of(in_ref.shape[1]):
        unit, inv = norm_parts(in_ref[:, here])
        unit_ref[:, here] = half(unit)
        inv_ref[:, here] = inv
        normed_ref[:, here] = half(unit * gain_ref[0])
    proj_ref[...] = dot(w_ref[0], normed_ref[...], 0, 0)
    for m, here in lane_rows_of(in_ref.shape[1]):
        keep = keep_ref[0, m : m + 1, :]
        for side in range(2):
            start = 2 * CH * side
            sig = sigmoid(proj_ref[start + CH : start + 2 * CH, here])
            first = keep * sig
            factor_ref[start : start + CH, here] = half(first)
            factor_ref[start + CH : start + 2 * CH, here] = half(
                first * proj_ref[start : start + CH, here] * (1.0 - sig)
            )
        if len(rest) > 1:
            rest[0][:, here] = half(sigmoid(proj_ref[4 * CH :, here]))


def rear_kernel(
    prod_ref, gate_ref, gout_ref, wout_ref, unit_ref, inv_ref, slope_ref, y_ref, update_ref
):
    for m, here in lane_rows_of(gate_ref.shape[1]):
        unit, inv = norm_parts(prod_ref[m].astype(F32))
        unit_ref[:, here] = half(unit)
        inv_ref[:, here] = inv
        y_ref[:, here] = half(unit * gout_ref[0])
    update_ref[...] = dot(wout_ref[0], y_ref[...], 0, 0)
    for _, here in lane_rows_of(gate_ref.shape[1]):
        gate = gate_ref[:, here].astype(F32)
        slope_ref[:, here] = half(update_ref[:, here] * gate * (1.0 - gate))


def middle_kernel(
    one_ref,
    gate_ref,
    prod_ref,
    keep_ref,
    gout_ref,
    wout_ref,
    gin_ref,
    w_ref,
    two_ref,
    sides_ref,
    gate_out_ref,
    y_ref,
    update_ref,
    proj_ref,
    wide_ref,
):
    for m, here in lane_rows_of(one_ref.shape[1]):
        unit, _ = norm_parts(prod_ref[m].astype(F32))
        y_ref[:, here] = half(unit * gout_ref[0])
    update_ref[...] = dot(wout_ref[0], y_ref[...], 0, 0)
    for _, here in lane_rows_of(one_ref.shape[1]):
        pair_two = one_ref[:, here] + gate_ref[:, here].astype(F32) * update_ref[:, here]
        two_ref[:, here] = pair_two
        unit, _ = norm_parts(pair_two)
        y_ref[:, here] = half(unit * gin_ref[0])
    proj_ref[...] = dot(w_ref[0], y_ref[...], 0, 0)
    put_sides(proj_ref, keep_ref, sides_ref, wide_ref)
    for _, here in lane_rows_of(one_ref.shape[1]):
        gate_out_ref[:, here] = half(sigmoid(proj_ref[4 * CH :, here]))


def transition(two_ref, gate_ref, prod_ref, gout_ref, wout_ref, gtr_ref, wup_ref, refs):
    y_ref, prod_unit_ref, prod_inv_ref, update_ref = refs[:4]
    three_ref, xt_ref, tr_unit_ref, tr_inv_ref, hidden_ref = refs[4:]
    rows = lane_rows_of(two_ref.shape[1])
    for m, here in rows:
        unit, inv = norm_parts(prod_ref[m].astype(F32))
        if prod_unit_ref is not None:
            prod_inv_ref[:, here] = inv
            prod_unit_ref[:, here] = half(unit)
        y_ref[:, here] = half(unit * gout_ref[0])
    update_ref[...] = dot(wout_ref[0], y_ref[...], 0, 0)
    for _, here in rows:
        pair_three = (
            two_ref[:, here] + gate_ref[:, here].astype(F32) * update_ref[:, here]
        )
        if three_ref is not None:
            three_ref[:, here] = pair_three
        unit, inv = norm_parts(pair_three)
        if tr_unit_ref is not None:
            tr_inv_ref[:, here] = inv
            tr_unit_ref[:, here] = half(unit)
        xt_ref[:, here] = half(unit * gtr_ref[0])
    hidden_ref[...] = dot(wup_ref[...], xt_ref[...], 0, 0)


def put_hidden_back(hidden_ref, dact_ref, dhid_ref, active_ref=None):
    for _, here in lane_rows_of(hidden_ref.shape[1]):
        for start in range(0, FT, CH):
            part = slice(start, start + CH)
            hidden = hidden_ref[part, here]
            sig = sigmoid(hidden)
            act32 = hidden * sig
            if active_ref is not None:
                active_ref[part, here] = half(act32)
            dhid_ref[part, here] = half(
                dact_ref[part, here].astype(F32) * (sig + act32 * (1.0 - sig))
            )


def turn_kernel(
    two_ref,
    gate_ref,
    prod_ref,
    cot_ref,
    dact_ref,
    gout_ref,
    wout_ref,
    gtr_ref,
    wup_ref,
    grad_ref,
    dprod_ref,
    dgtr_ref,
    dgout_ref,
    small_ref,
    xt_ref,
    tr_unit_ref,
    tr_inv_ref,
    prod_unit_ref,
    prod_inv_ref,
    update_ref,
    hidden_ref,
    dhid_ref,
    tr_total_ref,
    out_total_ref,
):
    rows = lane_rows_of(two_ref.shape[1])
    refs = (small_ref, prod_unit_ref, prod_inv_ref, update_ref)
    refs += (None, xt_ref, tr_unit_ref, tr_inv_ref, hidden_ref)
    transition(two_ref, gate_ref, prod_ref, gout_ref, wout_ref, gtr_ref, wup_ref, refs)
    put_hidden_back(hidden_ref, dact_ref, dhid_ref)
    small_ref[...] = half(dot(wup_ref[...], dhid_ref[...], 1, 0))
    for _, here in rows:
        grad = cot_ref[:, here].astype(F32) + norm_back(
            tr_unit_ref[:, here].astype(F32),
            tr_inv_ref[:, here],
            gtr_ref[0],
            small_ref[:, here].astype(F32),
        )
        grad_ref[:, here] = grad
        xt_ref[:, here] = half(grad * gate_ref[:, here].astype(F32))
    add_diagonal(dgtr_ref, tr_total_ref, small_ref, tr_unit_ref)
    small_ref[...] = half(dot(wout_ref[0], xt_ref[...], 1, 0))
    put_product_back(dprod_ref, prod_unit_ref, prod_inv_ref, gout_ref, small_ref)
    add_diagonal(dgout_ref, out_total_ref, small_ref, prod_unit_ref)


def put_product_back(dprod_ref, unit_ref, inv_ref, gain_ref, dy_ref):
    for m, here in lane_rows_of(unit_ref.shape[1]):
        dprod_ref[m] = half(
            norm_back(
                unit_ref[:, here].astype(F32),
                inv_ref[:, here],
                gain_ref[0],
                dy_ref[:, here].astype(F32),
            )
        )


def finish_kernel(
    two_ref,
    gate_ref,
    prod_ref,
    cot_ref,
    dact_ref,
    grad_ref,
    gout_ref,
    wout_ref,
    gtr_ref,
    wup_ref,
    wdown_ref,
    out_ref,
    dwdown_ref,
    dwup_ref,
    dwout_ref,
    y_ref,
    xt_ref,
    update_ref,
    three_ref,
    hidden_ref,
    dhid_ref,
    active_ref,
    dwup_t_ref,
):
    refs = (y_ref, None, None, update_ref, three_ref, xt_ref, None, None, hidden_ref)
    transition(two_ref, gate_ref, prod_ref, gout_ref, wout_ref, gtr_ref, wup_ref, refs)
    put_hidden_back(hidden_ref, dact_ref, dhid_ref, active_ref)
    update_ref[...] = dot(wdown_ref[...], active_ref[...], 0, 0)
    for m, here in lane_rows_of(two_ref.shape[1]):
        put_tile(out_ref, m, three_ref[:, here] + update_ref[:, here])
    add_to(dwdown_ref, dot(active_ref[...], cot_ref[...], 1, 1))
    add_to(dwup_t_ref, dot(dhid_ref[...], xt_ref[...], 1, 1))
    d_update = half(grad_ref[...] * gate_ref[...].astype(F32))
    add_to(dwout_ref, dot(y_ref[...], d_update, 1, 1))

    @pl.when(pl.program_id(0) == pl.num_programs(0) - 1)
    def _():
        put_flipped(dwup_ref, dwup_t_ref)


def put_front_grads(sides_ref, factor_ref, slope_ref, grad_ref, dproj_ref):
    for m, here in lane_rows_of(grad_ref.shape[1]):
        sides = get_double(sides_ref, m)
        for at in range(4):
            part = slice(CH * at, CH * at + CH)
            dproj_ref[part, here] = half(sides[at // 2] * factor_ref[part, here].astype(F32))
        dproj_ref[4 * CH :, here] = half(grad_ref[:, here] * slope_ref[:, here].astype(F32))


def front_back(unit_ref, inv_ref, gain_ref, dn_ref, here):
    return norm_back(
        unit_ref[:, here].astype(F32),
        inv_ref[:, here],
        gain_ref[0],
        dn_ref[:, here].astype(F32),
    )


def back_kernel(
    dsides_ref,
    factor_ref,
    slope_ref,
    unit_ref,
    inv_ref,
    grad_ref,
    gin_ref,
    w_ref,
    gate_ref,
    prod_unit_ref,
    prod_inv_ref,
    gout_ref,
    wout_ref,
    grad_out_ref,
    dprod_ref,
    dgin_ref,
    dgout_ref,
    dproj_ref,
    dupd_ref,
    small_ref,
    in_total_ref,
    out_total_ref,
):
    put_front_grads(dsides_ref, factor_ref, slope_ref, grad_ref, dproj_ref)
    small_ref[...] = half(dot(w_ref[0], dproj_ref[...], 1, 0))
    for _, here in lane_rows_of(grad_ref.shape[1]):
        grad = grad_ref[:, here] + front_back(unit_ref, inv_ref, gin_ref, small_ref, here)
        grad_out_ref[:, here] = grad
        dupd_ref[:, here] = half(grad * gate_ref[:, here].astype(F32))
    add_diagonal(dgin_ref, in_total_ref, small_ref, unit_ref)
    small_ref[...] = half(dot(wout_ref[0], dupd_ref[...], 1, 0))
    put_product_back(dprod_ref, prod_unit_ref, prod_inv_ref, gout_ref, small_ref)
    add_diagonal(dgout_ref, out_total_ref, small_ref, prod_unit_ref)


def put_flipped(out_ref, total_ref):
    for start in range(0, total_ref.shape[0], 128):
        out_ref[start : start + 128, :] = jnp.transpose(total_ref[start : start + 128, :])


def weights_kernel(
    dsides_ref,
    factor_ref,
    slope_ref,
    grad_ref,
    normed_ref,
    next_grad_ref,
    gate_ref,
    prod_unit_ref,
    gout_ref,
    dbias_ref,
    x_ref,
    dwin_ref,
    dwout_ref,
    dwb_ref,
    dproj_ref,
    dwin_t_ref,
):
    put_front_grads(dsides_ref, factor_ref, slope_ref, grad_ref, dproj_ref)
    add_to(dwin_t_ref, dot(dproj_ref[...], normed_ref[...], 1, 1))

    @pl.when(pl.program_id(0) == pl.num_programs(0) - 1)
    def _():
        put_flipped(dwin_ref, dwin_t_ref)

    d_update = half(next_grad_ref[...] * gate_ref[...].astype(F32))
    y_half = half(prod_unit_ref[...].astype(F32) * gout_ref[0])
    add_to(dwout_ref, dot(y_half, d_update, 1, 1))
    add_to(dwb_ref, dot(dbias_ref[...], x_ref[...], 1, 1))


def close_kernel(
    dsides_ref,
    factor_ref,
    slope_ref,
    unit_ref,
    inv_ref,
    grad_ref,
    keep_ref,
    gin_ref,
    w_ref,
    mids_ref,
    bd_ref,
    dbias_ref,
    wb_ref,
    out_ref,
    dmid_ref,
    dwin_ref,
    dgin_ref,
    dright_ref,
    dbout_ref,
    dproj_ref,
    small_ref,
    outer_ref,
    in_total_ref,
    dmid_t_ref,
    bias_ref,
    dwin_t_ref,
):
    put_front_grads(dsides_ref, factor_ref, slope_ref, grad_ref, dproj_ref)
    small_ref[...] = half(dot(w_ref[0], dproj_ref[...], 1, 0))
    bias_ref[...] = dot(wb_ref[...], dbias_ref[...], 1, 0)
    total = None
    for m, here in lane_rows_of(grad_ref.shape[1]):
        grad = grad_ref[:, here] + front_back(unit_ref, inv_ref, gin_ref, small_ref, here)
        put_tile(out_ref, m, grad + bias_ref[:, here])
        outer = grad * keep_ref[0, m : m + 1, :]
        outer_ref[128 * m : 128 * m + 128, :] = half(outer)
        total = outer if total is None else total + outer
    normed = half(unit_ref[...].astype(F32) * gin_ref[0])
    add_to(dmid_t_ref, dot(outer_ref[...], diagonal_blocks(bd_ref[0]), 1, 1))
    right = dot(mids_ref[...], outer_ref[...], 1, 0)
    which = lax.broadcasted_iota(jnp.int32, (8, 128), 0)
    lane = lax.broadcasted_iota(jnp.int32, (8, 128), 1) // 16
    for q in range(OP):
        picked = jnp.where(which == lane, right[8 * q : 8 * q + 8], 0.0)
        dright_ref[0, q : q + 1, :] = jnp.sum(picked, axis=0, keepdims=True)
    add_to(dwin_t_ref, dot(dproj_ref[...], normed, 1, 1))
    ones = jnp.ones((8, 128), F32)
    add_to(
        dbout_ref,
        lax.dot_general(
            ones,
            total,
            (((1,), (1,)), ((), ())),
            preferred_element_type=F32,
            precision=lax.Precision.HIGHEST,
        ),
    )
    add_diagonal(dgin_ref, in_total_ref, small_ref, unit_ref)

    @pl.when(pl.program_id(0) == pl.num_programs(0) - 1)
    def _():
        for m in range(dmid_t_ref.shape[0] // 128):
            stack = jnp.transpose(dmid_t_ref[128 * m : 128 * m + 128, :])
            for q in range(OP):
                dmid_ref[8 * m : 8 * m + 8, 128 * q : 128 * q + 128] = stack[
                    8 * q : 8 * q + 8
                ]
        put_flipped(dwin_ref, dwin_t_ref)


def tail_kernel(count, *refs):
    weight_refs, refs = refs[:count], refs[count:]
    dmid_ref, left_ref, wouter_ref, unit_ref, dright_ref, col_unit_ref = refs[:6]
    wouter_pad_ref, pick_left_ref, pick_right_ref, mask_ref = refs[6:10]
    out_ref, outer_ref, small_ref = refs[10:]
    d_mid = half(dmid_ref[...])
    outer = dot(left_ref[...], d_mid, 0, 0)
    for q in range(OP):
        outer_ref[OP * q : OP * q + OP, :] = outer[:, 128 * q : 128 * q + 128]
    d_left = dot(d_mid, wouter_ref[...], 1, 1)
    sums = [dot(half(d_left), unit_ref[...], 0, 0)]
    total = None
    for j in range(JH):
        units = jnp.concatenate([col_unit_ref[j]] * 2, axis=0)
        part = dot(half(dright_ref[j]), units, 1, 0)
        total = part if total is None else total + part
    sums = jnp.concatenate(sums + [total], axis=0)
    small_ref[: 2 * OP, :] = sums[:, :128]
    small_ref[2 * OP :, :] = sums[:, 128:]
    lefts, rights = None, [None, None]
    for s in range(2):
        part = half(dot(d_mid, wouter_pad_ref[s], 1, 1))
        part = dot(pick_left_ref[s], part, 1, 0)
        lefts = part if lefts is None else lefts + part
        for j in range(JH):
            above = jnp.zeros((HALF * s + OP, 128), F32)
            spread = [above, dright_ref[j]]
            if s == 0:
                spread.append(jnp.zeros((HALF, 128), F32))
            spread = jnp.concatenate(spread, axis=0)
            spread = half(jnp.transpose(spread))
            for h in range(2):
                part = dot(pick_right_ref[h, s, j], spread, 1, 0)
                rights[h] = part if rights[h] is None else rights[h] + part
    sources = list(weight_refs) + [outer_ref, small_ref]
    pieces = [(ref, at) for ref in sources for at in range(0, ref.shape[0], 8)]
    rows = mask_ref.shape[0] // 2
    cols = out_ref.shape[0] // rows
    for r in range(rows):
        nodes = mask_ref[r : r + 1] * lefts + mask_ref[rows + r : rows + r + 1] * rights[r % 2]
        for c in range(cols):
            at = 3 * (r * cols + c)
            parts = [ref[k : k + 8, :] for ref, k in pieces[at : at + 3]]
            parts += [jnp.zeros((8, 128), F32)] * (3 - len(parts))
            out_ref[r * cols + c] = half(
                jnp.concatenate(parts + [nodes[8 * c : 8 * c + 8]], axis=0)
            )


def last_kernel(counts, late_ref, wab_ref, gain_ref, out1_ref, gout1_ref, *refs):
    tin_ref, outer_ref, ab_ref, gnode_ref, bias_ref = refs[:5]
    gtin_ref, gtout_ref, bout_ref, tout_ref, all_ref = refs[5:]
    all_ref[...] = late_ref[...].astype(F32)
    starts = [sum(counts[:n]) for n in range(len(counts))]
    in0, gin0, bout, in1, out0, gin1, gout0, bias, outer, ab = starts
    for t, start in enumerate((in0, in1)):
        for n in range(5):
            rows = slice(start + 128 * n, start + 128 * n + 128)
            tin_ref[t, :, 128 * n : 128 * n + 128] = all_ref[rows, :]
    for t, start in enumerate((gin0, gin1)):
        gtin_ref[t : t + 1, :] = all_ref[start : start + 1, :]
    gtout_ref[0:1, :] = all_ref[gout0 : gout0 + 1, :]
    gtout_ref[1:2, :] = gout1_ref[0:1, :]
    tout_ref[0] = all_ref[out0 : out0 + CH, :]
    tout_ref[1] = out1_ref[...]
    bout_ref[...] = all_ref[bout : bout + 1, :]
    bias_ref[...] = all_ref[bias : bias + H, :]
    for q in range(OP):
        rows = slice(outer + OP * q, outer + OP * q + OP)
        outer_ref[:, 128 * q : 128 * q + 128] = all_ref[rows, :]
    for h in range(2):
        here = slice(128 * h, 128 * h + 128)
        unit = all_ref[ab + 2 * OP * h : ab + 2 * OP * (h + 1), :]
        weight = wab_ref[:, here].astype(F32)
        gnode_ref[h : h + 1, :] = jnp.sum(unit * weight, axis=0, keepdims=True)
        ab_ref[:, here] = unit * gain_ref[:, here]


GROUPS = 4
WIDE = 256


def pair_masks(width, dtype):
    lane = lax.broadcasted_iota(jnp.int32, (1, width), 1)
    real = (lane % 128) < 32 * JH
    return [(((lane // 16) % 2 == b) & real).astype(F32).astype(dtype) for b in range(2)]


def spread_items(piece, masks):
    parts = []
    for start in range(0, piece.shape[0], 16):
        parts += [piece[start : start + 16] * mask for mask in masks]
        if start % 48 == 32:
            parts.append(jnp.zeros((32, piece.shape[1]), piece.dtype))
    return jnp.concatenate(parts, axis=0)


def pick_items(values, masks):
    rows = []
    for start in range(0, values.shape[0], 32):
        if start % 128 != 96:
            rows.append(
                values[start : start + 16] * masks[0]
                + values[start + 16 : start + 32] * masks[1]
            )
    return jnp.concatenate(rows, axis=0)


def lane_group(rows):
    return lax.broadcasted_iota(jnp.int32, (rows, 128), 1) // 32


def turn_lanes(values, groups):
    groups = groups % 4
    return pltpu.roll(values, 32 * groups, 1) if groups else values


def split_lanes(thirds):
    group = lane_group(thirds[0].shape[0])
    outs = []
    for k in range(4):
        parts = [turn_lanes(p, j - k) for j, p in enumerate(thirds)]
        outs.append(jnp.where(group == 0, parts[0], jnp.where(group == 1, parts[1], parts[2])))
    return outs


def join_lanes(rows):
    group = lane_group(rows[0].shape[0])
    outs = []
    for j in range(JH):
        parts = [turn_lanes(p, k - j) for k, p in enumerate(rows)]
        low = jnp.where(group == 0, parts[0], parts[1])
        high = jnp.where(group == 2, parts[2], parts[3])
        outs.append(jnp.where(group < 2, low, high))
    return jnp.concatenate(outs, axis=0)


def thirds(values):
    rows = values.shape[0] // JH
    return [values[rows * j : rows * (j + 1)] for j in range(JH)]


def lanes_at(start, size):
    return pl.ds(pl.multiple_of(start, size), size)


def load_double(ref, l_ref, r_ref):
    cols = l_ref.shape[1] // WIDE

    def step(q, carry):
        for r in range(0, ref.shape[0] // cols, 2):
            parts = [split_lanes(thirds(ref[(r + h) * cols + q].astype(F32))) for h in range(2)]
            rows = slice(24 * r, 24 * r + 48)
            for k, out_ref in ((0, l_ref), (2, r_ref)):
                for g in range(2):
                    piece = jnp.concatenate([p[k + g] for p in parts], axis=0)
                    out_ref[rows, lanes_at(128 * (cols * g + q), 128)] = half(piece)
        return carry

    lax.fori_loop(0, cols, step, 0)


def load_single(ref, x_ref):
    cols = x_ref.shape[1] // WIDE

    def step(q, carry):
        for r in range(0, ref.shape[0] // cols, 2):
            parts = [split_lanes(thirds(ref[(r + h) * cols + q].astype(F32))) for h in range(2)]
            rows = slice(24 * r, 24 * r + 48)
            for g in range(2):
                piece = jnp.concatenate([p[k + g] for p in parts for k in (0, 2)], axis=0)
                x_ref[rows, lanes_at(128 * (cols * g + q), 128)] = half(piece)
        return carry

    lax.fori_loop(0, cols, step, 0)


def put_single(ref, row, col, tiles):
    ref[row, col] = half(
        join_lanes([tiles[0][:12], tiles[1][:12], tiles[0][12:], tiles[1][12:]])
    )


def put_double(ref, row, col, left, right):
    ref[row, col] = half(join_lanes(list(left) + list(right)))


def rows_at(at):
    return pl.ds(pl.multiple_of(at * 96, 32), 96)


def side_lanes(ref, g):
    half_width = ref.shape[1] // 2
    return slice(g * half_width, (g + 1) * half_width)


def block_lanes(ref, g, at):
    return lanes_at(g * (ref.shape[1] // 2) + at * WIDE, WIDE)


def stack_blocks(ref, g, at, masks):
    return jnp.concatenate(
        [
            spread_items(ref[96 * n : 96 * n + 96, block_lanes(ref, g, at)], masks)
            for n in range(GROUPS)
        ],
        axis=0,
    )


def unpack_kernel(s_ref, l_ref, r_ref):
    load_double(s_ref, l_ref, r_ref)


def copy_blocks(from_ref, to_ref, sems, at):
    here = pl.ds(2 * at, 2)
    return pltpu.make_async_copy(from_ref.at[:, here], to_ref.at[:, here], sems.at[at])


def out_product_kernel(s_ref, out_ref, p_ref, l_ref, r_ref, sems):
    residues = l_ref.shape[0]
    masks = pair_masks(l_ref.shape[1] // 2, BF16)
    load_double(s_ref, l_ref, r_ref)

    def step(at, carry):
        totals = []
        for g in range(2):
            wide = spread_items(r_ref[rows_at(at), side_lanes(r_ref, g)], masks)
            totals.append(dot(l_ref[:, side_lanes(l_ref, g)], wide, 1, 1))
        for r in range(residues // 24):
            for e in range(2):
                tiles = [
                    total[24 * r : 24 * r + 24, 128 * e : 128 * e + 128] for total in totals
                ]
                put_single(p_ref, r, 2 * at + e, tiles)
        copy_blocks(p_ref, out_ref, sems, at).start()
        return carry

    lax.fori_loop(0, GROUPS, step, 0)
    for at in range(GROUPS):
        copy_blocks(p_ref, out_ref, sems, at).wait()


def flip_all(ref, eye_ref, out_ref):
    for n in range(2 * GROUPS):
        part = slice(WIDE * n, WIDE * n + WIDE)
        out_ref[part, :] = half(dot(eye_ref[...], ref[:, part], 1, 1))


def flipped_rows(f_ref, g):
    rows = f_ref.shape[0] // 2
    return f_ref[rows * g : rows * g + rows, :]


def in_product_kernel(s_ref, eye_ref, out_ref, p_ref, l_ref, r_ref, f_ref, sems):
    masks = pair_masks(WIDE, F32)
    load_double(s_ref, l_ref, r_ref)
    flip_all(l_ref, eye_ref, f_ref)

    def step(to, carry):
        totals = [
            dot(flipped_rows(f_ref, g), r_ref[:, block_lanes(r_ref, g, to)], 1, 0)
            for g in range(2)
        ]
        for at in range(GROUPS):
            rows = [pick_items(t[WIDE * at : WIDE * at + WIDE], masks) for t in totals]
            for r in range(4):
                for e in range(2):
                    tiles = [
                        p[24 * r : 24 * r + 24, 128 * e : 128 * e + 128] for p in rows
                    ]
                    put_single(p_ref, 4 * at + r, 2 * to + e, tiles)
        copy_blocks(p_ref, out_ref, sems, to).start()
        return carry

    lax.fori_loop(0, GROUPS, step, 0)
    for to in range(GROUPS):
        copy_blocks(p_ref, out_ref, sems, to).wait()


def put_grads(d_ref, at, left, right):
    for r in range(left[0].shape[0] // 24):
        for e in range(2):
            here = (slice(24 * r, 24 * r + 24), slice(128 * e, 128 * e + 128))
            put_double(
                d_ref, r, 2 * at + e, [p[here] for p in left], [p[here] for p in right]
            )


def fetch_sides(l_in, r_in, l_ref, r_ref, sems):
    return [
        pltpu.make_async_copy(l_in, l_ref, sems.at[0]),
        pltpu.make_async_copy(r_in, r_ref, sems.at[1]),
    ]


def in_back_kernel(l_in, r_in, dp_ref, out_ref, d_ref, x_ref, l_ref, r_ref, in_sems, sems):
    fetched = fetch_sides(l_in, r_in, l_ref, r_ref, in_sems)
    for copy in fetched:
        copy.start()
    masks = pair_masks(l_ref.shape[1] // 2, BF16)
    one_masks = pair_masks(WIDE, BF16)
    load_single(dp_ref, x_ref)
    for copy in fetched:
        copy.wait()

    def step(at, carry):
        left, right = [], []
        for g in range(2):
            wide = spread_items(x_ref[rows_at(at), side_lanes(x_ref, g)], masks)
            left.append(dot(r_ref[:, side_lanes(r_ref, g)], wide, 1, 1))
            wide = stack_blocks(x_ref, g, at, one_masks)
            right.append(dot(l_ref[:, side_lanes(l_ref, g)], wide, 1, 0))
        put_grads(d_ref, at, left, right)
        copy_blocks(d_ref, out_ref, sems, at).start()
        return carry

    lax.fori_loop(0, GROUPS, step, 0)
    for at in range(GROUPS):
        copy_blocks(d_ref, out_ref, sems, at).wait()


def out_back_kernel(
    l_in, r_in, dp_ref, eye_ref, out_ref, d_ref, x_ref, f_ref, l_ref, r_ref, in_sems, sems
):
    fetched = fetch_sides(l_in, r_in, l_ref, r_ref, in_sems)
    for copy in fetched:
        copy.start()
    cols = l_ref.shape[1] // WIDE
    masks = pair_masks(WIDE, F32)
    one_masks = pair_masks(WIDE, BF16)
    load_single(dp_ref, x_ref)
    flip_all(x_ref, eye_ref, f_ref)
    for copy in fetched:
        copy.wait()

    def step(at, carry):
        left, right = [], []
        for g in range(2):
            total = dot(flipped_rows(f_ref, g), l_ref[:, block_lanes(l_ref, g, at)], 1, 0)
            rows = [
                pick_items(total[WIDE * n : WIDE * n + WIDE], masks) for n in range(GROUPS)
            ]
            right.append(jnp.concatenate(rows, axis=0))
            wide = stack_blocks(r_ref, g, at, one_masks)
            left.append(dot(x_ref[:, side_lanes(x_ref, g)], wide, 1, 0))
        put_grads(d_ref, at, left, right)
        copy_blocks(d_ref, out_ref, sems, at).start()
        return carry

    lax.fori_loop(0, GROUPS, step, 0)
    for at in range(GROUPS):
        copy_blocks(d_ref, out_ref, sems, at).wait()


def cost(flops, nbytes):
    return pl.CostEstimate(flops=int(flops), bytes_accessed=int(nbytes), transcendentals=0)


def spec_of(block, index):
    return pl.BlockSpec(memory_space=pl.ANY) if block is None else pl.BlockSpec(block, index)


def in_place(array):
    return (array, None, None)


def call(kernel, steps, ins, outs, flops, scratch=(), vmem=VMEM):
    nbytes = sum(a.size * a.dtype.itemsize for a, _, _ in ins)
    nbytes += sum(s.size * s.dtype.itemsize for s, _, _ in outs)
    return pl.pallas_call(
        kernel,
        grid=(steps,),
        in_specs=[spec_of(block, index) for _, block, index in ins],
        out_specs=[spec_of(block, index) for _, block, index in outs],
        out_shape=[shape for shape, _, _ in outs],
        scratch_shapes=list(scratch),
        compiler_params=pltpu.CompilerParams(vmem_limit_bytes=vmem),
        cost_estimate=cost(flops, nbytes),
        name=getattr(kernel, "func", kernel).__name__,
    )(*[a for a, _, _ in ins])


def whole(array):
    rank = len(array.shape)
    return (array, tuple(array.shape), lambda s: (0,) * rank)


def sds(shape, dtype):
    return jax.ShapeDtypeStruct(shape, dtype)


def per_device(
    node_feats,
    pair_feats,
    distances,
    lengths,
    node_cotan,
    pair_cotan,
    w_qkv,
    w_bias,
    w_dist,
    w_node_out,
    g_node,
    w_ab,
    w_outer,
    b_outer,
    g_tin,
    w_tin,
    g_tout,
    w_tout,
    g_trans,
    w_up,
    w_down,
):
    row_count = lax.axis_size("row")
    col_count = lax.axis_size("col")
    row_index = lax.axis_index("row")
    col_index = lax.axis_index("col")
    items, tile_rows, tile_cols = pair_feats.shape[:3]
    residues = tile_rows * row_count
    devices = row_count * col_count
    il, jl = tile_rows // 2, tile_cols // JH
    lane_rows = JH * il
    slots = lane_rows * 128
    steps = JH
    width = il * 128
    score_scale = HD ** (-0.5)

    def chan(array):
        return (array, (array.shape[0], width), lambda s: (0, s))

    def rows_of(array):
        return (array, (il, C, 128), lambda s: (s, 0, 0))

    def double(array):
        return (array, (1, 2, il, C, 128), lambda s: (s, 0, 0, 0, 0))

    def tile(array):
        return (array, (items, 2, il, jl, C), lambda s: (0, 0, 0, s, 0))

    def f_chan():
        return chan(sds((C, slots), F32))

    def f_whole(*shape):
        return whole(sds(shape, F32))

    columns = jnp.concatenate([b_outer[None], g_tin, g_tout, g_trans[None]], axis=0)
    columns = columns[:, :, None]

    def column(which):
        return (columns, (1, C, 1), lambda s: (which, 0, 0))

    def layer_of(array):
        return (array, (1,) + array.shape[1:], lambda s: (s, 0, 0))

    def layer(array, which):
        return (array, (1,) + array.shape[1:], lambda s: (which, 0, 0))

    def split_tile(array):
        return array.reshape((items, 2, il) + array.shape[2:])

    def to_slots(array):
        lead = array.shape[:-3]
        array = array.reshape(lead + (items, 2, il, JH, jl))
        at = len(lead)
        order = tuple(range(at)) + tuple(at + d for d in (3, 2, 1, 0, 4))
        return jnp.transpose(array, order).reshape(lead + (lane_rows, 128))

    def from_slots(array):
        lead = array.shape[:-2]
        array = array.reshape(lead + (JH, il, 2, items, jl))
        at = len(lead)
        order = tuple(range(at)) + tuple(at + d for d in (3, 2, 1, 0, 4))
        return jnp.transpose(array, order).reshape(lead + (items, tile_rows, tile_cols))

    def slot_index(dim):
        return lax.broadcasted_iota(jnp.int32, (JH, il, 128), dim)

    lane = slot_index(2)
    row_ids = row_index * tile_rows + (lane // HALF) * il + slot_index(1)
    col_ids = col_index * tile_cols + slot_index(0) * jl + lane % jl
    limit = jnp.tile(jnp.repeat(lengths, jl), 2)[None, None, :]
    keep = ((row_ids < limit) & (col_ids < limit)).astype(F32)
    eye = np.eye(C, dtype=ml_dtypes.bfloat16)
    eye_lanes = np.eye(256, dtype=ml_dtypes.bfloat16)

    def copies(array, axis):
        count = lax.axis_size(axis) if isinstance(axis, str) else devices
        return jnp.broadcast_to(array[None], (count,) + array.shape)

    def swap_all(array, axis):
        return lax.all_to_all(array, axis, split_axis=0, concat_axis=0, tiled=True)

    def tie(*arrays):
        return lax.optimization_barrier(arrays)

    node_rows = jnp.transpose(node_feats, (1, 0, 2)).reshape(tile_rows * items, D)
    cot_rows = jnp.transpose(node_cotan, (1, 0, 2)).reshape(tile_rows * items, D)
    node_full = node_rows.astype(F32)
    parts = tile_cols // tile_rows
    group = row_count // parts
    fetched = []
    for turn in range(parts):
        moves = []
        for src in range(devices):
            src_row, src_col = divmod(src, col_count)
            dst_row = ((src_row + turn) % parts) * group + src_col
            moves.append((src, dst_row * col_count + src_row // parts))
        fetched.append(lax.ppermute(node_rows, BOTH, moves))
    first = row_index // group
    fetched = jnp.stack(fetched)
    col_rows = jnp.concatenate(
        [
            lax.dynamic_index_in_dim(fetched, (first - h) % parts, 0, keepdims=False)
            for h in range(parts)
        ],
        axis=0,
    )
    share = tile_rows * items // col_count

    def node_norm(values):
        centered = values - jnp.mean(values, axis=-1, keepdims=True)
        inv = lax.rsqrt(jnp.mean(centered * centered, axis=-1, keepdims=True) + EPS)
        return centered * inv, inv

    heads_here = H // col_count
    head_width = heads_here * HD
    head_start = col_index * head_width
    w_local = jnp.concatenate(
        [
            lax.dynamic_slice_in_dim(w_qkv, part * D + head_start, head_width, 1)
            for part in range(3)
        ],
        axis=1,
    )
    wo_local = lax.dynamic_slice_in_dim(w_node_out, head_start, head_width, 0)
    node_unit, _ = node_norm(node_full)
    normed_node = half(node_unit * g_node)
    left_node = half(dot(normed_node, w_ab[:, :OP], 1, 0))
    col_unit, _ = node_norm(col_rows.astype(F32))
    def il_first(rows):
        rows = rows.reshape(2, il, items, rows.shape[1])
        return jnp.transpose(rows, (1, 0, 2, 3)).reshape(-1, rows.shape[3])

    left_node = il_first(left_node)
    perm = np.zeros((JH, jl, items, JH, 2, items, jl), ml_dtypes.bfloat16)
    for j in range(JH):
        for n in range(jl):
            for b in range(items):
                perm[j, n, b, j, :, b, n] = 1
    middle, right_wide = call(
        node_kernel,
        1,
        [
            whole(il_first(node_rows)),
            whole(col_rows),
            whole(g_node[None]),
            whole(jnp.transpose(w_ab)),
            whole(w_outer),
            whole(perm.reshape(tile_cols * items, JH * 128)),
        ],
        [
            whole(sds((tile_rows * items, OP * C), F32)),
            whole(sds((JH, OP, 128), F32)),
        ],
        1000,
    )
    dist_slots = to_slots(distances)

    def padded(arrays):
        flat = jnp.concatenate(arrays, axis=0)
        rows = -(-flat.shape[0] // (devices * 8)) * 8
        flat = jnp.pad(flat, ((0, devices * rows - flat.shape[0]), (0, 0)))
        return flat.reshape(devices, rows, 128)

    def to_channels(rows):
        return swap_all(jnp.transpose(rows, (1, 0, 2)), BOTH)

    def to_pairs(slabs):
        slabs = slabs.reshape((devices,) + slabs.shape[2:])
        got = jnp.transpose(swap_all(slabs, BOTH), (1, 0, 2))
        return got if got.shape[0] == lane_rows else got.reshape(sides.shape)

    sides = sds((JH, 2, il, C, 128), BF16)
    single = sds((lane_rows, C, 128), BF16)
    slab1 = (row_count, col_count, lane_rows, 128)
    slab2 = (row_count, col_count, 2 * lane_rows, 128)
    out1, out2 = in_place(sds(slab1, BF16)), in_place(sds(slab2, BF16))
    keep1, keep2 = pltpu.VMEM(slab1, BF16), pltpu.VMEM(slab2, BF16)
    in_sems, out_sems = pltpu.SemaphoreType.DMA((2,)), pltpu.SemaphoreType.DMA((GROUPS,))
    blocks = whole(sds((residues, col_count * 256), BF16))
    block = pltpu.VMEM((residues, col_count * 256), BF16)
    flips = pltpu.VMEM((col_count * 256, residues), BF16)
    chan_flops = 2 * col_count * col_count * residues * 256 * 256
    sums = f_whole(8, C)
    sides_out = (
        sds((C, 2 * lane_rows, 128), BF16),
        (C, 2 * il, 128),
        lambda s: (0, s, 0),
    )
    part = pltpu.VMEM((C, width), BF16)
    square = pltpu.VMEM((C, C), F32)
    wide = pltpu.VMEM((C, 2 * il, 128), F32)
    line = pltpu.VMEM((1, width), F32)

    def part32(rows=C):
        return pltpu.VMEM((rows, width), F32)


    def b_chan(rows=C):
        return chan(sds((rows, slots), BF16))

    g_in = [column(1 + t) for t in range(2)]
    g_out = [column(3 + t) for t in range(2)]
    keep_in = layer_of(keep)
    bd = (right_wide, (1,) + right_wide.shape[1:], lambda s: (s, 0, 0))
    pos_flops = 2 * slots * C * C

    def factors(values, t, more=()):
        return call(
            factor_kernel,
            steps,
            [chan(values), keep_in, g_in[t], layer(w_tin, t)],
            [b_chan(), chan(sds((1, slots), F32)), b_chan(), b_chan(4 * CH), *more],
            5 * pos_flops,
            [part32(5 * CH)],
        )

    pair_one, sides0, mids = call(
        open_kernel,
        steps,
        [
            tile(split_tile(pair_feats)),
            whole(eye),
            whole(middle),
            bd,
            column(0),
            keep_in,
            g_in[0],
            layer(w_tin, 0),
        ],
        [f_chan(), sides_out, whole(sds((2 * items * OP, width), BF16))],
        6 * pos_flops,
        [
            pltpu.VMEM((width, 2 * items * OP), BF16),
            pltpu.VMEM((width, 128), F32),
            part,
            part32(4 * CH),
            part,
            wide,
        ],
    )
    slabs0 = swap_all(sides0, BOTH)
    unit0, inv0, _, factor0, gate0 = factors(pair_one, 0, [b_chan()])
    x_chan, bias = call(
        bias_kernel,
        steps,
        [
            tile(split_tile(pair_feats)),
            whole(eye),
            whole(w_bias),
            (w_dist.reshape(-1, 1), (H, 1), lambda s: (0, 0)),
            chan(dist_slots.reshape(1, slots)),
        ],
        [b_chan(), b_chan(H)],
        pos_flops // 10,
    )

    qkv = half(dot(node_rows, w_local, 1, 0))
    own = copies(qkv[:, head_width:].reshape(-1, 128), "row")
    slabs0, own = tie(slabs0, own)
    everyone = swap_all(own, "row").reshape(residues, items, 2 * head_width)
    (p0,) = call(
        out_product_kernel,
        1,
        [whole(slabs0)],
        [out1],
        chan_flops,
        [keep1, block, block, out_sems],
        SMALL_VMEM,
    )
    p0, everyone = tie(p0, everyone)
    prod0 = to_pairs(p0)
    cot, d_active = call(
        cotangent_kernel,
        steps,
        [tile(split_tile(pair_cotan)), whole(eye), whole(w_down)],
        [b_chan(), b_chan(FT)],
        5 * pos_flops,
    )

    prod0, bias = tie(prod0, bias.reshape(H, lane_rows, 128))
    bias_rows = swap_all(bias, "col")
    pair_two, sides1, gate1 = call(
        middle_kernel,
        steps,
        [
            chan(pair_one),
            chan(gate0),
            rows_of(prod0),
            keep_in,
            g_out[0],
            layer(w_tout, 0),
            g_in[1],
            layer(w_tin, 1),
        ],
        [f_chan(), sides_out, b_chan()],
        6 * pos_flops,
        [part, part32(), part32(5 * CH), wide],
    )
    sides1, bias_rows = tie(sides1, bias_rows)
    slabs1 = swap_all(sides1, BOTH)
    unit1, inv1, normed1, factor1 = factors(pair_two, 1)

    def rear(product, gate, t):
        return call(
            rear_kernel,
            steps,
            [rows_of(product), chan(gate), g_out[t], layer(w_tout, t)],
            [b_chan(), chan(sds((1, slots), F32)), b_chan()],
            pos_flops,
            [part, part32()],
        )

    prod_unit0, prod_inv0, slope0 = rear(prod0, gate0, 0)

    bias_rows = from_slots(bias_rows.reshape(col_count, heads_here, lane_rows, 128))
    bias_rows = jnp.transpose(bias_rows, (2, 1, 3, 0, 4)).reshape(
        items, heads_here, tile_rows, residues
    )
    key_all = everyone[..., :head_width].reshape(residues, items, heads_here, HD)
    value_all = everyone[..., head_width:].reshape(residues, items, heads_here, HD)
    query = qkv[:, :head_width].reshape(tile_rows, items, heads_here, HD)
    all_ids = jnp.arange(residues, dtype=jnp.int32)
    key_keep = (all_ids[None, :] < lengths[:, None]).astype(F32)

    def product(spec, *operands):
        return jnp.einsum(spec, *operands, preferred_element_type=F32)

    scores = (
        product("ighd,jghd->ghij", query, key_all) * score_scale
        + bias_rows.astype(F32)
        + ((key_keep - 1.0) * 1000000000.0)[:, None, None, :]
    )
    probs = jax.nn.softmax(scores, axis=-1)
    probs_half = half(probs)
    attended = half(
        product("ghij,jghd->ighd", probs_half, value_all).reshape(
            tile_rows * items, head_width
        )
    )
    node_part = half(dot(attended, wo_local, 1, 0))
    d_attended = half(dot(cot_rows, wo_local, 1, 1)).reshape(tile_rows, items, heads_here, HD)
    d_probs = product("ighd,jghd->ghij", d_attended, value_all)
    d_value = product("ghij,ighd->jghd", probs_half, d_attended)
    d_scores = half(probs * (d_probs - jnp.sum(probs * d_probs, axis=-1, keepdims=True)))
    d_query = product("ghij,jghd->ighd", d_scores, key_all) * score_scale
    d_key = product("ghij,ighd->jghd", d_scores, query) * score_scale
    d_bias = jnp.transpose(
        d_scores.reshape(items, heads_here, tile_rows, col_count, tile_cols), (3, 1, 0, 2, 4)
    )
    d_bias = to_slots(d_bias).reshape(col_count, heads_here * lane_rows, 128)
    sent = jnp.concatenate([d_bias, node_part.reshape(col_count, -1, 128)], axis=1)
    d_kv = jnp.concatenate(
        [d_key.reshape(-1, head_width), d_value.reshape(-1, head_width)], axis=1
    )
    slabs1, sent = tie(slabs1, sent)
    got = swap_all(sent, "col")
    bias_lanes = heads_here * lane_rows
    d_bias = got[:, :bias_lanes].reshape(H, lane_rows, 128)
    node_sum = jnp.sum(got[:, bias_lanes:].astype(F32), axis=0)
    (p1,) = call(
        in_product_kernel,
        1,
        [whole(slabs1), whole(eye_lanes)],
        [out1],
        chan_flops,
        [keep1, block, block, flips, out_sems],
        SMALL_VMEM,
    )
    p1, d_bias, node_sum = tie(p1, d_bias, node_sum)
    prod1 = to_pairs(p1)
    d_bias32 = d_bias.astype(F32)
    grad_dist = from_slots(jnp.sum(d_bias32 * w_dist[:, None, None], axis=0))
    dw_dist = jnp.sum(d_bias32 * dist_slots[None], axis=(1, 2))
    d_bias_chan = d_bias.reshape(H, slots)

    l1, r1 = call(unpack_kernel, 1, [whole(slabs1)], [blocks, blocks], pos_flops)
    d_kv = half(d_kv).reshape(row_count, -1, 128)
    prod1, d_kv, cot, d_active, l1, r1 = tie(prod1, d_kv, cot, d_active, l1, r1)
    d_kv = swap_all(d_kv, "row")
    grad2, dprod1, dg_trans, dg_out1 = call(
        turn_kernel,
        steps,
        [
            chan(pair_two),
            chan(gate1),
            rows_of(prod1),
            chan(cot),
            chan(d_active),
            g_out[1],
            layer(w_tout, 1),
            column(5),
            whole(w_up),
        ],
        [f_chan(), rows_of(single), sums, sums],
        10 * pos_flops,
        [
            part,
            part,
            part,
            line,
            part,
            line,
            part32(),
            part32(FT),
            pltpu.VMEM((FT, width), BF16),
            square,
            square,
        ],
    )
    dprod1, d_kv = tie(dprod1, d_kv)
    dp1 = to_channels(dprod1)
    _, _, slope1 = rear(prod1, gate1, 1)
    pair_out, dw_down, dw_up, dw_out1 = call(
        finish_kernel,
        steps,
        [
            chan(pair_two),
            chan(gate1),
            rows_of(prod1),
            chan(cot),
            chan(d_active),
            chan(grad2),
            g_out[1],
            layer(w_tout, 1),
            column(5),
            whole(w_up),
            whole(w_down),
        ],
        [
            tile(sds((items, 2, il, tile_cols, C), F32)),
            f_whole(FT, C),
            f_whole(FT, C),
            f_whole(C, CH),
        ],
        13 * pos_flops,
        [
            part,
            part,
            part32(),
            part32(),
            part32(FT),
            pltpu.VMEM((FT, width), BF16),
            pltpu.VMEM((FT, width), BF16),
            pltpu.VMEM((FT, C), F32),
        ],
    )
    d_kv = jnp.sum(d_kv.astype(F32), axis=0).reshape(tile_rows * items, 2 * head_width)
    d_qkv = half(jnp.concatenate([d_query.reshape(-1, head_width), d_kv], axis=1))
    d_att = half(dot(d_qkv, w_local, 1, 1)).reshape(col_count, -1, 128)

    dp1, d_att, dw_down, dw_up, dw_out1 = tie(
        dp1, d_att, dw_down, dw_up, dw_out1
    )
    d_att = swap_all(d_att, "col")
    (d1,) = call(
        in_back_kernel,
        1,
        [in_place(l1), in_place(r1), whole(dp1)],
        [out2],
        2 * chan_flops,
        [keep2, block, block, block, in_sems, out_sems],
    )
    d1, d_att = tie(d1, d_att)
    dsides1 = to_pairs(d1)
    d_att = jnp.sum(d_att.astype(F32), axis=0).reshape(share, D)
    head_grads = jnp.concatenate(
        [dot(d_qkv, node_rows, 0, 0), dot(attended, cot_rows, 0, 0)], axis=0
    )

    mid_arrays = [
        dw_down,
        dw_up,
        dw_out1,
        jnp.pad(dw_dist[None], ((0, 7), (0, 128 - H))),
        dg_trans,
        dg_out1,
    ]
    dsides1, mid_sent, factor1, unit1, slope1, prod_unit0 = tie(
        dsides1, half(padded(mid_arrays)), factor1, unit1, slope1, prod_unit0
    )
    mid_part = swap_all(mid_sent, BOTH)
    grad1, dprod0, dg_in1, dg_out0 = call(
        back_kernel,
        steps,
        [
            double(dsides1),
            chan(factor1),
            chan(slope1),
            chan(unit1),
            chan(inv1),
            chan(grad2),
            g_in[1],
            layer(w_tin, 1),
            chan(gate0),
            chan(prod_unit0),
            chan(prod_inv0),
            g_out[0],
            layer(w_tout, 0),
        ],
        [f_chan(), rows_of(single), sums, sums],
        8 * pos_flops,
        [pltpu.VMEM((5 * CH, width), BF16), part, part, square, square],
    )
    dprod0, mid_part = tie(dprod0, mid_part)
    dp0 = to_channels(dprod0)
    mid_part = jnp.sum(mid_part.astype(F32), axis=0)

    dp0, head_grads = tie(dp0, head_grads.reshape(row_count, -1, 128))
    head_grads = swap_all(head_grads, "row")
    l0, r0 = call(unpack_kernel, 1, [whole(slabs0)], [blocks, blocks], pos_flops)
    (d0,) = call(
        out_back_kernel,
        1,
        [in_place(l0), in_place(r0), whole(dp0), whole(eye_lanes)],
        [out2],
        2 * chan_flops,
        [keep2, block, flips, block, block, in_sems, out_sems],
    )
    d0, head_grads = tie(d0, head_grads)
    dsides0 = to_pairs(d0)
    head_grads = jnp.sum(head_grads, axis=0)
    dw_in1, dw_out0, dw_bias_t = call(
        weights_kernel,
        steps,
        [
            double(dsides1),
            chan(factor1),
            chan(slope1),
            chan(grad2),
            chan(normed1),
            chan(grad1),
            chan(gate0),
            chan(prod_unit0),
            g_out[0],
            chan(d_bias_chan),
            chan(x_chan),
        ],
        [f_whole(5 * CH, C), f_whole(C, CH), f_whole(H, C)],
        6 * pos_flops,
        [pltpu.VMEM((5 * CH, width), BF16), pltpu.VMEM((5 * CH, C), F32)],
    )
    mid_part = half(jnp.concatenate([mid_part, head_grads], axis=0))

    places = jnp.zeros((2, 128, OP * C), BF16)
    places = places.at[0, :OP].set(w_outer).at[1, HALF : HALF + OP].set(w_outer)
    own_row = (jnp.arange(row_count) == row_index).astype(F32)
    own_col = (jnp.arange(row_count) // parts == col_index).astype(F32)
    masks = jnp.concatenate([own_row, own_col])[:, None]
    col_units = jnp.transpose(half(col_unit).reshape(JH, jl, items, D), (0, 2, 1, 3))
    col_units = col_units.reshape(JH, items * jl, D)
    node_share = lax.dynamic_slice_in_dim(node_full, col_index * share, share, 0)
    cot_share = lax.dynamic_slice_in_dim(cot_rows, col_index * share, share, 0)
    unit_share, inv_share = node_norm(node_share)
    out_share = node_share + node_sum.reshape(share, D)
    grad_base = cot_share.astype(F32) + d_att
    unit_il = il_first(half(node_unit))
    (
        dsides0,
        mid_sent,
        dw_in1,
        dw_out0,
        dw_bias_t,
        col_units,
        masks,
        places,
        unit_il,
        unit_share,
        inv_share,
        out_share,
        grad_base,
    ) = tie(
        dsides0,
        copies(mid_part, BOTH),
        dw_in1,
        dw_out0,
        dw_bias_t,
        col_units,
        masks,
        places,
        unit_il,
        unit_share,
        inv_share,
        out_share,
        grad_base,
    )
    mid_all = swap_all(mid_sent, BOTH)
    grad_pair, d_middle, dw_in0, dg_in0, d_right_wide, db_outer = call(
        close_kernel,
        steps,
        [
            double(dsides0),
            chan(factor0),
            chan(slope0),
            chan(unit0),
            chan(inv0),
            chan(grad1),
            keep_in,
            g_in[0],
            layer(w_tin, 0),
            whole(mids),
            bd,
            chan(d_bias_chan),
            whole(w_bias),
        ],
        [
            tile(sds((items, 2, il, tile_cols, C), F32)),
            whole(sds(middle.shape, F32)),
            f_whole(5 * CH, C),
            sums,
            (sds((JH, OP, 128), F32), (1, OP, 128), lambda s: (s, 0, 0)),
            sums,
        ],
        14 * pos_flops,
        [
            pltpu.VMEM((5 * CH, width), BF16),
            part,
            pltpu.VMEM((width, 128), BF16),
            square,
            pltpu.VMEM((width, 2 * items * OP), F32),
            part32(),
            pltpu.VMEM((5 * CH, C), F32),
        ],
    )
    mid_rows = mid_all.shape[1] - head_grads.shape[0]
    pick_left = np.zeros((2, col_count, 8, il, 2, items), ml_dtypes.bfloat16)
    pick_right = np.zeros((parts, 2, JH, col_count, 8, 2, items, jl), ml_dtypes.bfloat16)
    for c in range(col_count):
        for n in range(share):
            i, b = divmod(c * share + n, items)
            pick_left[n % 2, c, n // 2, i % il, i // il, b] = 1
            for h in range(parts):
                j = h * tile_rows + i
                pick_right[h, n % 2, j // jl, c, n // 2, :, b, j % jl] = 1
    pick_left = pick_left.reshape(2, 8 * col_count, tile_rows * items)
    pick_right = pick_right.reshape(parts, 2, JH, 8 * col_count, 128)
    late_arrays = [dw_in0, dg_in0, db_outer, dw_in1, dw_out0, dg_in1, dg_out0, dw_bias_t]
    late_rows = [a.shape[0] for a in late_arrays] + [OP * OP, 4 * OP]
    (sent,) = call(
        functools.partial(tail_kernel, len(late_arrays)),
        1,
        [whole(a) for a in late_arrays]
        + [
            whole(d_middle),
            whole(left_node),
            whole(w_outer),
            whole(unit_il),
            whole(d_right_wide),
            whole(col_units),
            whole(places),
            whole(pick_left),
            whole(pick_right),
            whole(masks),
        ],
        [whole(sds((devices, 32, 128), BF16))],
        1000,
        [pltpu.VMEM((OP * OP, 128), F32), pltpu.VMEM((4 * OP, 128), F32)],
    )
    sent, mid_all = tie(sent, mid_all)
    got = swap_all(sent, BOTH)
    head_grads = mid_all[:, mid_rows:].astype(F32).reshape(row_count, col_count, -1)
    head_grads = jnp.transpose(head_grads, (1, 0, 2)).reshape(col_count, 4, head_width, D)
    g_qkv = jnp.transpose(head_grads[:, :3], (3, 1, 0, 2)).reshape(D, 3 * D)
    g_node_out = head_grads[:, 3].reshape(D, D)

    def widen(blocks):
        count = blocks.shape[0] // 128
        return jnp.concatenate([blocks[128 * n : 128 * n + 128] for n in range(count)], axis=1)

    def cut(flat, counts):
        start, pieces = 0, []
        for rows in counts:
            pieces.append(flat[start : start + rows])
            start += rows
        return pieces

    (
        s_down,
        s_up,
        s_out1,
        s_dist,
        s_trans,
        s_gout1,
    ) = cut(mid_all[:, :mid_rows].reshape(-1, 128).astype(F32), [a.shape[0] for a in mid_arrays])
    s_up = widen(s_up)
    got, g_qkv, g_node_out, s_down, s_up, s_out1, s_gout1 = tie(
        got, g_qkv, g_node_out, s_down, s_up, s_out1, s_gout1
    )
    got = jnp.sum(got.astype(F32), axis=0)
    late_sent = copies(half(got[:24]), BOTH)
    node_part = half(got[24 : 24 + share // 2])
    late_sent, node_part = tie(late_sent, node_part)
    d_pair_rows = node_part.reshape(share, 2 * OP)
    d_normed = half(dot(d_pair_rows, w_ab, 1, 1)).astype(F32)
    scaled = d_normed * g_node
    grad_share = grad_base + inv_share * (
        scaled
        - jnp.mean(scaled, axis=-1, keepdims=True)
        - unit_share * jnp.mean(scaled * unit_share, axis=-1, keepdims=True)
    )
    late_all = swap_all(late_sent, BOTH)
    nodes = jnp.stack([out_share, grad_share])[None]
    reach = 1
    while reach < col_count:
        moves = [(c, c ^ reach) for c in range(col_count)]
        other = lax.ppermute(nodes, "col", moves)
        nodes = jnp.where(
            (col_index // reach) % 2 == 1,
            jnp.concatenate([other, nodes]),
            jnp.concatenate([nodes, other]),
        )
        reach *= 2

    def node_result(which):
        array = nodes[:, which].reshape(tile_rows, items, D)
        return jnp.transpose(array, (1, 0, 2))

    s_tin, s_outer, s_ab, s_gnode, s_bias, s_gtin, s_gtout, s_bout, s_tout = call(
        functools.partial(last_kernel, late_rows),
        1,
        [
            whole(late_all.reshape(-1, 128)),
            whole(jnp.transpose(w_ab)),
            whole(g_node[None]),
            whole(s_out1),
            whole(s_gout1),
        ],
        [
            f_whole(2, C, 5 * CH),
            f_whole(OP, OP * C),
            f_whole(2 * OP, D),
            f_whole(2, 128),
            f_whole(H, C),
            f_whole(2, C),
            f_whole(2, CH),
            f_whole(1, C),
            f_whole(2, CH, C),
        ],
        1000,
        [pltpu.VMEM((24 * devices, 128), F32)],
    )
    return (
        node_result(0),
        pair_out.reshape(pair_feats.shape),
        node_result(1),
        grad_pair.reshape(pair_feats.shape),
        grad_dist,
        g_qkv,
        jnp.transpose(s_bias),
        s_dist[0, :H],
        g_node_out,
        s_gnode.reshape(D),
        jnp.transpose(s_ab),
        s_outer,
        s_bout.reshape(C),
        s_gtin,
        s_tin,
        s_gtout,
        s_tout,
        s_trans[0],
        s_up,
        s_down,
    )


def solution(mesh):
    pair = P(None, "row", "col", None)
    node = P(None, "row", None)
    dist = P(None, "row", "col")
    return jax.shard_map(
        per_device,
        mesh=mesh,
        in_specs=(node, pair, dist, P(), node, pair) + (P(),) * 15,
        out_specs=(node, pair, node, pair, dist) + (P(),) * 15,
        check_vma=False,
    )
```

```python
import functools

import jax
import jax.numpy as jnp
import ml_dtypes
import numpy as np
from jax import lax
from jax.experimental import pallas as pl
from jax.experimental.pallas import tpu as pltpu
from jax.sharding import PartitionSpec as P

D = 256
C = 128
H = 8
HD = 32
CH = 128
OP = 32
FT = 512
ITEMS = 4
EPS = 1e-05
BOTH = ("row", "col")
F32 = jnp.float32
BF16 = jnp.bfloat16
HALF = 64
JH = 3
VMEM = 60 * 1024 * 1024
SMALL_VMEM = 28 * 1024 * 1024


def half(values):
    return values.astype(BF16)


def dot(lhs, rhs, lhs_dim, rhs_dim):
    return lax.dot_general(
        lhs, rhs, (((lhs_dim,), (rhs_dim,)), ((), ())), preferred_element_type=F32
    )


def sigmoid(values):
    return 0.5 * jnp.tanh(0.5 * values) + 0.5


def norm_parts(values):
    scale = 1.0 / values.shape[0]
    centered = values - jnp.sum(values, axis=0, keepdims=True) * scale
    spread = jnp.sum(centered * centered, axis=0, keepdims=True) * scale
    inv = lax.rsqrt(spread + EPS)
    return centered * inv, inv


def norm_back(unit, inv, gain, grad):
    scale = 1.0 / unit.shape[0]
    scaled = grad * gain
    first = jnp.sum(scaled, axis=0, keepdims=True) * scale
    second = jnp.sum(scaled * unit, axis=0, keepdims=True) * scale
    return inv * (scaled - first - unit * second)


def lane_rows_of(width):
    return [(m, slice(128 * m, 128 * m + 128)) for m in range(width // 128)]


def tile_rows_of(ref):
    items, parts, rows = ref.shape[:3]
    return jnp.concatenate(
        [ref[b, h, m] for m in range(rows) for h in range(parts) for b in range(items)],
        axis=0,
    )


def put_tile(ref, m, values):
    items, parts, _, cols = ref.shape[:4]
    flipped = jnp.transpose(values)
    start = 0
    for h in range(parts):
        for b in range(items):
            ref[b, h, m] = flipped[start : start + cols]
            start += cols


def low_lanes(rows):
    return lax.broadcasted_iota(jnp.int32, (rows, 128), 1) < HALF


def swap(values):
    return pltpu.roll(values, HALF, 1)


def get_double(ref, m):
    low = low_lanes(ref.shape[3])
    one, two = ref[0, 0, m].astype(F32), ref[0, 1, m].astype(F32)
    return jnp.where(low, one, swap(two)), jnp.where(low, swap(one), two)


def add_to(ref, values):
    @pl.when(pl.program_id(0) == 0)
    def _():
        ref[...] = values

    @pl.when(pl.program_id(0) != 0)
    def _():
        ref[...] += values


def add_diagonal(ref, total_ref, grad_ref, unit_ref):
    add_to(total_ref, dot(grad_ref[...], unit_ref[...], 1, 1))

    @pl.when(pl.program_id(0) == pl.num_programs(0) - 1)
    def _():
        rows = lax.broadcasted_iota(jnp.int32, total_ref.shape, 0)
        cols = lax.broadcasted_iota(jnp.int32, total_ref.shape, 1)
        picked = jnp.where(rows == cols, total_ref[...], 0.0)
        ref[...] = jnp.broadcast_to(jnp.sum(picked, axis=0, keepdims=True), ref.shape)


def bias_kernel(pair_ref, eye_ref, wb_ref, wd_ref, dist_ref, x_ref, bias_ref):
    x_chan = half(dot(eye_ref[...], tile_rows_of(pair_ref), 1, 1))
    x_ref[...] = x_chan
    bias_ref[...] = half(dot(wb_ref[...], x_chan, 0, 0) + wd_ref[...] * dist_ref[...])


def cotangent_kernel(cot_ref, eye_ref, wdown_plain_ref, out_ref, dact_ref):
    cot = half(dot(eye_ref[...], tile_rows_of(cot_ref), 1, 1))
    out_ref[...] = cot
    dact_ref[...] = half(dot(wdown_plain_ref[...], cot, 1, 0))


def put_sides(proj_ref, keep_ref, sides_ref, wide_ref):
    count = keep_ref.shape[1]
    for m, here in lane_rows_of(proj_ref.shape[1]):
        keep = keep_ref[0, m : m + 1, :]
        left = sigmoid(proj_ref[CH : 2 * CH, here]) * proj_ref[:CH, here] * keep
        right = (
            sigmoid(proj_ref[3 * CH : 4 * CH, here]) * proj_ref[2 * CH : 3 * CH, here] * keep
        )
        low = low_lanes(left.shape[0])
        wide_ref[:, m, :] = jnp.where(low, left, swap(right))
        wide_ref[:, m + count, :] = jnp.where(low, swap(left), right)
    sides_ref[...] = half(wide_ref[...])


def diagonal_blocks(right):
    which = lax.broadcasted_iota(jnp.int32, (8, 128), 0)
    lane = lax.broadcasted_iota(jnp.int32, (8, 128), 1) // 16
    same = (which == lane).astype(F32)
    return half(jnp.concatenate([same * right[q : q + 1] for q in range(OP)], axis=0))


def node_kernel(node_ref, col_ref, gain_ref, wab_ref, wout_ref, perm_ref, mid_ref, right_ref):
    def normed(ref):
        values = ref[...].astype(F32)
        scale = 1.0 / values.shape[1]
        centered = values - jnp.sum(values, axis=1, keepdims=True) * scale
        spread = jnp.sum(centered * centered, axis=1, keepdims=True) * scale
        return half(centered * lax.rsqrt(spread + EPS) * gain_ref[...])

    left = half(dot(wab_ref[...], normed(node_ref), 1, 1))
    mid_ref[...] = dot(left[:OP], wout_ref[...], 0, 0)
    right = half(dot(wab_ref[...], normed(col_ref), 1, 1))
    right = dot(right[OP:], perm_ref[...], 1, 0)
    for j in range(JH):
        right_ref[j] = right[:, 128 * j : 128 * j + 128]


def open_kernel(
    pair_ref,
    eye_ref,
    mid_ref,
    bd_ref,
    bout_ref,
    keep_ref,
    gain_ref,
    w_ref,
    one_ref,
    sides_ref,
    mids_ref,
    mid_t_ref,
    outer_ref,
    normed_ref,
    proj_ref,
    x_ref,
    wide_ref,
):
    @pl.when(pl.program_id(0) == 0)
    def _():
        for m in range(mids_ref.shape[1] // 128):
            rows = [
                mid_ref[8 * m : 8 * m + 8, 128 * q : 128 * q + 128] for q in range(OP)
            ]
            stack = jnp.concatenate(rows, axis=0)
            mids_ref[:, 128 * m : 128 * m + 128] = half(stack)
            mid_t_ref[128 * m : 128 * m + 128, :] = half(jnp.transpose(stack))

    x_ref[...] = half(dot(eye_ref[...], tile_rows_of(pair_ref), 1, 1))
    outer_ref[...] = dot(mid_t_ref[...], diagonal_blocks(bd_ref[0]), 1, 0)
    for m, here in lane_rows_of(x_ref.shape[1]):
        outer = outer_ref[128 * m : 128 * m + 128, :]
        keep = keep_ref[0, m : m + 1, :]
        pair_one = x_ref[:, here].astype(F32) + keep * (outer + bout_ref[0])
        one_ref[:, here] = pair_one
        unit, _ = norm_parts(pair_one)
        normed_ref[:, here] = half(unit * gain_ref[0])
    proj_ref[...] = dot(w_ref[0, :, : 4 * CH], normed_ref[...], 0, 0)
    put_sides(proj_ref, keep_ref, sides_ref, wide_ref)


def factor_kernel(
    in_ref, keep_ref, gain_ref, w_ref, unit_ref, inv_ref, normed_ref, factor_ref, *rest
):
    proj_ref = rest[-1]
    for _, here in lane_rows_of(in_ref.shape[1]):
        unit, inv = norm_parts(in_ref[:, here])
        unit_ref[:, here] = half(unit)
        inv_ref[:, here] = inv
        normed_ref[:, here] = half(unit * gain_ref[0])
    proj_ref[...] = dot(w_ref[0], normed_ref[...], 0, 0)
    for m, here in lane_rows_of(in_ref.shape[1]):
        keep = keep_ref[0, m : m + 1, :]
        for side in range(2):
            start = 2 * CH * side
            sig = sigmoid(proj_ref[start + CH : start + 2 * CH, here])
            first = keep * sig
            factor_ref[start : start + CH, here] = half(first)
            factor_ref[start + CH : start + 2 * CH, here] = half(
                first * proj_ref[start : start + CH, here] * (1.0 - sig)
            )
        if len(rest) > 1:
            rest[0][:, here] = half(sigmoid(proj_ref[4 * CH :, here]))


def rear_kernel(
    prod_ref, gate_ref, gout_ref, wout_ref, unit_ref, inv_ref, slope_ref, y_ref, update_ref
):
    for m, here in lane_rows_of(gate_ref.shape[1]):
        unit, inv = norm_parts(prod_ref[m].astype(F32))
        unit_ref[:, here] = half(unit)
        inv_ref[:, here] = inv
        y_ref[:, here] = half(unit * gout_ref[0])
    update_ref[...] = dot(wout_ref[0], y_ref[...], 0, 0)
    for _, here in lane_rows_of(gate_ref.shape[1]):
        gate = gate_ref[:, here].astype(F32)
        slope_ref[:, here] = half(update_ref[:, here] * gate * (1.0 - gate))


def middle_kernel(
    one_ref,
    gate_ref,
    prod_ref,
    keep_ref,
    gout_ref,
    wout_ref,
    gin_ref,
    w_ref,
    two_ref,
    sides_ref,
    gate_out_ref,
    y_ref,
    update_ref,
    proj_ref,
    wide_ref,
):
    for m, here in lane_rows_of(one_ref.shape[1]):
        unit, _ = norm_parts(prod_ref[m].astype(F32))
        y_ref[:, here] = half(unit * gout_ref[0])
    update_ref[...] = dot(wout_ref[0], y_ref[...], 0, 0)
    for _, here in lane_rows_of(one_ref.shape[1]):
        pair_two = one_ref[:, here] + gate_ref[:, here].astype(F32) * update_ref[:, here]
        two_ref[:, here] = pair_two
        unit, _ = norm_parts(pair_two)
        y_ref[:, here] = half(unit * gin_ref[0])
    proj_ref[...] = dot(w_ref[0], y_ref[...], 0, 0)
    put_sides(proj_ref, keep_ref, sides_ref, wide_ref)
    for _, here in lane_rows_of(one_ref.shape[1]):
        gate_out_ref[:, here] = half(sigmoid(proj_ref[4 * CH :, here]))


def transition(two_ref, gate_ref, prod_ref, gout_ref, wout_ref, gtr_ref, wup_ref, refs):
    y_ref, prod_unit_ref, prod_inv_ref, update_ref = refs[:4]
    three_ref, xt_ref, tr_unit_ref, tr_inv_ref, hidden_ref = refs[4:]
    rows = lane_rows_of(two_ref.shape[1])
    for m, here in rows:
        unit, inv = norm_parts(prod_ref[m].astype(F32))
        if prod_unit_ref is not None:
            prod_inv_ref[:, here] = inv
            prod_unit_ref[:, here] = half(unit)
        y_ref[:, here] = half(unit * gout_ref[0])
    update_ref[...] = dot(wout_ref[0], y_ref[...], 0, 0)
    for _, here in rows:
        pair_three = (
            two_ref[:, here] + gate_ref[:, here].astype(F32) * update_ref[:, here]
        )
        if three_ref is not None:
            three_ref[:, here] = pair_three
        unit, inv = norm_parts(pair_three)
        if tr_unit_ref is not None:
            tr_inv_ref[:, here] = inv
            tr_unit_ref[:, here] = half(unit)
        xt_ref[:, here] = half(unit * gtr_ref[0])


def put_hidden(wup_ref, xt_ref, hidden_ref, here):
    hidden_ref[:, here] = dot(wup_ref[...], xt_ref[:, here], 0, 0)


def groups_of(width):
    step = width // 3
    return [slice(step * n, step * n + step) for n in range(3)]


def put_hidden_back(hidden_ref, dact_ref, dhid_ref, group, active_ref=None):
    for at in range(group.start, group.stop, 128):
        here = slice(at, at + 128)
        for start in range(0, FT, CH):
            part = slice(start, start + CH)
            hidden = hidden_ref[part, here]
            sig = sigmoid(hidden)
            act32 = hidden * sig
            if active_ref is not None:
                active_ref[part, here] = half(act32)
            dhid_ref[part, here] = half(
                dact_ref[part, here].astype(F32) * (sig + act32 * (1.0 - sig))
            )


def turn_kernel(
    two_ref,
    gate_ref,
    prod_ref,
    cot_ref,
    dact_ref,
    gout_ref,
    wout_ref,
    gtr_ref,
    wup_ref,
    grad_ref,
    dprod_ref,
    dgtr_ref,
    dgout_ref,
    small_ref,
    xt_ref,
    tr_unit_ref,
    tr_inv_ref,
    prod_unit_ref,
    prod_inv_ref,
    update_ref,
    hidden_ref,
    dhid_ref,
    tr_total_ref,
    out_total_ref,
):
    rows = lane_rows_of(two_ref.shape[1])
    refs = (small_ref, prod_unit_ref, prod_inv_ref, update_ref)
    refs += (None, xt_ref, tr_unit_ref, tr_inv_ref, hidden_ref)
    transition(two_ref, gate_ref, prod_ref, gout_ref, wout_ref, gtr_ref, wup_ref, refs)
    one, two, three = groups_of(two_ref.shape[1])

    def put_xt_back(here):
        small_ref[:, here] = half(dot(wup_ref[...], dhid_ref[:, here], 1, 0))

    put_hidden(wup_ref, xt_ref, hidden_ref, one)
    put_hidden(wup_ref, xt_ref, hidden_ref, two)
    put_hidden_back(hidden_ref, dact_ref, dhid_ref, one)
    put_hidden(wup_ref, xt_ref, hidden_ref, three)
    put_xt_back(one)
    put_hidden_back(hidden_ref, dact_ref, dhid_ref, two)
    put_xt_back(two)
    put_hidden_back(hidden_ref, dact_ref, dhid_ref, three)
    put_xt_back(three)
    for _, here in rows:
        grad = cot_ref[:, here].astype(F32) + norm_back(
            tr_unit_ref[:, here].astype(F32),
            tr_inv_ref[:, here],
            gtr_ref[0],
            small_ref[:, here].astype(F32),
        )
        grad_ref[:, here] = grad
        xt_ref[:, here] = half(grad * gate_ref[:, here].astype(F32))
    add_diagonal(dgtr_ref, tr_total_ref, small_ref, tr_unit_ref)
    small_ref[...] = half(dot(wout_ref[0], xt_ref[...], 1, 0))
    put_product_back(dprod_ref, prod_unit_ref, prod_inv_ref, gout_ref, small_ref)
    add_diagonal(dgout_ref, out_total_ref, small_ref, prod_unit_ref)


def put_product_back(dprod_ref, unit_ref, inv_ref, gain_ref, dy_ref):
    for m, here in lane_rows_of(unit_ref.shape[1]):
        dprod_ref[m] = half(
            norm_back(
                unit_ref[:, here].astype(F32),
                inv_ref[:, here],
                gain_ref[0],
                dy_ref[:, here].astype(F32),
            )
        )


def finish_kernel(
    two_ref,
    gate_ref,
    prod_ref,
    cot_ref,
    dact_ref,
    grad_ref,
    gout_ref,
    wout_ref,
    gtr_ref,
    wup_ref,
    wdown_ref,
    out_ref,
    dwdown_ref,
    dwup_ref,
    dwout_ref,
    y_ref,
    xt_ref,
    update_ref,
    three_ref,
    hidden_ref,
    dhid_ref,
    active_ref,
    dwup_t_ref,
):
    refs = (y_ref, None, None, update_ref, three_ref, xt_ref, None, None, hidden_ref)
    transition(two_ref, gate_ref, prod_ref, gout_ref, wout_ref, gtr_ref, wup_ref, refs)
    for group in groups_of(two_ref.shape[1]):
        put_hidden(wup_ref, xt_ref, hidden_ref, group)
        put_hidden_back(hidden_ref, dact_ref, dhid_ref, group, active_ref)
    update_ref[...] = dot(wdown_ref[...], active_ref[...], 0, 0)
    for m, here in lane_rows_of(two_ref.shape[1]):
        put_tile(out_ref, m, three_ref[:, here] + update_ref[:, here])
    add_to(dwdown_ref, dot(active_ref[...], cot_ref[...], 1, 1))
    add_to(dwup_t_ref, dot(dhid_ref[...], xt_ref[...], 1, 1))
    d_update = half(grad_ref[...] * gate_ref[...].astype(F32))
    add_to(dwout_ref, dot(y_ref[...], d_update, 1, 1))

    @pl.when(pl.program_id(0) == pl.num_programs(0) - 1)
    def _():
        put_flipped(dwup_ref, dwup_t_ref)


def put_front_grads(sides_ref, factor_ref, slope_ref, grad_ref, dproj_ref):
    for m, here in lane_rows_of(grad_ref.shape[1]):
        sides = get_double(sides_ref, m)
        for at in range(4):
            part = slice(CH * at, CH * at + CH)
            dproj_ref[part, here] = half(sides[at // 2] * factor_ref[part, here].astype(F32))
        dproj_ref[4 * CH :, here] = half(grad_ref[:, here] * slope_ref[:, here].astype(F32))


def front_back(unit_ref, inv_ref, gain_ref, dn_ref, here):
    return norm_back(
        unit_ref[:, here].astype(F32),
        inv_ref[:, here],
        gain_ref[0],
        dn_ref[:, here].astype(F32),
    )


def back_kernel(
    dsides_ref,
    factor_ref,
    slope_ref,
    unit_ref,
    inv_ref,
    grad_ref,
    gin_ref,
    w_ref,
    gate_ref,
    prod_unit_ref,
    prod_inv_ref,
    gout_ref,
    wout_ref,
    grad_out_ref,
    dprod_ref,
    dgin_ref,
    dgout_ref,
    dproj_ref,
    dupd_ref,
    small_ref,
    in_total_ref,
    out_total_ref,
):
    put_front_grads(dsides_ref, factor_ref, slope_ref, grad_ref, dproj_ref)
    small_ref[...] = half(dot(w_ref[0], dproj_ref[...], 1, 0))
    for _, here in lane_rows_of(grad_ref.shape[1]):
        grad = grad_ref[:, here] + front_back(unit_ref, inv_ref, gin_ref, small_ref, here)
        grad_out_ref[:, here] = grad
        dupd_ref[:, here] = half(grad * gate_ref[:, here].astype(F32))
    add_diagonal(dgin_ref, in_total_ref, small_ref, unit_ref)
    small_ref[...] = half(dot(wout_ref[0], dupd_ref[...], 1, 0))
    put_product_back(dprod_ref, prod_unit_ref, prod_inv_ref, gout_ref, small_ref)
    add_diagonal(dgout_ref, out_total_ref, small_ref, prod_unit_ref)


def put_flipped(out_ref, total_ref):
    for start in range(0, total_ref.shape[0], 128):
        out_ref[start : start + 128, :] = jnp.transpose(total_ref[start : start + 128, :])


def weights_kernel(
    dsides_ref,
    factor_ref,
    slope_ref,
    grad_ref,
    normed_ref,
    next_grad_ref,
    gate_ref,
    prod_unit_ref,
    gout_ref,
    dbias_ref,
    x_ref,
    dwin_ref,
    dwout_ref,
    dwb_ref,
    dproj_ref,
    dwin_t_ref,
):
    put_front_grads(dsides_ref, factor_ref, slope_ref, grad_ref, dproj_ref)
    add_to(dwin_t_ref, dot(dproj_ref[...], normed_ref[...], 1, 1))

    @pl.when(pl.program_id(0) == pl.num_programs(0) - 1)
    def _():
        put_flipped(dwin_ref, dwin_t_ref)

    d_update = half(next_grad_ref[...] * gate_ref[...].astype(F32))
    y_half = half(prod_unit_ref[...].astype(F32) * gout_ref[0])
    add_to(dwout_ref, dot(y_half, d_update, 1, 1))
    add_to(dwb_ref, dot(dbias_ref[...], x_ref[...], 1, 1))


def close_kernel(
    dsides_ref,
    factor_ref,
    slope_ref,
    unit_ref,
    inv_ref,
    grad_ref,
    keep_ref,
    gin_ref,
    w_ref,
    mids_ref,
    bd_ref,
    dbias_ref,
    wb_ref,
    out_ref,
    dmid_ref,
    dwin_ref,
    dgin_ref,
    dright_ref,
    dbout_ref,
    dproj_ref,
    small_ref,
    outer_ref,
    in_total_ref,
    dmid_t_ref,
    bias_ref,
    dwin_t_ref,
):
    put_front_grads(dsides_ref, factor_ref, slope_ref, grad_ref, dproj_ref)
    small_ref[...] = half(dot(w_ref[0], dproj_ref[...], 1, 0))
    bias_ref[...] = dot(wb_ref[...], dbias_ref[...], 1, 0)
    total = None
    for m, here in lane_rows_of(grad_ref.shape[1]):
        grad = grad_ref[:, here] + front_back(unit_ref, inv_ref, gin_ref, small_ref, here)
        put_tile(out_ref, m, grad + bias_ref[:, here])
        outer = grad * keep_ref[0, m : m + 1, :]
        outer_ref[128 * m : 128 * m + 128, :] = half(outer)
        total = outer if total is None else total + outer
    normed = half(unit_ref[...].astype(F32) * gin_ref[0])
    add_to(dmid_t_ref, dot(outer_ref[...], diagonal_blocks(bd_ref[0]), 1, 1))
    right = dot(mids_ref[...], outer_ref[...], 1, 0)
    which = lax.broadcasted_iota(jnp.int32, (8, 128), 0)
    lane = lax.broadcasted_iota(jnp.int32, (8, 128), 1) // 16
    for q in range(OP):
        picked = jnp.where(which == lane, right[8 * q : 8 * q + 8], 0.0)
        dright_ref[0, q : q + 1, :] = jnp.sum(picked, axis=0, keepdims=True)
    add_to(dwin_t_ref, dot(dproj_ref[...], normed, 1, 1))
    ones = jnp.ones((8, 128), F32)
    add_to(
        dbout_ref,
        lax.dot_general(
            ones,
            total,
            (((1,), (1,)), ((), ())),
            preferred_element_type=F32,
            precision=lax.Precision.HIGHEST,
        ),
    )
    add_diagonal(dgin_ref, in_total_ref, small_ref, unit_ref)

    @pl.when(pl.program_id(0) == pl.num_programs(0) - 1)
    def _():
        for m in range(dmid_t_ref.shape[0] // 128):
            stack = jnp.transpose(dmid_t_ref[128 * m : 128 * m + 128, :])
            for q in range(OP):
                dmid_ref[8 * m : 8 * m + 8, 128 * q : 128 * q + 128] = stack[
                    8 * q : 8 * q + 8
                ]
        put_flipped(dwin_ref, dwin_t_ref)


def tail_kernel(count, *refs):
    weight_refs, refs = refs[:count], refs[count:]
    dmid_ref, left_ref, wouter_ref, unit_ref, dright_ref, col_unit_ref = refs[:6]
    place_ref, pick_left_ref, pick_right_ref, where_ref = refs[6:10]
    out_ref, outer_ref, small_ref = refs[10:]
    d_mid = half(dmid_ref[...])
    outer = dot(left_ref[...], d_mid, 0, 0)
    for q in range(OP):
        outer_ref[OP * q : OP * q + OP, :] = outer[:, 128 * q : 128 * q + 128]
    d_left = dot(d_mid, wouter_ref[...], 1, 1)
    sums = [dot(half(d_left), unit_ref[...], 0, 0)]
    total = None
    for j in range(JH):
        units = jnp.concatenate([col_unit_ref[j]] * 2, axis=0)
        part = dot(half(dright_ref[j]), units, 1, 0)
        total = part if total is None else total + part
    sums = jnp.concatenate(sums + [total], axis=0)
    small_ref[: 2 * OP, :] = sums[:, :128]
    small_ref[2 * OP :, :] = sums[:, 128:]
    lefts, rights = None, [None, None]
    for s in range(2):
        part = half(dot(half(d_left), place_ref[s], 1, 0))
        part = dot(pick_left_ref[s], part, 1, 0)
        lefts = part if lefts is None else lefts + part
        for j in range(JH):
            above = jnp.zeros((HALF * s + OP, 128), F32)
            spread = [above, dright_ref[j]]
            if s == 0:
                spread.append(jnp.zeros((HALF, 128), F32))
            spread = jnp.concatenate(spread, axis=0)
            spread = half(jnp.transpose(spread))
            for h in range(2):
                part = dot(pick_right_ref[h, s, j], spread, 1, 0)
                rights[h] = part if rights[h] is None else rights[h] + part
    sources = list(weight_refs) + [outer_ref, small_ref]
    pieces = [(ref, at) for ref in sources for at in range(0, ref.shape[0], 8)]
    cols = pick_left_ref.shape[1] // 8
    rows = out_ref.shape[0] // cols
    for r in range(rows):
        in_row = jnp.where(where_ref[0] == r, 1.0, 0.0)
        in_col = jnp.where(where_ref[1] == r // 2, 1.0, 0.0)
        nodes = in_row * lefts + in_col * rights[r % 2]
        for c in range(cols):
            at = 3 * (r * cols + c)
            parts = [ref[k : k + 8, :] for ref, k in pieces[at : at + 3]]
            parts += [jnp.zeros((8, 128), F32)] * (3 - len(parts))
            out_ref[r * cols + c] = half(
                jnp.concatenate(parts + [nodes[8 * c : 8 * c + 8]], axis=0)
            )


def last_kernel(counts, late_ref, wab_ref, gain_ref, out1_ref, gout1_ref, *refs):
    tin_ref, outer_ref, ab_ref, gnode_ref, bias_ref = refs[:5]
    gtin_ref, gtout_ref, bout_ref, tout_ref, all_ref = refs[5:]
    all_ref[...] = late_ref[...].astype(F32)
    starts = [sum(counts[:n]) for n in range(len(counts))]
    in0, gin0, bout, in1, out0, gin1, gout0, bias, outer, ab = starts
    for t, start in enumerate((in0, in1)):
        for n in range(5):
            rows = slice(start + 128 * n, start + 128 * n + 128)
            tin_ref[t, :, 128 * n : 128 * n + 128] = all_ref[rows, :]
    for t, start in enumerate((gin0, gin1)):
        gtin_ref[t : t + 1, :] = all_ref[start : start + 1, :]
    gtout_ref[0:1, :] = all_ref[gout0 : gout0 + 1, :]
    gtout_ref[1:2, :] = gout1_ref[0:1, :]
    tout_ref[0] = all_ref[out0 : out0 + CH, :]
    tout_ref[1] = out1_ref[...]
    bout_ref[...] = all_ref[bout : bout + 1, :]
    bias_ref[...] = all_ref[bias : bias + H, :]
    for q in range(OP):
        rows = slice(outer + OP * q, outer + OP * q + OP)
        outer_ref[:, 128 * q : 128 * q + 128] = all_ref[rows, :]
    for h in range(2):
        here = slice(128 * h, 128 * h + 128)
        unit = all_ref[ab + 2 * OP * h : ab + 2 * OP * (h + 1), :]
        weight = wab_ref[:, here].astype(F32)
        gnode_ref[h : h + 1, :] = jnp.sum(unit * weight, axis=0, keepdims=True)
        ab_ref[:, here] = unit * gain_ref[:, here]


GROUPS = 4
WIDE = 256


def pair_masks(width, dtype):
    lane = lax.broadcasted_iota(jnp.int32, (1, width), 1)
    real = (lane % 128) < 32 * JH
    return [(((lane // 16) % 2 == b) & real).astype(F32).astype(dtype) for b in range(2)]


def spread_items(piece, masks):
    parts = []
    for start in range(0, piece.shape[0], 16):
        parts += [piece[start : start + 16] * mask for mask in masks]
        if start % 48 == 32:
            parts.append(jnp.zeros((32, piece.shape[1]), piece.dtype))
    return jnp.concatenate(parts, axis=0)


def pick_items(values, masks):
    rows = []
    for start in range(0, values.shape[0], 32):
        if start % 128 != 96:
            rows.append(
                values[start : start + 16] * masks[0]
                + values[start + 16 : start + 32] * masks[1]
            )
    return jnp.concatenate(rows, axis=0)


def lane_group(rows):
    return lax.broadcasted_iota(jnp.int32, (rows, 128), 1) // 32


def turn_lanes(values, groups):
    groups = groups % 4
    return pltpu.roll(values, 32 * groups, 1) if groups else values


def split_lanes(thirds):
    group = lane_group(thirds[0].shape[0])
    outs = []
    for k in range(4):
        parts = [turn_lanes(p, j - k) for j, p in enumerate(thirds)]
        outs.append(jnp.where(group == 0, parts[0], jnp.where(group == 1, parts[1], parts[2])))
    return outs


def join_lanes(rows):
    group = lane_group(rows[0].shape[0])
    outs = []
    for j in range(JH):
        parts = [turn_lanes(p, k - j) for k, p in enumerate(rows)]
        low = jnp.where(group == 0, parts[0], parts[1])
        high = jnp.where(group == 2, parts[2], parts[3])
        outs.append(jnp.where(group < 2, low, high))
    return jnp.concatenate(outs, axis=0)


def thirds(values):
    rows = values.shape[0] // JH
    return [values[rows * j : rows * (j + 1)] for j in range(JH)]


def lanes_at(start, size):
    return pl.ds(pl.multiple_of(start, size), size)


def load_double(ref, l_ref, r_ref):
    cols = l_ref.shape[1] // WIDE

    def step(q, carry):
        for r in range(0, ref.shape[0] // cols, 2):
            parts = [split_lanes(thirds(ref[(r + h) * cols + q].astype(F32))) for h in range(2)]
            rows = slice(24 * r, 24 * r + 48)
            for k, out_ref in ((0, l_ref), (2, r_ref)):
                for g in range(2):
                    piece = jnp.concatenate([p[k + g] for p in parts], axis=0)
                    out_ref[rows, lanes_at(128 * (cols * g + q), 128)] = half(piece)
        return carry

    lax.fori_loop(0, cols, step, 0)


def load_single(ref, x_ref):
    cols = x_ref.shape[1] // WIDE

    def step(q, carry):
        for r in range(0, ref.shape[0] // cols, 2):
            parts = [split_lanes(thirds(ref[(r + h) * cols + q].astype(F32))) for h in range(2)]
            rows = slice(24 * r, 24 * r + 48)
            for g in range(2):
                piece = jnp.concatenate([p[k + g] for p in parts for k in (0, 2)], axis=0)
                x_ref[rows, lanes_at(128 * (cols * g + q), 128)] = half(piece)
        return carry

    lax.fori_loop(0, cols, step, 0)


def put_single(ref, row, col, tiles):
    ref[row, col] = half(
        join_lanes([tiles[0][:12], tiles[1][:12], tiles[0][12:], tiles[1][12:]])
    )


def put_double(ref, row, col, left, right):
    ref[row, col] = half(join_lanes(list(left) + list(right)))


def rows_at(at):
    return pl.ds(pl.multiple_of(at * 96, 32), 96)


def side_lanes(ref, g):
    half_width = ref.shape[1] // 2
    return slice(g * half_width, (g + 1) * half_width)


def block_lanes(ref, g, at):
    return lanes_at(g * (ref.shape[1] // 2) + at * WIDE, WIDE)


def stack_blocks(ref, g, at, masks):
    return jnp.concatenate(
        [
            spread_items(ref[96 * n : 96 * n + 96, block_lanes(ref, g, at)], masks)
            for n in range(GROUPS)
        ],
        axis=0,
    )


def unpack_kernel(s_ref, l_ref, r_ref):
    load_double(s_ref, l_ref, r_ref)


def copy_blocks(from_ref, to_ref, sems, at):
    here = pl.ds(2 * at, 2)
    return pltpu.make_async_copy(from_ref.at[:, here], to_ref.at[:, here], sems.at[at])


def out_product_kernel(s_ref, out_ref, p_ref, l_ref, r_ref, sems):
    residues = l_ref.shape[0]
    masks = pair_masks(l_ref.shape[1] // 2, BF16)
    load_double(s_ref, l_ref, r_ref)

    def step(at, carry):
        totals = []
        for g in range(2):
            wide = spread_items(r_ref[rows_at(at), side_lanes(r_ref, g)], masks)
            totals.append(dot(l_ref[:, side_lanes(l_ref, g)], wide, 1, 1))
        for r in range(residues // 24):
            for e in range(2):
                tiles = [
                    total[24 * r : 24 * r + 24, 128 * e : 128 * e + 128] for total in totals
                ]
                put_single(p_ref, r, 2 * at + e, tiles)
        copy_blocks(p_ref, out_ref, sems, at).start()
        return carry

    lax.fori_loop(0, GROUPS, step, 0)
    for at in range(GROUPS):
        copy_blocks(p_ref, out_ref, sems, at).wait()


def flip_all(ref, eye_ref, out_ref):
    for n in range(2 * GROUPS):
        part = slice(WIDE * n, WIDE * n + WIDE)
        out_ref[part, :] = half(dot(eye_ref[...], ref[:, part], 1, 1))


def flipped_rows(f_ref, g):
    rows = f_ref.shape[0] // 2
    return f_ref[rows * g : rows * g + rows, :]


def in_product_kernel(s_ref, eye_ref, out_ref, p_ref, l_ref, r_ref, f_ref, sems):
    masks = pair_masks(WIDE, F32)
    load_double(s_ref, l_ref, r_ref)
    flip_all(l_ref, eye_ref, f_ref)

    def step(to, carry):
        totals = [
            dot(flipped_rows(f_ref, g), r_ref[:, block_lanes(r_ref, g, to)], 1, 0)
            for g in range(2)
        ]
        for at in range(GROUPS):
            rows = [pick_items(t[WIDE * at : WIDE * at + WIDE], masks) for t in totals]
            for r in range(4):
                for e in range(2):
                    tiles = [
                        p[24 * r : 24 * r + 24, 128 * e : 128 * e + 128] for p in rows
                    ]
                    put_single(p_ref, 4 * at + r, 2 * to + e, tiles)
        copy_blocks(p_ref, out_ref, sems, to).start()
        return carry

    lax.fori_loop(0, GROUPS, step, 0)
    for to in range(GROUPS):
        copy_blocks(p_ref, out_ref, sems, to).wait()


def put_grads(d_ref, at, left, right):
    for r in range(left[0].shape[0] // 24):
        for e in range(2):
            here = (slice(24 * r, 24 * r + 24), slice(128 * e, 128 * e + 128))
            put_double(
                d_ref, r, 2 * at + e, [p[here] for p in left], [p[here] for p in right]
            )


def fetch_sides(l_in, r_in, l_ref, r_ref, sems):
    return [
        pltpu.make_async_copy(l_in, l_ref, sems.at[0]),
        pltpu.make_async_copy(r_in, r_ref, sems.at[1]),
    ]


def in_back_kernel(l_in, r_in, dp_ref, out_ref, d_ref, x_ref, l_ref, r_ref, in_sems, sems):
    fetched = fetch_sides(l_in, r_in, l_ref, r_ref, in_sems)
    for copy in fetched:
        copy.start()
    masks = pair_masks(l_ref.shape[1] // 2, BF16)
    one_masks = pair_masks(WIDE, BF16)
    load_single(dp_ref, x_ref)
    for copy in fetched:
        copy.wait()

    def step(at, carry):
        left, right = [], []
        for g in range(2):
            wide = spread_items(x_ref[rows_at(at), side_lanes(x_ref, g)], masks)
            left.append(dot(r_ref[:, side_lanes(r_ref, g)], wide, 1, 1))
            wide = stack_blocks(x_ref, g, at, one_masks)
            right.append(dot(l_ref[:, side_lanes(l_ref, g)], wide, 1, 0))
        put_grads(d_ref, at, left, right)
        copy_blocks(d_ref, out_ref, sems, at).start()
        return carry

    lax.fori_loop(0, GROUPS, step, 0)
    for at in range(GROUPS):
        copy_blocks(d_ref, out_ref, sems, at).wait()


def out_back_kernel(
    l_in, r_in, dp_ref, eye_ref, out_ref, d_ref, x_ref, f_ref, l_ref, r_ref, in_sems, sems
):
    fetched = fetch_sides(l_in, r_in, l_ref, r_ref, in_sems)
    for copy in fetched:
        copy.start()
    cols = l_ref.shape[1] // WIDE
    masks = pair_masks(WIDE, F32)
    one_masks = pair_masks(WIDE, BF16)
    load_single(dp_ref, x_ref)
    flip_all(x_ref, eye_ref, f_ref)
    for copy in fetched:
        copy.wait()

    def step(at, carry):
        left, right = [], []
        for g in range(2):
            total = dot(flipped_rows(f_ref, g), l_ref[:, block_lanes(l_ref, g, at)], 1, 0)
            rows = [
                pick_items(total[WIDE * n : WIDE * n + WIDE], masks) for n in range(GROUPS)
            ]
            right.append(jnp.concatenate(rows, axis=0))
            wide = stack_blocks(r_ref, g, at, one_masks)
            left.append(dot(x_ref[:, side_lanes(x_ref, g)], wide, 1, 0))
        put_grads(d_ref, at, left, right)
        copy_blocks(d_ref, out_ref, sems, at).start()
        return carry

    lax.fori_loop(0, GROUPS, step, 0)
    for at in range(GROUPS):
        copy_blocks(d_ref, out_ref, sems, at).wait()


def cost(flops, nbytes):
    return pl.CostEstimate(flops=int(flops), bytes_accessed=int(nbytes), transcendentals=0)


def spec_of(block, index):
    if block is None:
        return pl.BlockSpec(memory_space=index or pl.ANY)
    return pl.BlockSpec(block, index)


def in_place(array):
    return (array, None, None)


def call(kernel, steps, ins, outs, flops, scratch=(), vmem=VMEM):
    nbytes = sum(a.size * a.dtype.itemsize for a, _, _ in ins)
    nbytes += sum(s.size * s.dtype.itemsize for s, _, _ in outs)
    return pl.pallas_call(
        kernel,
        grid=(steps,),
        in_specs=[spec_of(block, index) for _, block, index in ins],
        out_specs=[spec_of(block, index) for _, block, index in outs],
        out_shape=[shape for shape, _, _ in outs],
        scratch_shapes=list(scratch),
        compiler_params=pltpu.CompilerParams(vmem_limit_bytes=vmem),
        cost_estimate=cost(flops, nbytes),
        name=getattr(kernel, "func", kernel).__name__,
    )(*[a for a, _, _ in ins])


def whole(array):
    rank = len(array.shape)
    return (array, tuple(array.shape), lambda s: (0,) * rank)


def sds(shape, dtype):
    return jax.ShapeDtypeStruct(shape, dtype)


def per_device(
    node_feats,
    pair_feats,
    distances,
    lengths,
    node_cotan,
    pair_cotan,
    w_qkv,
    w_bias,
    w_dist,
    w_node_out,
    g_node,
    w_ab,
    w_outer,
    b_outer,
    g_tin,
    w_tin,
    g_tout,
    w_tout,
    g_trans,
    w_up,
    w_down,
):
    row_count = lax.axis_size("row")
    col_count = lax.axis_size("col")
    row_index = lax.axis_index("row")
    col_index = lax.axis_index("col")
    items, tile_rows, tile_cols = pair_feats.shape[:3]
    residues = tile_rows * row_count
    devices = row_count * col_count
    il, jl = tile_rows // 2, tile_cols // JH
    lane_rows = JH * il
    slots = lane_rows * 128
    steps = JH
    width = il * 128
    score_scale = HD ** (-0.5)

    def chan(array):
        return (array, (array.shape[0], width), lambda s: (0, s))

    def rows_of(array):
        return (array, (il, C, 128), lambda s: (s, 0, 0))

    def double(array):
        return (array, (1, 2, il, C, 128), lambda s: (s, 0, 0, 0, 0))

    def tile(array):
        return (array, (items, 2, il, jl, C), lambda s: (0, 0, 0, s, 0))

    def f_chan():
        return chan(sds((C, slots), F32))

    def f_whole(*shape):
        return whole(sds(shape, F32))

    columns = jnp.concatenate([b_outer[None], g_tin, g_tout, g_trans[None]], axis=0)
    columns = columns[:, :, None]

    def column(which):
        return (columns, (1, C, 1), lambda s: (which, 0, 0))

    def layer_of(array):
        return (array, (1,) + array.shape[1:], lambda s: (s, 0, 0))

    def layer(array, which):
        return (array, (1,) + array.shape[1:], lambda s: (which, 0, 0))

    def split_tile(array):
        return array.reshape((items, 2, il) + array.shape[2:])

    def to_slots(array):
        lead = array.shape[:-3]
        array = array.reshape(lead + (items, 2, il, JH, jl))
        at = len(lead)
        order = tuple(range(at)) + tuple(at + d for d in (3, 2, 1, 0, 4))
        return jnp.transpose(array, order).reshape(lead + (lane_rows, 128))

    def from_slots(array):
        lead = array.shape[:-2]
        array = array.reshape(lead + (JH, il, 2, items, jl))
        at = len(lead)
        order = tuple(range(at)) + tuple(at + d for d in (3, 2, 1, 0, 4))
        return jnp.transpose(array, order).reshape(lead + (items, tile_rows, tile_cols))

    def slot_index(dim):
        return lax.broadcasted_iota(jnp.int32, (JH, il, 128), dim)

    lane = slot_index(2)
    row_ids = row_index * tile_rows + (lane // HALF) * il + slot_index(1)
    col_ids = col_index * tile_cols + slot_index(0) * jl + lane % jl
    limit = jnp.tile(jnp.repeat(lengths, jl), 2)[None, None, :]
    keep = ((row_ids < limit) & (col_ids < limit)).astype(F32)
    eye = np.eye(C, dtype=ml_dtypes.bfloat16)
    eye_lanes = np.eye(256, dtype=ml_dtypes.bfloat16)

    def copies(array, axis):
        count = lax.axis_size(axis) if isinstance(axis, str) else devices
        return jnp.broadcast_to(array[None], (count,) + array.shape)

    def swap_all(array, axis):
        return lax.all_to_all(array, axis, split_axis=0, concat_axis=0, tiled=True)

    def tie(*arrays):
        return lax.optimization_barrier(arrays)

    node_rows = jnp.transpose(node_feats, (1, 0, 2)).reshape(tile_rows * items, D)
    cot_rows = jnp.transpose(node_cotan, (1, 0, 2)).reshape(tile_rows * items, D)
    node_full = node_rows.astype(F32)
    parts = tile_cols // tile_rows
    group = row_count // parts
    fetched = []
    for turn in range(parts):
        moves = []
        for src in range(devices):
            src_row, src_col = divmod(src, col_count)
            dst_row = ((src_row + turn) % parts) * group + src_col
            moves.append((src, dst_row * col_count + src_row // parts))
        fetched.append(lax.ppermute(node_rows, BOTH, moves))
    first = row_index // group
    fetched = jnp.stack(fetched)
    col_rows = jnp.concatenate(
        [
            lax.dynamic_index_in_dim(fetched, (first - h) % parts, 0, keepdims=False)
            for h in range(parts)
        ],
        axis=0,
    )
    share = tile_rows * items // col_count

    def node_norm(values):
        centered = values - jnp.mean(values, axis=-1, keepdims=True)
        inv = lax.rsqrt(jnp.mean(centered * centered, axis=-1, keepdims=True) + EPS)
        return centered * inv, inv

    heads_here = H // col_count
    head_width = heads_here * HD
    head_start = col_index * head_width
    w_local = jnp.concatenate(
        [
            lax.dynamic_slice_in_dim(w_qkv, part * D + head_start, head_width, 1)
            for part in range(3)
        ],
        axis=1,
    )
    wo_local = lax.dynamic_slice_in_dim(w_node_out, head_start, head_width, 0)
    node_unit, _ = node_norm(node_full)
    normed_node = half(node_unit * g_node)
    left_node = half(dot(normed_node, w_ab[:, :OP], 1, 0))
    col_unit, _ = node_norm(col_rows.astype(F32))
    def il_first(rows):
        rows = rows.reshape(2, il, items, rows.shape[1])
        return jnp.transpose(rows, (1, 0, 2, 3)).reshape(-1, rows.shape[3])

    left_node = il_first(left_node)
    perm = np.zeros((JH, jl, items, JH, 2, items, jl), ml_dtypes.bfloat16)
    for j in range(JH):
        for n in range(jl):
            for b in range(items):
                perm[j, n, b, j, :, b, n] = 1
    middle, right_wide = call(
        node_kernel,
        1,
        [
            whole(il_first(node_rows)),
            whole(col_rows),
            whole(g_node[None]),
            whole(jnp.transpose(w_ab)),
            whole(w_outer),
            whole(perm.reshape(tile_cols * items, JH * 128)),
        ],
        [
            whole(sds((tile_rows * items, OP * C), F32)),
            whole(sds((JH, OP, 128), F32)),
        ],
        1000,
    )
    dist_slots = to_slots(distances)

    def padded(arrays):
        flat = jnp.concatenate(arrays, axis=0)
        rows = -(-flat.shape[0] // (devices * 8)) * 8
        flat = jnp.pad(flat, ((0, devices * rows - flat.shape[0]), (0, 0)))
        return flat.reshape(devices, rows, 128)

    def to_channels(rows):
        return swap_all(jnp.transpose(rows, (1, 0, 2)), BOTH)

    def to_pairs(slabs):
        slabs = slabs.reshape((devices,) + slabs.shape[2:])
        got = jnp.transpose(swap_all(slabs, BOTH), (1, 0, 2))
        return got if got.shape[0] == lane_rows else got.reshape(sides.shape)

    sides = sds((JH, 2, il, C, 128), BF16)
    single = sds((lane_rows, C, 128), BF16)
    slab1 = (row_count, col_count, lane_rows, 128)
    slab2 = (row_count, col_count, 2 * lane_rows, 128)
    out1, out2 = in_place(sds(slab1, BF16)), in_place(sds(slab2, BF16))
    keep1, keep2 = pltpu.VMEM(slab1, BF16), pltpu.VMEM(slab2, BF16)
    in_sems, out_sems = pltpu.SemaphoreType.DMA((2,)), pltpu.SemaphoreType.DMA((GROUPS,))
    blocks = whole(sds((residues, col_count * 256), BF16))
    block = pltpu.VMEM((residues, col_count * 256), BF16)
    flips = pltpu.VMEM((col_count * 256, residues), BF16)
    chan_flops = 2 * col_count * col_count * residues * 256 * 256
    sums = f_whole(8, C)
    sides_out = (
        sds((C, 2 * lane_rows, 128), BF16),
        (C, 2 * il, 128),
        lambda s: (0, s, 0),
    )
    part = pltpu.VMEM((C, width), BF16)
    square = pltpu.VMEM((C, C), F32)
    wide = pltpu.VMEM((C, 2 * il, 128), F32)
    line = pltpu.VMEM((1, width), F32)

    def part32(rows=C):
        return pltpu.VMEM((rows, width), F32)


    def b_chan(rows=C):
        return chan(sds((rows, slots), BF16))

    g_in = [column(1 + t) for t in range(2)]
    g_out = [column(3 + t) for t in range(2)]
    keep_in = layer_of(keep)
    bd = (right_wide, (1,) + right_wide.shape[1:], lambda s: (s, 0, 0))
    pos_flops = 2 * slots * C * C

    def factors(values, t, more=()):
        return call(
            factor_kernel,
            steps,
            [chan(values), keep_in, g_in[t], layer(w_tin, t)],
            [b_chan(), chan(sds((1, slots), F32)), b_chan(), b_chan(4 * CH), *more],
            5 * pos_flops,
            [part32(5 * CH)],
        )

    pair_one, sides0, mids = call(
        open_kernel,
        steps,
        [
            tile(split_tile(pair_feats)),
            whole(eye),
            whole(middle),
            bd,
            column(0),
            keep_in,
            g_in[0],
            layer(w_tin, 0),
        ],
        [f_chan(), sides_out, whole(sds((2 * items * OP, width), BF16))],
        6 * pos_flops,
        [
            pltpu.VMEM((width, 2 * items * OP), BF16),
            pltpu.VMEM((width, 128), F32),
            part,
            part32(4 * CH),
            part,
            wide,
        ],
    )
    slabs0 = swap_all(sides0, BOTH)
    unit0, inv0, _, factor0, gate0 = factors(pair_one, 0, [b_chan()])
    x_chan, bias = call(
        bias_kernel,
        steps,
        [
            tile(split_tile(pair_feats)),
            whole(eye),
            whole(w_bias),
            (w_dist.reshape(-1, 1), (H, 1), lambda s: (0, 0)),
            chan(dist_slots.reshape(1, slots)),
        ],
        [b_chan(), b_chan(H)],
        pos_flops // 10,
    )

    qkv = half(dot(node_rows, w_local, 1, 0))
    own = copies(qkv[:, head_width:].reshape(-1, 128), "row")
    slabs0, own = tie(slabs0, own)
    everyone = swap_all(own, "row").reshape(residues, items, 2 * head_width)
    (p0,) = call(
        out_product_kernel,
        1,
        [whole(slabs0)],
        [out1],
        chan_flops,
        [keep1, block, block, out_sems],
        SMALL_VMEM,
    )
    p0, everyone = tie(p0, everyone)
    prod0 = to_pairs(p0)
    cot, d_active = call(
        cotangent_kernel,
        steps,
        [tile(split_tile(pair_cotan)), whole(eye), whole(w_down)],
        [b_chan(), b_chan(FT)],
        5 * pos_flops,
    )

    prod0, bias = tie(prod0, bias.reshape(H, lane_rows, 128))
    bias_rows = swap_all(bias, "col")
    pair_two, sides1, gate1 = call(
        middle_kernel,
        steps,
        [
            chan(pair_one),
            chan(gate0),
            rows_of(prod0),
            keep_in,
            g_out[0],
            layer(w_tout, 0),
            g_in[1],
            layer(w_tin, 1),
        ],
        [f_chan(), sides_out, b_chan()],
        6 * pos_flops,
        [part, part32(), part32(5 * CH), wide],
    )
    sides1, bias_rows = tie(sides1, bias_rows)
    slabs1 = swap_all(sides1, BOTH)
    unit1, inv1, normed1, factor1 = factors(pair_two, 1)

    def rear(product, gate, t):
        return call(
            rear_kernel,
            steps,
            [rows_of(product), chan(gate), g_out[t], layer(w_tout, t)],
            [b_chan(), chan(sds((1, slots), F32)), b_chan()],
            pos_flops,
            [part, part32()],
        )

    prod_unit0, prod_inv0, slope0 = rear(prod0, gate0, 0)

    bias_rows = from_slots(bias_rows.reshape(col_count, heads_here, lane_rows, 128))
    bias_rows = jnp.transpose(bias_rows, (2, 1, 3, 0, 4)).reshape(
        items, heads_here, tile_rows, residues
    )
    key_all = everyone[..., :head_width].reshape(residues, items, heads_here, HD)
    value_all = everyone[..., head_width:].reshape(residues, items, heads_here, HD)
    query = qkv[:, :head_width].reshape(tile_rows, items, heads_here, HD)
    all_ids = jnp.arange(residues, dtype=jnp.int32)
    key_keep = (all_ids[None, :] < lengths[:, None]).astype(F32)

    def product(spec, *operands):
        return jnp.einsum(spec, *operands, preferred_element_type=F32)

    scores = (
        product("ighd,jghd->ghij", query, key_all) * score_scale
        + bias_rows.astype(F32)
        + ((key_keep - 1.0) * 1000000000.0)[:, None, None, :]
    )
    probs = jax.nn.softmax(scores, axis=-1)
    probs_half = half(probs)
    attended = half(
        product("ghij,jghd->ighd", probs_half, value_all).reshape(
            tile_rows * items, head_width
        )
    )
    node_part = half(dot(attended, wo_local, 1, 0))
    d_attended = half(dot(cot_rows, wo_local, 1, 1)).reshape(tile_rows, items, heads_here, HD)
    d_probs = product("ighd,jghd->ghij", d_attended, value_all)
    d_value = product("ghij,ighd->jghd", probs_half, d_attended)
    d_scores = half(probs * (d_probs - jnp.sum(probs * d_probs, axis=-1, keepdims=True)))
    d_query = product("ghij,jghd->ighd", d_scores, key_all) * score_scale
    d_key = product("ghij,ighd->jghd", d_scores, query) * score_scale
    d_bias = jnp.transpose(
        d_scores.reshape(items, heads_here, tile_rows, col_count, tile_cols), (3, 1, 0, 2, 4)
    )
    d_bias = to_slots(d_bias).reshape(col_count, heads_here * lane_rows, 128)
    sent = jnp.concatenate([d_bias, node_part.reshape(col_count, -1, 128)], axis=1)
    d_kv = jnp.concatenate(
        [d_key.reshape(-1, head_width), d_value.reshape(-1, head_width)], axis=1
    )
    slabs1, sent = tie(slabs1, sent)
    got = swap_all(sent, "col")
    bias_lanes = heads_here * lane_rows
    d_bias = got[:, :bias_lanes].reshape(H, lane_rows, 128)
    node_sum = jnp.sum(got[:, bias_lanes:].astype(F32), axis=0)
    (p1,) = call(
        in_product_kernel,
        1,
        [whole(slabs1), whole(eye_lanes)],
        [out1],
        chan_flops,
        [keep1, block, block, flips, out_sems],
        SMALL_VMEM,
    )
    p1, d_bias, node_sum = tie(p1, d_bias, node_sum)
    prod1 = to_pairs(p1)
    d_bias32 = d_bias.astype(F32)
    grad_dist = from_slots(jnp.sum(d_bias32 * w_dist[:, None, None], axis=0))
    dw_dist = jnp.sum(d_bias32 * dist_slots[None], axis=(1, 2))
    d_bias_chan = d_bias.reshape(H, slots)

    l1, r1 = call(unpack_kernel, 1, [whole(slabs1)], [blocks, blocks], pos_flops)
    d_kv = half(d_kv).reshape(row_count, -1, 128)
    prod1, d_kv, cot, d_active, l1, r1 = tie(prod1, d_kv, cot, d_active, l1, r1)
    d_kv = swap_all(d_kv, "row")
    grad2, dprod1, dg_trans, dg_out1 = call(
        turn_kernel,
        steps,
        [
            chan(pair_two),
            chan(gate1),
            rows_of(prod1),
            chan(cot),
            chan(d_active),
            g_out[1],
            layer(w_tout, 1),
            column(5),
            whole(w_up),
        ],
        [f_chan(), rows_of(single), sums, sums],
        10 * pos_flops,
        [
            part,
            part,
            part,
            line,
            part,
            line,
            part32(),
            part32(FT),
            pltpu.VMEM((FT, width), BF16),
            square,
            square,
        ],
    )
    dprod1, d_kv = tie(dprod1, d_kv)
    dp1 = to_channels(dprod1)
    _, _, slope1 = rear(prod1, gate1, 1)
    pair_out, dw_down, dw_up, dw_out1 = call(
        finish_kernel,
        steps,
        [
            chan(pair_two),
            chan(gate1),
            rows_of(prod1),
            chan(cot),
            chan(d_active),
            chan(grad2),
            g_out[1],
            layer(w_tout, 1),
            column(5),
            whole(w_up),
            whole(w_down),
        ],
        [
            tile(sds((items, 2, il, tile_cols, C), F32)),
            f_whole(FT, C),
            f_whole(FT, C),
            f_whole(C, CH),
        ],
        13 * pos_flops,
        [
            part,
            part,
            part32(),
            part32(),
            part32(FT),
            pltpu.VMEM((FT, width), BF16),
            pltpu.VMEM((FT, width), BF16),
            pltpu.VMEM((FT, C), F32),
        ],
    )
    d_kv = jnp.sum(d_kv.astype(F32), axis=0).reshape(tile_rows * items, 2 * head_width)
    d_qkv = half(jnp.concatenate([d_query.reshape(-1, head_width), d_kv], axis=1))
    d_att = half(dot(d_qkv, w_local, 1, 1)).reshape(col_count, -1, 128)

    dp1, d_att, dw_down, dw_up, dw_out1 = tie(
        dp1, d_att, dw_down, dw_up, dw_out1
    )
    d_att = swap_all(d_att, "col")
    (d1,) = call(
        in_back_kernel,
        1,
        [in_place(l1), in_place(r1), whole(dp1)],
        [out2],
        2 * chan_flops,
        [keep2, block, block, block, in_sems, out_sems],
    )
    d1, d_att = tie(d1, d_att)
    dsides1 = to_pairs(d1)
    d_att = jnp.sum(d_att.astype(F32), axis=0).reshape(share, D)
    head_grads = jnp.concatenate(
        [dot(d_qkv, node_rows, 0, 0), dot(attended, cot_rows, 0, 0)], axis=0
    )

    mid_arrays = [
        dw_down,
        dw_up,
        dw_out1,
        jnp.pad(dw_dist[None], ((0, 7), (0, 128 - H))),
        dg_trans,
        dg_out1,
    ]
    dsides1, mid_sent, factor1, unit1, slope1, prod_unit0 = tie(
        dsides1, half(padded(mid_arrays)), factor1, unit1, slope1, prod_unit0
    )
    mid_part = swap_all(mid_sent, BOTH)
    grad1, dprod0, dg_in1, dg_out0 = call(
        back_kernel,
        steps,
        [
            double(dsides1),
            chan(factor1),
            chan(slope1),
            chan(unit1),
            chan(inv1),
            chan(grad2),
            g_in[1],
            layer(w_tin, 1),
            chan(gate0),
            chan(prod_unit0),
            chan(prod_inv0),
            g_out[0],
            layer(w_tout, 0),
        ],
        [f_chan(), rows_of(single), sums, sums],
        8 * pos_flops,
        [pltpu.VMEM((5 * CH, width), BF16), part, part, square, square],
    )
    dprod0, mid_part = tie(dprod0, mid_part)
    dp0 = to_channels(dprod0)
    mid_part = jnp.sum(mid_part.astype(F32), axis=0)

    dp0, head_grads = tie(dp0, head_grads.reshape(row_count, -1, 128))
    head_grads = swap_all(head_grads, "row")
    l0, r0 = call(unpack_kernel, 1, [whole(slabs0)], [blocks, blocks], pos_flops)
    (d0,) = call(
        out_back_kernel,
        1,
        [in_place(l0), in_place(r0), whole(dp0), whole(eye_lanes)],
        [out2],
        2 * chan_flops,
        [keep2, block, flips, block, block, in_sems, out_sems],
    )
    d0, head_grads = tie(d0, head_grads)
    dsides0 = to_pairs(d0)
    head_grads = jnp.sum(head_grads, axis=0)
    dw_in1, dw_out0, dw_bias_t = call(
        weights_kernel,
        steps,
        [
            double(dsides1),
            chan(factor1),
            chan(slope1),
            chan(grad2),
            chan(normed1),
            chan(grad1),
            chan(gate0),
            chan(prod_unit0),
            g_out[0],
            chan(d_bias_chan),
            chan(x_chan),
        ],
        [f_whole(5 * CH, C), f_whole(C, CH), f_whole(H, C)],
        6 * pos_flops,
        [pltpu.VMEM((5 * CH, width), BF16), pltpu.VMEM((5 * CH, C), F32)],
    )
    mid_part = half(jnp.concatenate([mid_part, head_grads], axis=0))

    places = np.zeros((2, OP, 128), ml_dtypes.bfloat16)
    for n in range(OP):
        places[0, n, n] = places[1, n, HALF + n] = 1
    where = jnp.stack([row_index, col_index]).astype(jnp.int32)
    col_units = jnp.transpose(half(col_unit).reshape(JH, jl, items, D), (0, 2, 1, 3))
    col_units = col_units.reshape(JH, items * jl, D)
    node_share = lax.dynamic_slice_in_dim(node_full, col_index * share, share, 0)
    cot_share = lax.dynamic_slice_in_dim(cot_rows, col_index * share, share, 0)
    unit_share, inv_share = node_norm(node_share)
    out_share = node_share + node_sum.reshape(share, D)
    grad_base = cot_share.astype(F32) + d_att
    unit_il = il_first(half(node_unit))
    (
        dsides0,
        mid_sent,
        dw_in1,
        dw_out0,
        dw_bias_t,
        col_units,
        unit_il,
        unit_share,
        inv_share,
        out_share,
        grad_base,
    ) = tie(
        dsides0,
        copies(mid_part, BOTH),
        dw_in1,
        dw_out0,
        dw_bias_t,
        col_units,
        unit_il,
        unit_share,
        inv_share,
        out_share,
        grad_base,
    )
    mid_all = swap_all(mid_sent, BOTH)
    grad_pair, d_middle, dw_in0, dg_in0, d_right_wide, db_outer = call(
        close_kernel,
        steps,
        [
            double(dsides0),
            chan(factor0),
            chan(slope0),
            chan(unit0),
            chan(inv0),
            chan(grad1),
            keep_in,
            g_in[0],
            layer(w_tin, 0),
            whole(mids),
            bd,
            chan(d_bias_chan),
            whole(w_bias),
        ],
        [
            tile(sds((items, 2, il, tile_cols, C), F32)),
            whole(sds(middle.shape, F32)),
            f_whole(5 * CH, C),
            sums,
            (sds((JH, OP, 128), F32), (1, OP, 128), lambda s: (s, 0, 0)),
            sums,
        ],
        14 * pos_flops,
        [
            pltpu.VMEM((5 * CH, width), BF16),
            part,
            pltpu.VMEM((width, 128), BF16),
            square,
            pltpu.VMEM((width, 2 * items * OP), F32),
            part32(),
            pltpu.VMEM((5 * CH, C), F32),
        ],
    )
    mid_rows = mid_all.shape[1] - head_grads.shape[0]
    pick_left = np.zeros((2, col_count, 8, il, 2, items), ml_dtypes.bfloat16)
    pick_right = np.zeros((parts, 2, JH, col_count, 8, 2, items, jl), ml_dtypes.bfloat16)
    for c in range(col_count):
        for n in range(share):
            i, b = divmod(c * share + n, items)
            pick_left[n % 2, c, n // 2, i % il, i // il, b] = 1
            for h in range(parts):
                j = h * tile_rows + i
                pick_right[h, n % 2, j // jl, c, n // 2, :, b, j % jl] = 1
    pick_left = pick_left.reshape(2, 8 * col_count, tile_rows * items)
    pick_right = pick_right.reshape(parts, 2, JH, 8 * col_count, 128)
    late_arrays = [dw_in0, dg_in0, db_outer, dw_in1, dw_out0, dg_in1, dg_out0, dw_bias_t]
    late_rows = [a.shape[0] for a in late_arrays] + [OP * OP, 4 * OP]
    (sent,) = call(
        functools.partial(tail_kernel, len(late_arrays)),
        1,
        [whole(a) for a in late_arrays]
        + [
            whole(d_middle),
            whole(left_node),
            whole(w_outer),
            whole(unit_il),
            whole(d_right_wide),
            whole(col_units),
            whole(places),
            whole(pick_left),
            whole(pick_right),
            (where, None, pltpu.SMEM),
        ],
        [whole(sds((devices, 32, 128), BF16))],
        1000,
        [pltpu.VMEM((OP * OP, 128), F32), pltpu.VMEM((4 * OP, 128), F32)],
    )
    sent, mid_all = tie(sent, mid_all)
    got = swap_all(sent, BOTH)
    head_grads = mid_all[:, mid_rows:].astype(F32).reshape(row_count, col_count, -1)
    head_grads = jnp.transpose(head_grads, (1, 0, 2)).reshape(col_count, 4, head_width, D)
    g_qkv = jnp.transpose(head_grads[:, :3], (3, 1, 0, 2)).reshape(D, 3 * D)
    g_node_out = head_grads[:, 3].reshape(D, D)

    def widen(blocks):
        count = blocks.shape[0] // 128
        return jnp.concatenate([blocks[128 * n : 128 * n + 128] for n in range(count)], axis=1)

    def cut(flat, counts):
        start, pieces = 0, []
        for rows in counts:
            pieces.append(flat[start : start + rows])
            start += rows
        return pieces

    (
        s_down,
        s_up,
        s_out1,
        s_dist,
        s_trans,
        s_gout1,
    ) = cut(mid_all[:, :mid_rows].reshape(-1, 128).astype(F32), [a.shape[0] for a in mid_arrays])
    s_up = widen(s_up)
    got, g_qkv, g_node_out, s_down, s_up, s_out1, s_gout1 = tie(
        got, g_qkv, g_node_out, s_down, s_up, s_out1, s_gout1
    )
    got = jnp.sum(got.astype(F32), axis=0)
    late_sent = copies(half(got[:24]), BOTH)
    node_part = half(got[24 : 24 + share // 2])
    late_sent, node_part = tie(late_sent, node_part)
    d_pair_rows = node_part.reshape(share, 2 * OP)
    d_normed = half(dot(d_pair_rows, w_ab, 1, 1)).astype(F32)
    scaled = d_normed * g_node
    grad_share = grad_base + inv_share * (
        scaled
        - jnp.mean(scaled, axis=-1, keepdims=True)
        - unit_share * jnp.mean(scaled * unit_share, axis=-1, keepdims=True)
    )
    late_all = swap_all(late_sent, BOTH)
    nodes = jnp.stack([out_share, grad_share])[None]
    reach = 1
    while reach < col_count:
        moves = [(c, c ^ reach) for c in range(col_count)]
        other = lax.ppermute(nodes, "col", moves)
        nodes = jnp.where(
            (col_index // reach) % 2 == 1,
            jnp.concatenate([other, nodes]),
            jnp.concatenate([nodes, other]),
        )
        reach *= 2

    def node_result(which):
        array = nodes[:, which].reshape(tile_rows, items, D)
        return jnp.transpose(array, (1, 0, 2))

    s_tin, s_outer, s_ab, s_gnode, s_bias, s_gtin, s_gtout, s_bout, s_tout = call(
        functools.partial(last_kernel, late_rows),
        1,
        [
            whole(late_all.reshape(-1, 128)),
            whole(jnp.transpose(w_ab)),
            whole(g_node[None]),
            whole(s_out1),
            whole(s_gout1),
        ],
        [
            f_whole(2, C, 5 * CH),
            f_whole(OP, OP * C),
            f_whole(2 * OP, D),
            f_whole(2, 128),
            f_whole(H, C),
            f_whole(2, C),
            f_whole(2, CH),
            f_whole(1, C),
            f_whole(2, CH, C),
        ],
        1000,
        [pltpu.VMEM((24 * devices, 128), F32)],
    )
    return (
        node_result(0),
        pair_out.reshape(pair_feats.shape),
        node_result(1),
        grad_pair.reshape(pair_feats.shape),
        grad_dist,
        g_qkv,
        jnp.transpose(s_bias),
        s_dist[0, :H],
        g_node_out,
        s_gnode.reshape(D),
        jnp.transpose(s_ab),
        s_outer,
        s_bout.reshape(C),
        s_gtin,
        s_tin,
        s_gtout,
        s_tout,
        s_trans[0],
        s_up,
        s_down,
    )


def solution(mesh):
    pair = P(None, "row", "col", None)
    node = P(None, "row", None)
    dist = P(None, "row", "col")
    return jax.shard_map(
        per_device,
        mesh=mesh,
        in_specs=(node, pair, dist, P(), node, pair) + (P(),) * 15,
        out_specs=(node, pair, node, pair, dist) + (P(),) * 15,
        check_vma=False,
    )
```
